128 devices in a mesh: items: 32 (over z, y_lo, x), vars: 4 (over y_hi, core).
Axes of the slice: x: 4, y: 4 (y_hi: 2, y_lo: 2; y = y_hi * 2 + y_lo), z: 4, core: 2. Of those that a mesh axis runs over, the one named last changes fastest.
Arguments:
- patches: bfloat16 [768, 2, 256, 320], P('items', None, None, 'vars'), may hold values from -6 to 6
- visible: int32 [768, 64], P('items'), may hold values from 0 to 255, as said below
- recon_cotangent: bfloat16 [768, 128, 320], P('items', None, 'vars'), may hold values from -6 to 6
- embed_weight: bfloat16 [320, 768], P('vars'), may hold values from -0.3125 to 0.3125
- embed_bias: bfloat16 [768], replicated, may hold values from -3 to 3
- position_table: bfloat16 [512, 768], replicated, may hold values from -3 to 3
- attn_norm_gain: bfloat16 [768], replicated, may hold values from 0.5 to 1.5
- attn_norm_bias: bfloat16 [768], replicated, may hold values from -2 to 2
- qkv_weight: bfloat16 [768, 2304], replicated, may hold values from -0.21875 to 0.21875
- qkv_bias: bfloat16 [2, 768], replicated, may hold values from -3 to 3
- proj_weight: bfloat16 [768, 768], replicated, may hold values from -0.75 to 0.75
- proj_bias: bfloat16 [768], replicated, may hold values from -2 to 2
- mlp_norm_gain: bfloat16 [768], replicated, may hold values from 0.5 to 1.5
- mlp_norm_bias: bfloat16 [768], replicated, may hold values from -2 to 2
- up_weight: bfloat16 [768, 3072], replicated, may hold values from -0.21875 to 0.21875
- up_bias: bfloat16 [3072], replicated, may hold values from -3 to 3
- down_weight: bfloat16 [3072, 768], replicated, may hold values from -0.109375 to 0.109375
- down_bias: bfloat16 [768], replicated, may hold values from -2 to 2
- head_weight: bfloat16 [768, 320], P(None, 'vars'), may hold values from -0.21875 to 0.21875
- head_bias: bfloat16 [320], P('vars'), may hold values from -3 to 3
Outputs:
- reconstruction: bfloat16 [768, 128, 320], P('items', None, 'vars')
- patch_grad: bfloat16 [768, 2, 256, 320], P('items', None, None, 'vars')
- embed_weight_grad: float32 [320, 768], P('vars')
- embed_bias_grad: float32 [768], replicated
- position_grad: float32 [512, 768], replicated
- attn_gain_grad: float32 [768], replicated
- attn_shift_grad: float32 [768], replicated
- qkv_weight_grad: float32 [768, 2304], replicated
- qkv_bias_grad: float32 [2, 768], replicated
- proj_weight_grad: float32 [768, 768], replicated
- proj_bias_grad: float32 [768], replicated
- mlp_gain_grad: float32 [768], replicated
- mlp_shift_grad: float32 [768], replicated
- up_weight_grad: float32 [768, 3072], replicated
- up_bias_grad: float32 [3072], replicated
- down_weight_grad: float32 [3072, 768], replicated
- down_bias_grad: float32 [768], replicated
- head_weight_grad: float32 [768, 320], P(None, 'vars')
- head_bias_grad: float32 [320], P('vars')
The draws below stay inside these ranges and needn't reach their ends.
Inputs may be any that keep to these rules, and one draw needn't show every extreme that they name: `visible`: each row holds 64 distinct patch numbers.
All inputs are finite; a program needn't handle non-finite values.
Results may differ from the reference program's by a relative error of at most 0.013.
Values may be sent and summed in bfloat16 or wider, within the bound.
No kernel may reach another device: no remote copies, remote signals or barrier semaphores. Data moves between devices by JAX's collectives and lax.ppermute only.
A program may use at most 256 MiB of HBM per device.

```python
import math
import jax
import jax.numpy as jnp
from jax import lax

D = 768
HEADS = 12
HEAD_DIM = 64
FF = 3072
NPATCH = 256
NVIS = 64
FEAT = 320
ITEMS = 768


def draw_visible(key, part):
    key = jax.random.fold_in(key, 7)
    item_keys = jax.random.split(key, ITEMS)
    orders = jax.vmap(lambda item_key: jax.random.permutation(item_key, NPATCH))(item_keys)
    chosen = orders[:, :NVIS].astype(jnp.int32)
    inner = jax.random.permutation(jax.random.fold_in(key, 1), NPATCH - 2)[:NVIS - 2] + 1
    ends = jnp.array([0, NPATCH - 1], dtype=jnp.int32)
    first_row = jnp.concatenate([ends, inner.astype(jnp.int32)])
    first_row = jax.random.permutation(jax.random.fold_in(key, 2), first_row)
    return chosen.at[0].set(first_row).astype(jnp.int32)


def block_levels(rng, extent, cuts, low, largest):
    def one(dim, parts):
        draws = jax.random.uniform(jax.random.fold_in(jax.random.fold_in(rng, 6), dim), (parts,), jnp.float32, low / len(cuts), largest / len(cuts))
        return jnp.repeat(jnp.exp(draws), extent[dim] // parts).reshape((-1,) + (1,) * (len(extent) - dim - 1))

    level = one(*cuts[0])
    for cut in cuts[1:]:
        level = level * one(*cut)
    return level


def scatter_about(stream_key, dims, scale, limit, cuts=(), held_as=jnp.bfloat16):
    result = scale * jax.random.normal(stream_key, dims, jnp.float32)
    if cuts:
        result = result * block_levels(stream_key, dims, cuts, -0.22, 0.18)
    return jnp.clip(result, -limit, limit).astype(held_as)


def setup_inputs(seed: int = 0) -> dict:
    seeds = jax.random.split(jax.random.key(seed), 21)
    patches = scatter_about(seeds[0], (ITEMS, 2, NPATCH, FEAT), 1.0, 6.0, ((0, 32), (3, 4)))
    visible = draw_visible(jax.random.fold_in(seeds[20], 71), 0)
    recon_cotangent = scatter_about(seeds[2], (ITEMS, 2 * NVIS, FEAT), 1.0, 6.0, ((0, 32), (2, 4)))
    embed_weight = scatter_about(seeds[3], (FEAT, D), FEAT ** -0.5, 0.3125, ((0, 4),))
    embed_bias = scatter_about(seeds[4], (D,), 0.5, 3.0)
    position_table = scatter_about(seeds[5], (2 * NPATCH, D), 0.5, 3.0)
    attn_norm_gain = jnp.clip(1.0 + 0.1 * jax.random.normal(seeds[6], (D,), jnp.float32), 0.5, 1.5).astype(jnp.bfloat16)
    attn_norm_bias = scatter_about(seeds[7], (D,), 0.3, 2.0)
    qkv_weight = scatter_about(seeds[8], (D, 3 * D), D ** -0.5, 0.21875)
    qkv_bias = scatter_about(seeds[9], (2, D), 0.5, 3.0)
    proj_weight = scatter_about(seeds[10], (D, D), (max(1, D // 12)) ** -0.5, 0.75)
    proj_bias = scatter_about(seeds[11], (D,), 0.3, 2.0)
    mlp_norm_gain = jnp.clip(1.0 + 0.1 * jax.random.normal(seeds[12], (D,), jnp.float32), 0.5, 1.5).astype(jnp.bfloat16)
    mlp_norm_bias = scatter_about(seeds[13], (D,), 0.3, 2.0)
    up_weight = scatter_about(seeds[14], (D, FF), D ** -0.5, 0.21875)
    up_bias = scatter_about(seeds[15], (FF,), 0.5, 3.0)
    down_weight = scatter_about(seeds[16], (FF, D), FF ** -0.5, 0.109375)
    down_bias = scatter_about(seeds[17], (D,), 0.3, 2.0)
    head_weight = scatter_about(seeds[18], (D, FEAT), D ** -0.5, 0.21875, ((1, 4),))
    head_bias = scatter_about(seeds[19], (FEAT,), 0.5, 3.0, ((0, 4),))
    return {"patches": patches, "visible": visible, "recon_cotangent": recon_cotangent, "embed_weight": embed_weight, "embed_bias": embed_bias, "position_table": position_table, "attn_norm_gain": attn_norm_gain, "attn_norm_bias": attn_norm_bias, "qkv_weight": qkv_weight, "qkv_bias": qkv_bias, "proj_weight": proj_weight, "proj_bias": proj_bias, "mlp_norm_gain": mlp_norm_gain, "mlp_norm_bias": mlp_norm_bias, "up_weight": up_weight, "up_bias": up_bias, "down_weight": down_weight, "down_bias": down_bias, "head_weight": head_weight, "head_bias": head_bias}


@jax.custom_vjp
def low(v):
    return lax.optimization_barrier(v.astype(jnp.bfloat16)).astype(jnp.float32)

@jax.custom_vjp
def low_back(v):
    return v

def low_keep(v):
    return (low(v), None)

def low_pass(kept, grad):
    return (grad,)

def back_keep(v):
    return (v, None)

def back_low(kept, grad):
    return (low(grad),)
low.defvjp(low_keep, low_pass)
low_back.defvjp(back_keep, back_low)

def layer_norm(values, gain, shift):
    centre = values - lax.optimization_barrier(jnp.mean(values, axis=-1, keepdims=True))
    spread = lax.optimization_barrier(jnp.mean(centre * centre, axis=-1, keepdims=True))
    return centre * lax.rsqrt(spread + 1e-06) * gain + shift

def forward(inputs, params, position):
    embed_weight, embed_bias, position_table, attn_norm_gain, attn_norm_bias, qkv_weight, qkv_bias, proj_weight, proj_bias, mlp_norm_gain, mlp_norm_bias, up_weight, up_bias, down_weight, down_bias, head_weight, head_bias = params
    highest = lax.Precision.HIGHEST
    item_count = inputs.shape[0]
    row_count = inputs.shape[1]
    projected = low_back(jnp.einsum('grf,fd->grd', inputs, embed_weight, precision=highest))
    embedded = projected + embed_bias + position_table[position]
    normed_one = low(layer_norm(embedded, attn_norm_gain, attn_norm_bias))
    mixed = jnp.einsum('grd,de->gre', normed_one, qkv_weight, precision=highest)
    head_shape = (item_count, row_count, HEADS, HEAD_DIM)
    queries = low_back(low(mixed[..., :D] + qkv_bias[0])).reshape(head_shape)
    key_rows = low_back(low(mixed[..., D:2 * D])).reshape(head_shape)
    value_rows = low_back(low(mixed[..., 2 * D:] + qkv_bias[1])).reshape(head_shape)
    scores = low_back(jnp.einsum('gqhc,gkhc->ghqk', queries, key_rows, precision=highest) * HEAD_DIM ** (-0.5))
    row_max = lax.optimization_barrier(jnp.max(scores, axis=-1, keepdims=True))
    weights = jnp.exp(scores - row_max)
    probabilities = weights / lax.optimization_barrier(jnp.sum(weights, axis=-1, keepdims=True))
    heads_out = jnp.einsum('ghqk,gkhc->gqhc', low(probabilities), value_rows, precision=highest)
    attended = low_back(low(heads_out.reshape(item_count, row_count, D)))
    residual_one = embedded + low_back(jnp.einsum('grd,de->gre', attended, proj_weight, precision=highest)) + proj_bias
    normed_two = low(layer_norm(residual_one, mlp_norm_gain, mlp_norm_bias))
    hidden_pre = low_back(jnp.einsum('grd,df->grf', normed_two, up_weight, precision=highest) + up_bias)
    activated = low(jax.nn.gelu(hidden_pre))
    block_out = residual_one + low_back(jnp.einsum('grf,fd->grd', activated, down_weight, precision=highest)) + down_bias
    return jnp.einsum('grd,df->grf', low(block_out), head_weight, precision=highest) + head_bias

def scatter_rows(rows, chosen):
    grid = jnp.zeros((2, NPATCH, FEAT), rows.dtype)
    return grid.at[:, chosen].set(rows.reshape(2, NVIS, FEAT))

def reference(patches, visible, recon_cotangent, embed_weight, embed_bias, position_table, attn_norm_gain, attn_norm_bias, qkv_weight, qkv_bias, proj_weight, proj_bias, mlp_norm_gain, mlp_norm_bias, up_weight, up_bias, down_weight, down_bias, head_weight, head_bias):
    params = tuple((weight.astype(jnp.float32) for weight in (embed_weight, embed_bias, position_table, attn_norm_gain, attn_norm_bias, qkv_weight, qkv_bias, proj_weight, proj_bias, mlp_norm_gain, mlp_norm_bias, up_weight, up_bias, down_weight, down_bias, head_weight, head_bias)))
    row_count = 2 * NVIS
    group_size = math.gcd(ITEMS, max(1, 4096 // row_count))
    group_steps = ITEMS // group_size

    def one_group(totals, slices):
        patch_block, visible_block, cot_block = slices
        gather_index = jnp.broadcast_to(visible_block[:, None, :, None], (group_size, 2, NVIS, FEAT))
        inputs = jnp.take_along_axis(patch_block.astype(jnp.float32), gather_index, axis=2)
        inputs = inputs.reshape(group_size, row_count, FEAT)
        position = jnp.concatenate([visible_block, visible_block + NPATCH], axis=1).astype(jnp.int32)
        output, pullback = jax.vjp(lambda values, weights: forward(values, weights, position), inputs, params)
        grad_inputs, grad_params = pullback(cot_block.astype(jnp.float32))
        placed = jax.vmap(scatter_rows)(grad_inputs.astype(jnp.bfloat16), visible_block)
        totals = jax.tree.map(jnp.add, totals, grad_params)
        return (totals, (output.astype(jnp.bfloat16), placed))
    zeros = jax.tree.map(jnp.zeros_like, params)
    totals, (recon, placed) = lax.scan(one_group, zeros, (patches.reshape(group_steps, group_size, 2, NPATCH, FEAT), visible.reshape(group_steps, group_size, NVIS), recon_cotangent.reshape(group_steps, group_size, row_count, FEAT)))
    return (recon.reshape(ITEMS, row_count, FEAT), placed.reshape(ITEMS, 2, NPATCH, FEAT), totals[0], totals[1], totals[2], totals[3], totals[4], totals[5], totals[6], totals[7], totals[8], totals[9], totals[10], totals[11], totals[12], totals[13], totals[14], totals[15], totals[16])
```

```python
import jax
import jax.numpy as jnp
from jax import lax
from jax.sharding import PartitionSpec as P

HEADS = 12
HEAD_DIM = 64


def layer_norm(values, gain, shift):
    centre = values - jnp.mean(values, axis=-1, keepdims=True)
    spread = jnp.mean(centre * centre, axis=-1, keepdims=True)
    return centre * lax.rsqrt(spread + 1e-06) * gain + shift


def matmul(left, right):
    return jnp.dot(left, right, preferred_element_type=jnp.float32)


def matmul_tn(left, right):
    return lax.dot_general(
        left, right, (((0,), (0,)), ((), ())), preferred_element_type=jnp.float32
    )


def matmul_nt(left, right):
    return lax.dot_general(
        left, right, (((1,), (1,)), ((), ())), preferred_element_type=jnp.float32
    )


def exchange(rows):
    return lax.all_to_all(rows, "vars", 0, 1, tiled=True)


def return_rows(rows, width):
    return lax.all_to_all(rows, "vars", 1, 0, tiled=True)


def body(
    patches,
    visible,
    recon_cotangent,
    embed_weight,
    embed_bias,
    position_table,
    attn_norm_gain,
    attn_norm_bias,
    qkv_weight,
    qkv_bias,
    proj_weight,
    proj_bias,
    mlp_norm_gain,
    mlp_norm_bias,
    up_weight,
    up_bias,
    down_weight,
    down_bias,
    head_weight,
    head_bias,
):
    groups = lax.axis_size("vars")
    my_group = lax.axis_index("vars")
    batch_items = patches.shape[0]
    patch_count = patches.shape[2]
    group_feats = patches.shape[3]
    visible_count = visible.shape[1]
    item_rows = 2 * visible_count
    own_items = batch_items // groups
    own_rows = own_items * item_rows
    model_width = qkv_weight.shape[0]
    patch_numbers = lax.broadcasted_iota(jnp.int32, (1, 1, patch_count), 2)
    selector = (visible[:, :, None] == patch_numbers).astype(jnp.bfloat16)
    picked = jnp.einsum(
        "bjp,btpf->btjf", selector, patches, preferred_element_type=jnp.float32
    ).astype(jnp.bfloat16)
    picked = picked.reshape(batch_items * item_rows, group_feats)
    picked = exchange(picked)
    bias_row = jnp.pad(head_bias, (0, model_width - group_feats))[None]
    shards = lax.all_gather(
        jnp.concatenate([embed_weight, head_weight.T, bias_row], axis=0), "vars", axis=0
    )
    embed_weight = shards[:, :group_feats].reshape(groups * group_feats, model_width)
    head_rows = shards[:, group_feats : 2 * group_feats].reshape(groups * group_feats, model_width)
    head_bias = shards[:, 2 * group_feats, :group_feats].reshape(groups * group_feats)
    cot_flat = exchange(recon_cotangent.reshape(batch_items * item_rows, group_feats))
    own_visible = lax.dynamic_slice_in_dim(visible, my_group * own_items, own_items, 0)
    position = jnp.concatenate([own_visible, own_visible + patch_count], axis=1).reshape(own_rows)
    slot_numbers = lax.broadcasted_iota(jnp.int32, (1, 2 * patch_count), 1)
    position_hot = (position[:, None] == slot_numbers).astype(jnp.bfloat16)
    projected = matmul(picked, embed_weight)
    embedded = projected + embed_bias.astype(jnp.float32) + matmul(position_hot, position_table)
    norm_one, pull_one = jax.vjp(
        layer_norm, embedded, attn_norm_gain.astype(jnp.float32), attn_norm_bias.astype(jnp.float32)
    )
    normed_one = norm_one.astype(jnp.bfloat16)
    joined_bias = jnp.concatenate(
        [
            qkv_bias[0].astype(jnp.float32),
            jnp.zeros((model_width,), jnp.float32),
            qkv_bias[1].astype(jnp.float32),
        ]
    )
    qkv_low = (matmul(normed_one, qkv_weight) + joined_bias).astype(jnp.bfloat16)
    qkv_low = qkv_low.reshape(own_items, item_rows, 3, HEADS, HEAD_DIM)
    queries = qkv_low[:, :, 0]
    key_rows = qkv_low[:, :, 1]
    value_rows = qkv_low[:, :, 2]
    score_scale = HEAD_DIM ** (-0.5)
    scores = (
        jnp.einsum("gqhc,gkhc->ghqk", queries, key_rows, preferred_element_type=jnp.float32)
        * score_scale
    )
    row_max = jnp.max(scores, axis=-1, keepdims=True)
    weights = jnp.exp(scores - row_max)
    denominator = jnp.sum(weights, axis=-1, keepdims=True)
    probabilities = weights / denominator
    log_total = row_max + jnp.log(denominator)
    heads_out = jnp.einsum(
        "ghqk,gkhc->gqhc",
        probabilities.astype(jnp.bfloat16),
        value_rows,
        preferred_element_type=jnp.float32,
    )
    attended = heads_out.reshape(own_rows, model_width).astype(jnp.bfloat16)
    residual_one = embedded + matmul(attended, proj_weight) + proj_bias.astype(jnp.float32)
    norm_two, pull_two = jax.vjp(
        layer_norm,
        residual_one,
        mlp_norm_gain.astype(jnp.float32),
        mlp_norm_bias.astype(jnp.float32),
    )
    normed_two = norm_two.astype(jnp.bfloat16)
    hidden_pre = matmul(normed_two, up_weight) + up_bias.astype(jnp.float32)
    activated, pull_gelu = jax.vjp(jax.nn.gelu, hidden_pre)
    activated_low = activated.astype(jnp.bfloat16)
    block_out = residual_one + matmul(activated_low, down_weight) + down_bias.astype(jnp.float32)
    out_low = block_out.astype(jnp.bfloat16)
    recon_flat = matmul_nt(out_low, head_rows) + head_bias.astype(jnp.float32)
    recon_flat = return_rows(recon_flat.astype(jnp.bfloat16), group_feats)
    reconstruction = recon_flat.reshape(batch_items, item_rows, group_feats)
    grad_out = matmul(cot_flat, head_rows)
    head_grad = matmul_tn(cot_flat, out_low)
    head_shift_grad = jnp.sum(cot_flat.astype(jnp.float32), axis=0)
    down_low = grad_out.astype(jnp.bfloat16)
    down_grad = matmul_tn(activated_low, down_low)
    down_shift_grad = jnp.sum(grad_out, axis=0)
    (grad_hidden,) = pull_gelu(matmul_nt(down_low, down_weight))
    hidden_low = grad_hidden.astype(jnp.bfloat16)
    up_grad = matmul_tn(normed_two, hidden_low)
    up_shift_grad = jnp.sum(hidden_low.astype(jnp.float32), axis=0)
    grad_res, mlp_gain_grad, mlp_shift_grad = pull_two(matmul_nt(hidden_low, up_weight))
    grad_res = grad_res + grad_out
    res_low = grad_res.astype(jnp.bfloat16)
    proj_grad = matmul_tn(attended, res_low)
    proj_shift_grad = jnp.sum(grad_res, axis=0)
    attn_grad = matmul_nt(res_low, proj_weight).astype(jnp.bfloat16)
    attn_grad = attn_grad.reshape(own_items, item_rows, HEADS, HEAD_DIM)
    scores_again = (
        jnp.einsum("gqhc,gkhc->ghqk", queries, key_rows, preferred_element_type=jnp.float32)
        * score_scale
    )
    probs_again = jnp.exp(scores_again - log_total)
    grad_probs = jnp.einsum(
        "gqhc,gkhc->ghqk", attn_grad, value_rows, preferred_element_type=jnp.float32
    )
    grad_values = jnp.einsum(
        "ghqk,gqhc->gkhc",
        probs_again.astype(jnp.bfloat16),
        attn_grad,
        preferred_element_type=jnp.float32,
    )
    grad_scores = probs_again * (
        grad_probs - jnp.sum(probs_again * grad_probs, axis=-1, keepdims=True)
    )
    scores_low = grad_scores.astype(jnp.bfloat16)
    grad_queries = (
        jnp.einsum("ghqk,gkhc->gqhc", scores_low, key_rows, preferred_element_type=jnp.float32)
        * score_scale
    )
    grad_keys = (
        jnp.einsum("ghqk,gqhc->gkhc", scores_low, queries, preferred_element_type=jnp.float32)
        * score_scale
    )
    grad_qkv = jnp.stack([grad_queries, grad_keys, grad_values], axis=2).astype(jnp.bfloat16)
    grad_qkv = grad_qkv.reshape(own_rows, 3 * model_width)
    qkv_grad = matmul_tn(normed_one, grad_qkv)
    qkv_wide = grad_qkv.astype(jnp.float32)
    qkv_shift_grad = jnp.stack(
        [
            jnp.sum(qkv_wide[:, :model_width], axis=0),
            jnp.sum(qkv_wide[:, 2 * model_width :], axis=0),
        ]
    )
    grad_norm_in, attn_gain_grad, attn_shift_grad = pull_one(matmul_nt(grad_qkv, qkv_weight))
    grad_embedded = grad_norm_in + grad_res
    embed_shift_grad = jnp.sum(grad_embedded, axis=0)
    position_grad = lax.dot_general(
        position_hot.astype(jnp.float32),
        grad_embedded,
        (((0,), (0,)), ((), ())),
        precision=lax.Precision.HIGHEST,
    )
    embedded_low = grad_embedded.astype(jnp.bfloat16)
    embed_grad = matmul_tn(picked, embedded_low)
    grad_rows = return_rows(matmul_nt(embedded_low, embed_weight).astype(jnp.bfloat16), group_feats)
    parts = (
        down_grad,
        up_grad,
        qkv_grad,
        proj_grad,
        position_grad,
        embed_grad,
        head_grad,
        qkv_shift_grad,
        up_shift_grad.reshape(-1, model_width),
        embed_shift_grad[None],
        attn_gain_grad[None],
        attn_shift_grad[None],
        proj_shift_grad[None],
        mlp_gain_grad[None],
        mlp_shift_grad[None],
        down_shift_grad[None],
        jnp.pad(head_shift_grad, (0, model_width - head_shift_grad.shape[0]))[None],
    )
    small = jnp.concatenate([part.astype(jnp.bfloat16) for part in parts[4:]], axis=0)
    big = lax.psum(tuple(part.astype(jnp.bfloat16) for part in parts[:4]) + (small,), ("items", "vars"))
    big = [part.astype(jnp.float32) for part in big]
    down_grad, up_grad, qkv_grad, proj_grad, small = big
    cuts = []
    start = 0
    for part in parts[4:]:
        cuts.append(small[start : start + part.shape[0]])
        start += part.shape[0]
    position_grad, embed_grad, head_grad, qkv_shift_grad, up_shift_grad = cuts[:5]
    up_shift_grad = up_shift_grad.reshape(-1)
    embed_shift_grad, attn_gain_grad, attn_shift_grad, proj_shift_grad = [c[0] for c in cuts[5:9]]
    mlp_gain_grad, mlp_shift_grad, down_shift_grad, head_shift_grad = [c[0] for c in cuts[9:]]
    embed_grad = lax.dynamic_slice_in_dim(embed_grad, my_group * group_feats, group_feats, 0)
    head_grad = lax.dynamic_slice_in_dim(head_grad, my_group * group_feats, group_feats, 0).T
    head_shift_grad = lax.dynamic_slice_in_dim(
        head_shift_grad, my_group * group_feats, group_feats, 0
    )
    placed_rows = grad_rows.reshape(batch_items, 2, visible_count, group_feats)
    patch_grad = jnp.einsum(
        "bjp,btjf->btpf", selector, placed_rows, preferred_element_type=jnp.float32
    ).astype(jnp.bfloat16)
    return (
        reconstruction,
        patch_grad,
        embed_grad,
        embed_shift_grad,
        position_grad,
        attn_gain_grad,
        attn_shift_grad,
        qkv_grad,
        qkv_shift_grad,
        proj_grad,
        proj_shift_grad,
        mlp_gain_grad,
        mlp_shift_grad,
        up_grad,
        up_shift_grad,
        down_grad,
        down_shift_grad,
        head_grad,
        head_shift_grad,
    )


def solution(mesh):
    in_specs = (
        P("items", None, None, "vars"),
        P("items", None),
        P("items", None, "vars"),
        P("vars", None),
        P(),
        P(),
        P(),
        P(),
        P(),
        P(),
        P(),
        P(),
        P(),
        P(),
        P(),
        P(),
        P(),
        P(),
        P(None, "vars"),
        P("vars"),
    )
    out_specs = (
        P("items", None, "vars"),
        P("items", None, None, "vars"),
        P("vars", None),
        P(),
        P(),
        P(),
        P(),
        P(),
        P(),
        P(),
        P(),
        P(),
        P(),
        P(),
        P(),
        P(),
        P(),
        P(None, "vars"),
        P("vars"),
    )
    return jax.shard_map(body, mesh=mesh, in_specs=in_specs, out_specs=out_specs, check_vma=False)
```

```python
import functools

import jax
import jax.numpy as jnp
from jax import lax
from jax.experimental import pallas as pl
from jax.experimental.pallas import tpu as pltpu
from jax.sharding import Mesh
from jax.sharding import PartitionSpec as P

HEADS = 12
HEAD_DIM = 64
D = 768
FF = 3072
ITEM_ROWS = 128
OWN_ITEMS = 6
ROWS = OWN_ITEMS * ITEM_ROWS
GROUPS = 4
WIDTH = 80
PAIRS = HEADS // 2
SLOTS = 512
FF_TILE = 768
CHUNK = 256
F32 = jnp.float32
BF16 = jnp.bfloat16
VMEM_LIMIT = 58 * 1024 * 1024

ITEMS_AXES = ("z", "ylo", "x")
VARS_AXES = ("yhi", "core")
ALL_AXES = ITEMS_AXES + VARS_AXES


def dot(left, right):
    return jnp.dot(left, right, preferred_element_type=F32)


def dot_nt(left, right):
    return lax.dot_general(left, right, (((1,), (1,)), ((), ())), preferred_element_type=F32)


def dot_tn(left, right):
    return lax.dot_general(left, right, (((0,), (0,)), ((), ())), preferred_element_type=F32)


def normalise(values):
    centre = values - jnp.mean(values, axis=-1, keepdims=True)
    scale = lax.rsqrt(jnp.mean(centre * centre, axis=-1, keepdims=True) + 1e-06)
    return centre * scale, scale


def norm_back(grad, unit, scale, gain):
    wide = grad * gain
    first = jnp.mean(wide, axis=-1, keepdims=True)
    second = jnp.mean(wide * unit, axis=-1, keepdims=True)
    return scale * (wide - first - unit * second)


def column_sum(values):
    return jnp.sum(values, axis=0, keepdims=True)


def low_half():
    return lax.broadcasted_iota(jnp.int32, (ITEM_ROWS, ITEM_ROWS), 1) < HEAD_DIM


def stack_heads(block, first):
    zero = jnp.zeros_like(block)
    return jnp.concatenate([jnp.where(first, block, zero), jnp.where(first, zero, block)], axis=0)


def join_heads(both, first):
    return jnp.where(first, both[:ITEM_ROWS], both[ITEM_ROWS:])


def call(kernel, out_shape, flops, moved, **kwargs):
    return pl.pallas_call(
        kernel,
        out_shape=out_shape,
        compiler_params=pltpu.CompilerParams(vmem_limit_bytes=VMEM_LIMIT),
        cost_estimate=pl.CostEstimate(flops=flops, bytes_accessed=moved, transcendentals=0),
        **kwargs,
    )


def shape(*dims, dtype=F32):
    return jax.ShapeDtypeStruct(dims, dtype)


EMBED_BIAS, GAIN_ONE, SHIFT_ONE, PROJ_BIAS, GAIN_TWO, SHIFT_TWO, DOWN_BIAS, HEAD_BIAS = range(8)


def attention_kernel(
    inputs, embed_weight, position, table, small, qkv_weight, qkv_bias, proj_weight,
    embedded, normed_one, qkv, probs, attended, residual, normed_two,
):
    def embed(step, carry):
        rows = pl.ds(pl.multiple_of(step * CHUNK, CHUNK), CHUNK)
        slots = lax.broadcasted_iota(jnp.int32, (CHUNK, SLOTS), 1)
        hot = (position[rows, :] == slots).astype(BF16)
        total = dot(hot, table[...]) + small[EMBED_BIAS : EMBED_BIAS + 1, :]
        for group in range(GROUPS):
            total += dot(inputs[group, rows, :], embed_weight[group])
        embedded[rows, :] = total
        unit, _ = normalise(total)
        normed = unit * small[GAIN_ONE : GAIN_ONE + 1, :] + small[SHIFT_ONE : SHIFT_ONE + 1, :]
        normed_one[rows, :] = normed.astype(BF16)
        return carry

    lax.fori_loop(0, ROWS // CHUNK, embed, 0)

    def project(step, carry):
        columns = pl.ds(pl.multiple_of(step * CHUNK, CHUNK), CHUNK)
        mixed = dot(normed_one[...], qkv_weight[:, columns]) + qkv_bias[:, columns]
        qkv[:, columns] = mixed.astype(BF16)
        return carry

    lax.fori_loop(0, 3 * D // CHUNK, project, 0)
    first = low_half()

    def attend(item, carry):
        rows = pl.ds(pl.multiple_of(item * ITEM_ROWS, ITEM_ROWS), ITEM_ROWS)
        for pair in range(PAIRS):
            lanes = slice(pair * ITEM_ROWS, (pair + 1) * ITEM_ROWS)
            queries = qkv[rows, lanes] * jnp.asarray(HEAD_DIM**-0.5, BF16)
            keys = qkv[rows, D + pair * ITEM_ROWS : D + (pair + 1) * ITEM_ROWS]
            values = qkv[rows, 2 * D + pair * ITEM_ROWS : 2 * D + (pair + 1) * ITEM_ROWS]
            scores = dot_nt(stack_heads(queries, first), keys)
            weights = jnp.exp(scores - jnp.max(scores, axis=-1, keepdims=True))
            weights = weights * (1.0 / jnp.sum(weights, axis=-1, keepdims=True))
            weights = weights.astype(BF16)
            spot = pl.multiple_of((item * PAIRS + pair) * CHUNK, CHUNK)
            probs[pl.ds(spot, CHUNK), :] = weights
            attended[rows, lanes] = join_heads(dot(weights, values), first).astype(BF16)
        return carry

    lax.fori_loop(0, OWN_ITEMS, attend, 0)

    def finish(step, carry):
        rows = pl.ds(pl.multiple_of(step * CHUNK, CHUNK), CHUNK)
        total = embedded[rows, :] + dot(attended[rows, :], proj_weight[...])
        total += small[PROJ_BIAS : PROJ_BIAS + 1, :]
        residual[rows, :] = total
        unit, _ = normalise(total)
        normed = unit * small[GAIN_TWO : GAIN_TWO + 1, :] + small[SHIFT_TWO : SHIFT_TWO + 1, :]
        normed_two[rows, :] = normed.astype(BF16)
        return carry

    lax.fori_loop(0, ROWS // CHUNK, finish, 0)


def attention_forward(inputs, embed_weight, position, table, small, qkv_weight, qkv_bias, proj_weight):
    return call(
        attention_kernel,
        (
            shape(ROWS, D),
            shape(ROWS, D, dtype=BF16),
            shape(ROWS, 3 * D, dtype=BF16),
            shape(OWN_ITEMS * PAIRS * CHUNK, ITEM_ROWS, dtype=BF16),
            shape(ROWS, D, dtype=BF16),
            shape(ROWS, D),
            shape(ROWS, D, dtype=BF16),
        ),
        9_000_000_000,
        24_000_000,
    )(inputs, embed_weight, position, table, small, qkv_weight, qkv_bias, proj_weight)


def mlp_kernel(
    normed_two, residual, up_weight, up_bias, down_weight, small, head_rows, head_bias, cotangent,
    activated, slope, recon, head_grad, head_sum, grad_out, down_low, down_sum, total,
):
    step = pl.program_id(0)
    bias = up_bias[...]

    @pl.when(step == 0)
    def _():
        total[...] = residual[...] + small[DOWN_BIAS : DOWN_BIAS + 1, :]

    for start in range(0, ROWS, CHUNK):
        rows = slice(start, start + CHUNK)
        hidden = dot(normed_two[rows, :], up_weight[...]) + bias
        square = hidden * hidden
        inner = 0.7978845608028654 * (1.0 + 0.044715 * square)
        curve = jnp.tanh(hidden * inner)
        half = 0.5 + 0.5 * curve
        low = (hidden * half).astype(BF16)
        activated[rows, :] = low
        rise = 0.7978845608028654 * (1.0 + 3 * 0.044715 * square)
        slope[rows, :] = (half + hidden * half * (1.0 - curve) * rise).astype(BF16)
        total[rows, :] += dot(low, down_weight[...])

    @pl.when(step == pl.num_programs(0) - 1)
    def _():
        low = total[...].astype(BF16)
        grad = jnp.zeros((ROWS, D), F32)
        for group in range(GROUPS):
            recon[group] = (dot_nt(low, head_rows[group]) + head_bias[group]).astype(BF16)
            own = cotangent[group]
            head_grad[group] = dot_tn(own, low).astype(BF16)
            head_sum[group] = column_sum(own.astype(F32))
            grad += dot(own, head_rows[group])
        grad_out[...] = grad
        down_low[...] = grad.astype(BF16)
        down_sum[...] = column_sum(grad)


def mlp_forward(normed_two, residual, up_weight, up_bias, down_weight, small, head_rows, head_bias, cotangent):
    whole = lambda *dims: pl.BlockSpec(dims, lambda step: (0,) * len(dims))
    columns = lambda rows: pl.BlockSpec((rows, FF_TILE), lambda step: (0, step))
    return call(
        mlp_kernel,
        (
            shape(ROWS, FF, dtype=BF16),
            shape(ROWS, FF, dtype=BF16),
            shape(GROUPS, ROWS, WIDTH, dtype=BF16),
            shape(GROUPS, WIDTH, D, dtype=BF16),
            shape(GROUPS, 1, WIDTH),
            shape(ROWS, D),
            shape(ROWS, D, dtype=BF16),
            shape(1, D),
        ),
        9_000_000_000,
        30_000_000,
        grid=(FF // FF_TILE,),
        in_specs=[
            whole(ROWS, D),
            whole(ROWS, D),
            columns(D),
            columns(1),
            pl.BlockSpec((FF_TILE, D), lambda step: (step, 0)),
            whole(8, D),
            whole(GROUPS, WIDTH, D),
            whole(GROUPS, 1, WIDTH),
            whole(GROUPS, ROWS, WIDTH),
        ],
        out_specs=[
            columns(ROWS),
            columns(ROWS),
            whole(GROUPS, ROWS, WIDTH),
            whole(GROUPS, WIDTH, D),
            whole(GROUPS, 1, WIDTH),
            whole(ROWS, D),
            whole(ROWS, D),
            whole(1, D),
        ],
        scratch_shapes=[pltpu.VMEM((ROWS, D), F32)],
    )(normed_two, residual, up_weight, up_bias, down_weight, small, head_rows, head_bias, cotangent)


def mlp_back_kernel(
    half, down_low, activated, slope, normed_two, down_weight, up_weight, before,
    up_grad, down_grad, up_sum, after, flipped,
):
    step = pl.program_id(0)

    @pl.when(step == 0)
    def _():
        after[...] = before[...]
        flipped[...] = normed_two[...].T

    low = down_low[...]
    grad = dot_nt(low, down_weight[...]) * slope[...].astype(F32)
    hidden_low = grad.astype(BF16)
    up_sum[...] = column_sum(hidden_low.astype(F32))
    cut = FF_TILE // 2
    for part in range(2):
        lanes = slice(part * cut, (part + 1) * cut)
        up_grad[part] = dot(flipped[...], hidden_low[:, lanes]).astype(BF16)
        down_grad[part] = dot_tn(activated[:, lanes], low).astype(BF16)
    after[...] += dot_nt(hidden_low, up_weight[...])


def mlp_backward(half, down_low, activated, slope, normed_two, down_weight, up_weight, before):
    whole = lambda *dims: pl.BlockSpec(dims, lambda step, half: (0,) * len(dims))
    columns = lambda rows: pl.BlockSpec((rows, FF_TILE), lambda step, half: (0, 2 * half[0] + step))
    return call(
        mlp_back_kernel,
        (
            shape(4, D, FF // 8, dtype=BF16),
            shape(4, FF // 8, D, dtype=BF16),
            shape(1, FF // 2),
            shape(ROWS, D),
        ),
        7_300_000_000,
        20_000_000,
        grid_spec=pltpu.PrefetchScalarGridSpec(
            num_scalar_prefetch=1,
            grid=(FF // 2 // FF_TILE,),
            in_specs=[
                whole(ROWS, D),
                columns(ROWS),
                columns(ROWS),
                whole(ROWS, D),
                pl.BlockSpec((FF_TILE, D), lambda step, half: (2 * half[0] + step, 0)),
                columns(D),
                whole(ROWS, D),
            ],
            out_specs=[
                pl.BlockSpec((2, D, FF // 8), lambda step, half: (step, 0, 0)),
                pl.BlockSpec((2, FF // 8, D), lambda step, half: (step, 0, 0)),
                pl.BlockSpec((1, FF_TILE), lambda step, half: (0, step)),
                whole(ROWS, D),
            ],
            scratch_shapes=[pltpu.VMEM((D, ROWS), BF16)],
        ),
    )(half, down_low, activated, slope, normed_two, down_weight, up_weight, before)


def attention_back_kernel(
    grad_normed, grad_out, residual, small, attended, proj_weight, qkv, probs, normed_one, qkv_weight,
    embedded, inputs, embed_weight, position,
    qkv_grad, proj_grad, extra_grad, sums, grad_inputs, grad_qkv, grad_res, attn_grad, embedded_low,
):
    gain_two = small[GAIN_TWO : GAIN_TWO + 1, :]

    def second_norm(step, carry):
        rows = pl.ds(pl.multiple_of(step * CHUNK, CHUNK), CHUNK)
        unit, scale = normalise(residual[rows, :])
        grad = grad_normed[rows, :]
        total = grad_out[rows, :] + norm_back(grad, unit, scale, gain_two)
        grad_res[rows, :] = total
        low = total.astype(BF16)
        embedded_low[rows, :] = low
        attn_grad[rows, :] = dot_nt(low, proj_weight[...]).astype(BF16)
        gain, shift, bias = carry
        return gain + column_sum(grad * unit), shift + column_sum(grad), bias + column_sum(total)

    none = jnp.zeros((1, D), F32)
    gain, shift, bias = lax.fori_loop(0, ROWS // CHUNK, second_norm, (none, none, none))
    sums[0:1, :] = gain
    sums[1:2, :] = shift
    sums[2:3, :] = bias
    proj_grad[...] = dot_tn(attended[...], embedded_low[...]).astype(BF16)
    first = low_half()
    scaling = jnp.asarray(HEAD_DIM**-0.5, F32)

    def attend(item, carry):
        rows = pl.ds(pl.multiple_of(item * ITEM_ROWS, ITEM_ROWS), ITEM_ROWS)
        for pair in range(PAIRS):
            lanes = [
                slice(part * D + pair * ITEM_ROWS, part * D + (pair + 1) * ITEM_ROWS)
                for part in range(3)
            ]
            queries = stack_heads(qkv[rows, lanes[0]], first)
            keys = qkv[rows, lanes[1]]
            values = qkv[rows, lanes[2]]
            cot = stack_heads(attn_grad[rows, lanes[0]], first)
            spot = pl.multiple_of((item * PAIRS + pair) * CHUNK, CHUNK)
            low = probs[pl.ds(spot, CHUNK), :]
            wide = low.astype(F32)
            grad_probs = dot_nt(cot, values)
            grad_qkv[rows, lanes[2]] = dot_tn(low, cot).astype(BF16)
            centre = jnp.sum(wide * grad_probs, axis=-1, keepdims=True)
            scores_low = (wide * (grad_probs - centre)).astype(BF16)
            grad_queries = join_heads(dot(scores_low, keys), first)
            grad_qkv[rows, lanes[0]] = (grad_queries * scaling).astype(BF16)
            grad_qkv[rows, lanes[1]] = (dot_tn(scores_low, queries) * scaling).astype(BF16)
        return carry

    lax.fori_loop(0, OWN_ITEMS, attend, 0)
    flipped = attn_grad
    flipped[...] = normed_one[...].T

    def weight(step, carry):
        columns = pl.ds(pl.multiple_of(step * CHUNK, CHUNK), CHUNK)
        qkv_grad[:, columns] = dot(flipped[...], grad_qkv[:, columns]).astype(BF16)
        return carry

    lax.fori_loop(0, 3 * D // CHUNK, weight, 0)
    sums[3:4, :] = column_sum(grad_qkv[:, :D].astype(F32))
    sums[4:5, :] = column_sum(grad_qkv[:, 2 * D :].astype(F32))
    gain_one = small[GAIN_ONE : GAIN_ONE + 1, :]

    def first_norm(step, carry):
        rows = pl.ds(pl.multiple_of(step * CHUNK, CHUNK), CHUNK)
        grad = dot_nt(grad_qkv[rows, :], qkv_weight[...])
        unit, scale = normalise(embedded[rows, :])
        total = grad_res[rows, :] + norm_back(grad, unit, scale, gain_one)
        low = total.astype(BF16)
        embedded_low[rows, :] = low
        for group in range(GROUPS):
            grad_inputs[group, rows, :] = dot_nt(low, embed_weight[group]).astype(BF16)
        gain, shift, bias = carry
        return gain + column_sum(grad * unit), shift + column_sum(grad), bias + column_sum(total)

    gain, shift, bias = lax.fori_loop(0, ROWS // CHUNK, first_norm, (none, none, none))
    sums[5:6, :] = gain
    sums[6:7, :] = shift
    sums[7:8, :] = bias
    slots = lax.broadcasted_iota(jnp.int32, (SLOTS, ROWS), 0)
    hot = (position[...] == slots).astype(BF16)
    extra_grad[0:SLOTS, :] = dot(hot, embedded_low[...]).astype(BF16)
    for group in range(GROUPS):
        start = SLOTS + group * WIDTH
        extra_grad[start : start + WIDTH, :] = dot_tn(inputs[group], embedded_low[...]).astype(BF16)


def attention_backward(*operands):
    return call(
        attention_back_kernel,
        (
            shape(D, 3 * D, dtype=BF16),
            shape(D, D, dtype=BF16),
            shape(SLOTS + GROUPS * WIDTH, D, dtype=BF16),
            shape(8, D),
            shape(GROUPS, ROWS, WIDTH, dtype=BF16),
        ),
        15_000_000_000,
        30_000_000,
        scratch_shapes=[
            pltpu.VMEM((ROWS, 3 * D), BF16),
            pltpu.VMEM((ROWS, D), F32),
            pltpu.VMEM((ROWS, D), BF16),
            pltpu.VMEM((ROWS, D), BF16),
        ],
    )(*operands)


def body(
    patches,
    visible,
    recon_cotangent,
    embed_weight,
    embed_bias,
    position_table,
    attn_norm_gain,
    attn_norm_bias,
    qkv_weight,
    qkv_bias,
    proj_weight,
    proj_bias,
    mlp_norm_gain,
    mlp_norm_bias,
    up_weight,
    up_bias,
    down_weight,
    down_bias,
    head_weight,
    head_bias,
):
    my_group = lax.axis_index(VARS_AXES)
    core = lax.axis_index("core")
    batch_items = patches.shape[0]
    patch_count = patches.shape[2]
    batch_rows = batch_items * ITEM_ROWS
    patch_numbers = lax.broadcasted_iota(jnp.int32, (1, 1, patch_count), 2)
    selector = (visible[:, :, None] == patch_numbers).astype(BF16)
    picked = jnp.einsum("bjp,btpf->btjf", selector, patches, preferred_element_type=F32).astype(BF16)

    def exchange(rows):
        return lax.all_to_all(rows.reshape(GROUPS, ROWS, WIDTH), VARS_AXES, 0, 0)

    head_pad = jnp.pad(head_bias, (0, D - WIDTH))[None]
    shards = lax.all_gather(
        jnp.concatenate([embed_weight, head_weight.T, head_pad], axis=0), VARS_AXES, axis=0
    )
    embed_rows = shards[:, :WIDTH]
    head_rows = shards[:, WIDTH : 2 * WIDTH]
    head_biases = shards[:, 2 * WIDTH :, :WIDTH].astype(F32)
    inputs = exchange(picked)
    cotangent = exchange(recon_cotangent)
    own_visible = lax.dynamic_slice_in_dim(visible, my_group * OWN_ITEMS, OWN_ITEMS, 0)
    position = jnp.concatenate([own_visible, own_visible + patch_count], axis=1)
    zero = jnp.zeros((D,), BF16)
    small = jnp.stack(
        [
            embed_bias,
            attn_norm_gain,
            attn_norm_bias,
            proj_bias,
            mlp_norm_gain,
            mlp_norm_bias,
            down_bias,
            zero,
        ]
    ).astype(F32)
    joined_bias = jnp.concatenate([qkv_bias[0], zero, qkv_bias[1]]).astype(F32)[None]

    embedded, normed_one, qkv, probs, attended, residual, normed_two = attention_forward(
        inputs,
        embed_rows,
        position.reshape(ROWS, 1),
        position_table,
        small,
        qkv_weight,
        joined_bias,
        proj_weight,
    )
    activated, slope, recon, head_grad, head_sum, grad_out, down_low, down_sum = mlp_forward(
        normed_two,
        residual,
        up_weight,
        up_bias.astype(F32)[None],
        down_weight,
        small,
        head_rows,
        head_biases,
        cotangent,
    )
    reconstruction = exchange(recon).reshape(batch_items, ITEM_ROWS, WIDTH)

    grad_normed = jnp.zeros((ROWS, D), F32)
    up_parts, down_parts, sum_parts = [], [], []
    for half in (0, 1):
        up_part, down_part, sum_part, grad_normed = mlp_backward(
            jnp.full((1,), half, jnp.int32),
            down_low,
            activated,
            slope,
            normed_two,
            down_weight,
            up_weight,
            grad_normed,
        )
        up_parts.append(up_part)
        down_parts.append(down_part)
        sum_parts.append(sum_part)
    qkv_grad, proj_grad, extra_grad, sums, grad_inputs = attention_backward(
        grad_normed,
        grad_out,
        residual,
        small,
        attended,
        proj_weight,
        qkv,
        probs,
        normed_one,
        qkv_weight,
        embedded,
        inputs,
        embed_rows,
        position.reshape(1, ROWS),
    )
    placed = exchange(grad_inputs).reshape(batch_items, 2, ITEM_ROWS // 2, WIDTH)
    patch_grad = jnp.einsum("bjp,btjf->btpf", selector, placed, preferred_element_type=F32).astype(BF16)

    rest = jnp.concatenate(
        [
            extra_grad,
            head_grad.reshape(GROUPS * WIDTH, D),
            sums.astype(BF16),
            jnp.concatenate(sum_parts, axis=1).reshape(FF // D, D).astype(BF16),
            down_sum.astype(BF16),
            jnp.pad(head_sum.reshape(1, GROUPS * WIDTH), ((0, 0), (0, D - GROUPS * WIDTH))).astype(BF16),
        ],
        axis=0,
    )
    up_parts, down_parts, qkv_grad, proj_grad, rest = lax.psum(
        (up_parts, down_parts, qkv_grad, proj_grad, rest), ALL_AXES
    )
    up_grad = jnp.concatenate([part[i] for part in up_parts for i in range(4)], axis=1)
    down_grad = jnp.concatenate([part.reshape(FF // 2, D) for part in down_parts], axis=0)
    rest = rest.astype(F32)
    start = SLOTS + GROUPS * WIDTH
    embed_grad = lax.dynamic_slice_in_dim(rest, SLOTS + my_group * WIDTH, WIDTH, 0)
    head_grad = lax.dynamic_slice_in_dim(rest, start + my_group * WIDTH, WIDTH, 0).T
    sums = rest[start + GROUPS * WIDTH :]
    head_shift = lax.dynamic_slice_in_dim(sums[13], my_group * WIDTH, WIDTH, 0)
    return (
        reconstruction,
        patch_grad,
        embed_grad,
        sums[7],
        rest[:SLOTS],
        sums[5],
        sums[6],
        qkv_grad.astype(F32),
        sums[3:5],
        proj_grad.astype(F32),
        sums[2],
        sums[0],
        sums[1],
        up_grad.astype(F32),
        sums[8:12].reshape(FF),
        down_grad.astype(F32),
        sums[12],
        head_grad,
        head_shift,
    )


def solution(mesh):
    items, groups = ITEMS_AXES, VARS_AXES
    fine = Mesh(mesh.devices.reshape(4, 2, 4, 2, 2), ALL_AXES)
    in_specs = (
        P(items, None, None, groups),
        P(items, None),
        P(items, None, groups),
        P(groups, None),
        *[P()] * 14,
        P(None, groups),
        P(groups),
    )
    out_specs = (
        P(items, None, groups),
        P(items, None, None, groups),
        P(groups, None),
        *[P()] * 14,
        P(None, groups),
        P(groups),
    )
    return jax.shard_map(body, mesh=fine, in_specs=in_specs, out_specs=out_specs, check_vma=False)
```

```python
import functools

import jax
import jax.numpy as jnp
from jax import lax
from jax.experimental import pallas as pl
from jax.experimental.pallas import tpu as pltpu
from jax.sharding import Mesh
from jax.sharding import PartitionSpec as P

HEADS = 12
HEAD_DIM = 64
D = 768
FF = 3072
ITEM_ROWS = 128
OWN_ITEMS = 6
ROWS = OWN_ITEMS * ITEM_ROWS
GROUPS = 4
WIDTH = 80
PAIRS = HEADS // 2
SLOTS = 512
FF_TILE = 768
CUT = 384
REST = 1280
CHUNK = 256
F32 = jnp.float32
BF16 = jnp.bfloat16
VMEM_LIMIT = 58 * 1024 * 1024

ITEMS_AXES = ("z", "ylo", "x")
VARS_AXES = ("yhi", "core")
ALL_AXES = ITEMS_AXES + VARS_AXES


def dot(left, right):
    return jnp.dot(left, right, preferred_element_type=F32)


def dot_nt(left, right):
    return lax.dot_general(left, right, (((1,), (1,)), ((), ())), preferred_element_type=F32)


def dot_tn(left, right):
    return lax.dot_general(left, right, (((0,), (0,)), ((), ())), preferred_element_type=F32)


def normalise(values):
    centre = values - jnp.mean(values, axis=-1, keepdims=True)
    scale = lax.rsqrt(jnp.mean(centre * centre, axis=-1, keepdims=True) + 1e-06)
    return centre * scale, scale


def norm_back(grad, unit, scale, gain):
    wide = grad * gain
    first = jnp.mean(wide, axis=-1, keepdims=True)
    second = jnp.mean(wide * unit, axis=-1, keepdims=True)
    return scale * (wide - first - unit * second)


def column_sum(values):
    return jnp.sum(values, axis=0, keepdims=True)


def low_half():
    return lax.broadcasted_iota(jnp.int32, (ITEM_ROWS, ITEM_ROWS), 1) < HEAD_DIM


def stack_heads(block, first):
    zero = jnp.zeros_like(block)
    return jnp.concatenate([jnp.where(first, block, zero), jnp.where(first, zero, block)], axis=0)


def join_heads(both, first):
    return jnp.where(first, both[:ITEM_ROWS], both[ITEM_ROWS:])


def call(kernel, out_shape, **kwargs):
    return pl.pallas_call(
        kernel,
        out_shape=out_shape,
        compiler_params=pltpu.CompilerParams(vmem_limit_bytes=VMEM_LIMIT),
        cost_estimate=pl.CostEstimate(flops=1_000_000, bytes_accessed=10_000, transcendentals=0),
        **kwargs,
    )


def shape(*dims, dtype=F32):
    return jax.ShapeDtypeStruct(dims, dtype)


def pick_kernel(me, patches, visible, cotangent, embed_weight, head_rows, head_bias, *outs):
    step = pl.program_id(0)
    inputs_out, cot_out, head_sum = outs[:4], outs[4:8], outs[8]

    @pl.when(step == 0)
    def _():
        head_sum[...] = jnp.zeros_like(head_sum)

    numbers = lax.broadcasted_iota(jnp.int32, (SLOTS // 2, ITEM_ROWS // 2), 0)
    picked = []
    total = jnp.zeros((WIDTH, ITEM_ROWS), F32)
    for item in range(OWN_ITEMS):
        hot = (visible[0, item : item + 1, :] == numbers).astype(BF16)
        rows = [dot(patches[0, item, time], hot) for time in range(2)]
        picked.append(jnp.concatenate(rows, axis=1).astype(BF16))
        total += cotangent[0, item].astype(F32)
    head_sum[...] += total
    for index in range(GROUPS):

        @pl.when(step == index)
        def _():
            for item in range(OWN_ITEMS):
                lanes = slice(item * ITEM_ROWS, (item + 1) * ITEM_ROWS)
                inputs_out[index][0:WIDTH, lanes] = picked[item]
                cot_out[index][0:WIDTH, lanes] = cotangent[0, item]
            inputs_out[index][WIDTH:, :] = embed_weight[...]
            cot_out[index][WIDTH : 2 * WIDTH, :] = head_rows[...]
            cot_out[index][2 * WIDTH :, :] = jnp.zeros((16, D), BF16)
            rows = lax.broadcasted_iota(jnp.int32, (16, WIDTH), 0)
            bias = jnp.where(rows == 0, head_bias[...].astype(F32), 0.0)
            cot_out[index][2 * WIDTH :, 0:WIDTH] = bias.astype(BF16)


def pick(me, patches, visible, cotangent, embed_weight, head_rows, head_bias):
    whole = lambda *dims: pl.BlockSpec(dims, lambda step, me: (0,) * len(dims))

    def part(*dims):
        return pl.BlockSpec((1,) + dims, lambda step, me: (me[0] ^ step,) + (0,) * len(dims))

    outs = call(
        pick_kernel,
        [shape(2 * WIDTH, D, dtype=BF16)] * 4
        + [shape(2 * WIDTH + 16, D, dtype=BF16)] * 4
        + [shape(WIDTH, ITEM_ROWS)],
        grid_spec=pltpu.PrefetchScalarGridSpec(
            num_scalar_prefetch=1,
            grid=(GROUPS,),
            in_specs=[
                part(OWN_ITEMS, 2, WIDTH, SLOTS // 2),
                part(OWN_ITEMS, ITEM_ROWS // 2),
                part(OWN_ITEMS, WIDTH, ITEM_ROWS),
                whole(WIDTH, D),
                whole(WIDTH, D),
                whole(1, WIDTH),
            ],
            out_specs=[whole(2 * WIDTH, D)] * 4
            + [whole(2 * WIDTH + 16, D)] * 4
            + [whole(WIDTH, ITEM_ROWS)],
        ),
    )(me, patches, visible, cotangent, embed_weight, head_rows, head_bias)
    return outs[:4], outs[4:8], outs[8]


def put_kernel(visible, rows, out):
    numbers = lax.broadcasted_iota(jnp.int32, (SLOTS // 2, ITEM_ROWS // 2), 0)
    cut = ITEM_ROWS // 2
    for item in range(OWN_ITEMS):
        hot = (visible[0, item : item + 1, :] == numbers).astype(BF16)
        for time in range(2):
            block = rows[0, item, :, time * cut : (time + 1) * cut]
            out[0, item, time] = dot_nt(block, hot).astype(BF16)


def put(visible, rows):
    def part(*dims):
        return pl.BlockSpec((1,) + dims, lambda step: (step,) + (0,) * len(dims))

    return call(
        put_kernel,
        shape(GROUPS, OWN_ITEMS, 2, WIDTH, SLOTS // 2, dtype=BF16),
        grid=(GROUPS,),
        in_specs=[part(OWN_ITEMS, ITEM_ROWS // 2), part(OWN_ITEMS, WIDTH, ITEM_ROWS)],
        out_specs=part(OWN_ITEMS, 2, WIDTH, SLOTS // 2),
    )(visible, rows)


EMBED_BIAS, GAIN_ONE, SHIFT_ONE, PROJ_BIAS, GAIN_TWO, SHIFT_TWO, DOWN_BIAS, HEAD_BIAS = range(8)


def attention_kernel(
    first_in, second_in, third_in, fourth_in, position, table, small, qkv_weight, qkv_bias, proj_weight,
    embedded, flipped_one, qkv, probs, flipped_attended, residual, normed_two, flipped_two, normed_one, attended,
):
    def embed(step, carry):
        rows = pl.ds(pl.multiple_of(step * CHUNK, CHUNK), CHUNK)
        slots = lax.broadcasted_iota(jnp.int32, (CHUNK, SLOTS), 1)
        hot = (position[rows, :] == slots).astype(BF16)
        total = dot(hot, table[...]) + small[EMBED_BIAS : EMBED_BIAS + 1, :]
        for source in (first_in, second_in, third_in, fourth_in):
            total += dot_tn(source[0:WIDTH, rows], source[WIDTH:, :])
        embedded[rows, :] = total
        unit, _ = normalise(total)
        normed = unit * small[GAIN_ONE : GAIN_ONE + 1, :] + small[SHIFT_ONE : SHIFT_ONE + 1, :]
        normed_one[rows, :] = normed.astype(BF16)
        flipped_one[:, rows] = normed.astype(BF16).T
        return carry

    lax.fori_loop(0, ROWS // CHUNK, embed, 0)

    def project(step, carry):
        columns = pl.ds(pl.multiple_of(step * CHUNK, CHUNK), CHUNK)
        mixed = dot(normed_one[...], qkv_weight[:, columns]) + qkv_bias[:, columns]
        qkv[:, columns] = mixed.astype(BF16)
        return carry

    lax.fori_loop(0, 3 * D // CHUNK, project, 0)
    first = low_half()

    def attend(item, carry):
        rows = pl.ds(pl.multiple_of(item * ITEM_ROWS, ITEM_ROWS), ITEM_ROWS)
        for pair in range(PAIRS):
            lanes = slice(pair * ITEM_ROWS, (pair + 1) * ITEM_ROWS)
            queries = qkv[rows, lanes] * jnp.asarray(HEAD_DIM**-0.5, BF16)
            keys = qkv[rows, D + pair * ITEM_ROWS : D + (pair + 1) * ITEM_ROWS]
            values = qkv[rows, 2 * D + pair * ITEM_ROWS : 2 * D + (pair + 1) * ITEM_ROWS]
            scores = dot_nt(stack_heads(queries, first), keys)
            weights = jnp.exp(scores - jnp.max(scores, axis=-1, keepdims=True))
            weights = weights * (1.0 / jnp.sum(weights, axis=-1, keepdims=True))
            weights = weights.astype(BF16)
            spot = pl.multiple_of((item * PAIRS + pair) * CHUNK, CHUNK)
            probs[pl.ds(spot, CHUNK), :] = weights
            attended[rows, lanes] = join_heads(dot(weights, values), first).astype(BF16)
        return carry

    lax.fori_loop(0, OWN_ITEMS, attend, 0)

    def finish(step, carry):
        rows = pl.ds(pl.multiple_of(step * CHUNK, CHUNK), CHUNK)
        mixed = attended[rows, :]
        flipped_attended[:, rows] = mixed.T
        total = embedded[rows, :] + dot(mixed, proj_weight[...])
        total += small[PROJ_BIAS : PROJ_BIAS + 1, :]
        residual[rows, :] = total
        unit, _ = normalise(total)
        normed = unit * small[GAIN_TWO : GAIN_TWO + 1, :] + small[SHIFT_TWO : SHIFT_TWO + 1, :]
        normed_two[rows, :] = normed.astype(BF16)
        flipped_two[:, rows] = normed.astype(BF16).T
        return carry

    lax.fori_loop(0, ROWS // CHUNK, finish, 0)


def attention_forward(*operands):
    return call(
        attention_kernel,
        (
            shape(ROWS, D),
            shape(D, ROWS, dtype=BF16),
            shape(ROWS, 3 * D, dtype=BF16),
            shape(OWN_ITEMS * PAIRS * CHUNK, ITEM_ROWS, dtype=BF16),
            shape(D, ROWS, dtype=BF16),
            shape(ROWS, D),
            shape(ROWS, D, dtype=BF16),
            shape(D, ROWS, dtype=BF16),
        ),
        scratch_shapes=[pltpu.VMEM((ROWS, D), BF16), pltpu.VMEM((ROWS, D), BF16)],
    )(*operands)


def mlp_kernel(
    place, normed_two, residual, up_weight, up_bias, down_weight, small, head_sum,
    first_in, second_in, third_in, fourth_in,
    slope, down_grad, recon, head_grad, grad_out, down_low, total, low_rows, activated,
):
    step = pl.program_id(0)
    me = place[0]
    bias = up_bias[...]
    sources = (first_in, second_in, third_in, fourth_in)

    @pl.when(step == 0)
    def _():
        total[...] = residual[...] + small[DOWN_BIAS : DOWN_BIAS + 1, :]
        for start in range(0, ROWS, CHUNK):
            rows = slice(start, start + CHUNK)
            grad = jnp.zeros((CHUNK, D), F32)
            for source in sources:
                grad += dot_tn(source[0:WIDTH, rows], source[WIDTH : 2 * WIDTH, :])
            grad_out[rows, :] = grad
            down_low[rows, :] = grad.astype(BF16)

    for start in range(0, ROWS, CHUNK):
        rows = slice(start, start + CHUNK)
        hidden = dot(normed_two[rows, :], up_weight[...]) + bias
        square = hidden * hidden
        inner = 0.7978845608028654 * (1.0 + 0.044715 * square)
        curve = jnp.tanh(hidden * inner)
        half = 0.5 + 0.5 * curve
        low = (hidden * half).astype(BF16)
        activated[rows, :] = low
        rise = 0.7978845608028654 * (1.0 + 3 * 0.044715 * square)
        slope[rows, :] = (half + hidden * half * (1.0 - curve) * rise).astype(BF16)
        total[rows, :] += dot(low, down_weight[...])

    down_grad[...] = dot_tn(activated[...], down_low[...]).astype(BF16)

    @pl.when(step == pl.num_programs(0) - 1)
    def _():
        low_rows[...] = total[...].astype(BF16)
        low = low_rows[...]
        for index, source in enumerate(sources):
            group = me ^ index
            column = source[2 * WIDTH :, 0:ITEM_ROWS].astype(F32).T[0:WIDTH, 0:1]
            made = (dot_nt(source[WIDTH : 2 * WIDTH, :], low) + column).astype(BF16)
            for item in range(OWN_ITEMS):
                block = made[:, item * ITEM_ROWS : (item + 1) * ITEM_ROWS]
                recon[pl.ds(group, 1), item] = block[None]
            rows = pl.ds(pl.multiple_of(group * WIDTH, 16), WIDTH)
            head_grad[rows, :] = dot(source[0:WIDTH, :], low).astype(BF16)
        rows = lax.broadcasted_iota(jnp.int32, (16, D), 0)
        padded = jnp.concatenate([head_sum[...], jnp.zeros((ITEM_ROWS - WIDTH, ITEM_ROWS), F32)], axis=0)
        line = column_sum(padded.T)
        line = jnp.concatenate([line, jnp.zeros((1, D - ITEM_ROWS), F32)], axis=1)
        own = jnp.where(rows == 1 + me, line, 0.0)
        sums = jnp.where(rows == 0, column_sum(grad_out[...]), own)
        head_grad[GROUPS * WIDTH :, :] = sums.astype(BF16)


def mlp_forward(place, *operands):
    whole = lambda *dims: pl.BlockSpec(dims, lambda step, place: (0,) * len(dims))
    columns = lambda rows: pl.BlockSpec((rows, FF_TILE), lambda step, place: (0, step))
    tile = pl.BlockSpec((FF_TILE, D), lambda step, place: (step, 0))
    return call(
        mlp_kernel,
        (
            shape(ROWS, FF, dtype=BF16),
            shape(FF, D, dtype=BF16),
            shape(GROUPS, OWN_ITEMS, WIDTH, ITEM_ROWS, dtype=BF16),
            shape(GROUPS * WIDTH + 16, D, dtype=BF16),
            shape(ROWS, D),
            shape(ROWS, D, dtype=BF16),
        ),
        grid_spec=pltpu.PrefetchScalarGridSpec(
            num_scalar_prefetch=1,
            grid=(FF // FF_TILE,),
            in_specs=[
                whole(ROWS, D),
                whole(ROWS, D),
                columns(D),
                columns(1),
                tile,
                whole(8, D),
                whole(WIDTH, ITEM_ROWS),
            ]
            + [whole(2 * WIDTH + 16, D)] * 4,
            out_specs=[
                columns(ROWS),
                tile,
                whole(GROUPS, OWN_ITEMS, WIDTH, ITEM_ROWS),
                whole(GROUPS * WIDTH + 16, D),
                whole(ROWS, D),
                whole(ROWS, D),
            ],
            scratch_shapes=[
                pltpu.VMEM((ROWS, D), F32),
                pltpu.VMEM((ROWS, D), BF16),
                pltpu.VMEM((ROWS, FF_TILE), BF16),
            ],
        ),
    )(place, *operands)


def mlp_back_kernel(
    down_low, slope, flipped, down_weight, up_weight, up_grad, up_sum, after
):
    @pl.when(pl.program_id(0) == 0)
    def _():
        after[...] = jnp.zeros_like(after)

    grad = dot_nt(down_low[...], down_weight[...]) * slope[...].astype(F32)
    hidden_low = grad.astype(BF16)
    up_sum[...] = column_sum(hidden_low.astype(F32))
    up_grad[...] = dot(flipped[...], hidden_low).astype(BF16)
    after[...] += dot_nt(hidden_low, up_weight[...])


def mlp_backward(*operands):
    whole = pl.BlockSpec((ROWS, D), lambda step: (0, 0))
    columns = lambda rows: pl.BlockSpec((rows, FF_TILE), lambda step: (0, step))
    tile = pl.BlockSpec((FF_TILE, D), lambda step: (step, 0))
    return call(
        mlp_back_kernel,
        (shape(FF, D, dtype=BF16), shape(1, FF), shape(ROWS, D)),
        grid=(FF // FF_TILE,),
        in_specs=[whole, columns(ROWS), whole, tile, columns(D)],
        out_specs=[tile, columns(1), whole],
    )(*operands)


def attention_back_kernel(
    grad_normed, grad_out, residual, small, proj_weight, qkv, probs,
    grads, grad_res, sums, attn_grad,
):
    gain_two = small[GAIN_TWO : GAIN_TWO + 1, :]

    def second_norm(step, carry):
        rows = pl.ds(pl.multiple_of(step * CHUNK, CHUNK), CHUNK)
        unit, scale = normalise(residual[rows, :])
        grad = grad_normed[rows, :]
        total = grad_out[rows, :] + norm_back(grad, unit, scale, gain_two)
        grad_res[rows, :] = total
        low = total.astype(BF16)
        grads[rows, 3 * D :] = low
        attn_grad[rows, :] = dot_nt(low, proj_weight[...]).astype(BF16)
        gain, shift, bias = carry
        return gain + column_sum(grad * unit), shift + column_sum(grad), bias + column_sum(total)

    none = jnp.zeros((1, D), F32)
    gain, shift, bias = lax.fori_loop(0, ROWS // CHUNK, second_norm, (none, none, none))
    sums[0:1, :] = gain
    sums[1:2, :] = shift
    sums[2:3, :] = bias
    first = low_half()
    scaling = jnp.asarray(HEAD_DIM**-0.5, F32)

    def attend(item, carry):
        rows = pl.ds(pl.multiple_of(item * ITEM_ROWS, ITEM_ROWS), ITEM_ROWS)
        for pair in range(PAIRS):
            lanes = [
                slice(part * D + pair * ITEM_ROWS, part * D + (pair + 1) * ITEM_ROWS)
                for part in range(3)
            ]
            queries = stack_heads(qkv[rows, lanes[0]], first)
            keys = qkv[rows, lanes[1]]
            values = qkv[rows, lanes[2]]
            cot = stack_heads(attn_grad[rows, lanes[0]], first)
            spot = pl.multiple_of((item * PAIRS + pair) * CHUNK, CHUNK)
            low = probs[pl.ds(spot, CHUNK), :]
            wide = low.astype(F32)
            grad_probs = dot_nt(cot, values)
            grads[rows, lanes[2]] = dot_tn(low, cot).astype(BF16)
            centre = jnp.sum(wide * grad_probs, axis=-1, keepdims=True)
            scores_low = (wide * (grad_probs - centre)).astype(BF16)
            grad_queries = join_heads(dot(scores_low, keys), first)
            grads[rows, lanes[0]] = (grad_queries * scaling).astype(BF16)
            grads[rows, lanes[1]] = (dot_tn(scores_low, queries) * scaling).astype(BF16)
        return carry

    lax.fori_loop(0, OWN_ITEMS, attend, 0)
    sums[3:4, :] = column_sum(grads[:, :D].astype(F32))
    sums[4:5, :] = column_sum(grads[:, 2 * D : 3 * D].astype(F32))


def attention_backward(*operands):
    return call(
        attention_back_kernel,
        (shape(ROWS, 4 * D, dtype=BF16), shape(ROWS, D), shape(8, D)),
        scratch_shapes=[pltpu.VMEM((ROWS, D), BF16)],
    )(*operands)


def weight_kernel(grads, flipped_one, flipped_attended, out):
    step = pl.program_id(0)

    def write(left):
        out[...] = dot(left[...], grads[...]).astype(BF16)

    pl.when(step < 3)(lambda: write(flipped_one))
    pl.when(step == 3)(lambda: write(flipped_attended))


def weight_gradients(*operands):
    whole = pl.BlockSpec((D, ROWS), lambda step: (0, 0))
    return call(
        weight_kernel,
        shape(4 * D, D, dtype=BF16),
        grid=(4,),
        in_specs=[pl.BlockSpec((ROWS, D), lambda step: (0, step)), whole, whole],
        out_specs=pl.BlockSpec((D, D), lambda step: (step, 0)),
    )(*operands)


EMBED_AT = SLOTS
HEAD_AT = EMBED_AT + GROUPS * WIDTH
SUMS_AT = HEAD_AT + GROUPS * WIDTH + 16


def embed_back_kernel(
    place, grads, qkv_weight, embedded, grad_res, small, first_in, second_in, third_in, fourth_in,
    position, up_sum, sums, head_grad,
    out, grad_inputs, embedded_low, rest,
):
    gain_one = small[GAIN_ONE : GAIN_ONE + 1, :]
    me = place[0]
    sources = (first_in, second_in, third_in, fourth_in)

    def first_norm(step, carry):
        rows = pl.ds(pl.multiple_of(step * CHUNK, CHUNK), CHUNK)
        grad = dot_nt(grads[rows, : 3 * D], qkv_weight[...])
        unit, scale = normalise(embedded[rows, :])
        total = grad_res[rows, :] + norm_back(grad, unit, scale, gain_one)
        low = total.astype(BF16)
        embedded_low[rows, :] = low
        for index, source in enumerate(sources):
            made = dot_nt(source[WIDTH:, :], low).astype(BF16)
            for part in range(CHUNK // ITEM_ROWS):
                block = made[:, part * ITEM_ROWS : (part + 1) * ITEM_ROWS]
                item = step * (CHUNK // ITEM_ROWS) + part
                grad_inputs[pl.ds(me ^ index, 1), pl.ds(item, 1)] = block[None, None]
        gain, shift, bias = carry
        return gain + column_sum(grad * unit), shift + column_sum(grad), bias + column_sum(total)

    none = jnp.zeros((1, D), F32)
    gain, shift, bias = lax.fori_loop(0, ROWS // CHUNK, first_norm, (none, none, none))
    slots = lax.broadcasted_iota(jnp.int32, (SLOTS, ROWS), 0)
    hot = (position[...] == slots).astype(BF16)
    rest[0:SLOTS, :] = dot(hot, embedded_low[...])
    for index, source in enumerate(sources):
        rows = pl.ds(pl.multiple_of(EMBED_AT + (me ^ index) * WIDTH, 16), WIDTH)
        rest[rows, :] = dot(source[0:WIDTH, :], embedded_low[...])
    rest[HEAD_AT:SUMS_AT, :] = head_grad[...].astype(F32)
    rest[SUMS_AT:, :] = jnp.zeros((REST - SUMS_AT, D), F32)
    for row, value in enumerate((gain, shift, bias)):
        rest[SUMS_AT + row : SUMS_AT + row + 1, :] = value
    rest[SUMS_AT + 3 : SUMS_AT + 8, :] = sums[0:5, :]
    for row in range(FF // D):
        at = SUMS_AT + 8 + row
        rest[at : at + 1, :] = up_sum[:, row * D : (row + 1) * D]
    out[...] = rest[...].astype(BF16)


def embed_backward(place, *operands):
    vmem = pl.BlockSpec(memory_space=pltpu.VMEM)
    return call(
        embed_back_kernel,
        (
            shape(REST, D, dtype=BF16),
            shape(GROUPS, OWN_ITEMS, WIDTH, ITEM_ROWS, dtype=BF16),
        ),
        in_specs=[pl.BlockSpec(memory_space=pltpu.SMEM)] + [vmem] * len(operands),
        out_specs=[vmem] * 2,
        scratch_shapes=[pltpu.VMEM((ROWS, D), BF16), pltpu.VMEM((REST, D), F32)],
    )(place, *operands)


def widen_kernel(down, up, mixed, down_out, up_out, qkv_out, proj_out):
    step = pl.program_id(0)

    def write(source, out):
        out[...] = source[...].astype(F32)

    pl.when(step < 4)(lambda: write(down, down_out))
    pl.when(jnp.logical_and(step >= 4, step < 8))(lambda: write(up, up_out))
    pl.when(jnp.logical_and(step >= 8, step < 11))(lambda: write(mixed, qkv_out))
    pl.when(step == 11)(lambda: write(mixed, proj_out))


def widen(*tiles):
    turn = lambda step, first, count: jnp.clip(step - first, 0, count - 1)
    below = lambda first, count: pl.BlockSpec((D, D), lambda step: (turn(step, first, count), 0))
    beside = lambda first, count: pl.BlockSpec((D, D), lambda step: (0, turn(step, first, count)))
    return call(
        widen_kernel,
        (shape(FF, D), shape(D, FF), shape(D, 3 * D), shape(D, D)),
        grid=(12,),
        in_specs=[below(0, 4), below(4, 4), below(8, 4)],
        out_specs=[below(0, 4), beside(4, 4), beside(8, 3), below(11, 1)],
    )(*tiles)


def tie(value, *tokens):
    return lax.optimization_barrier((value, tokens))[0]


def sum_over_devices(values):
    devices = lax.axis_size(ALL_AXES)
    parts = values.reshape(devices, -1, ITEM_ROWS)
    parts = lax.all_to_all(parts, ALL_AXES, 0, 0)
    share = jnp.sum(parts.astype(F32), axis=0).astype(BF16)
    parts = lax.all_to_all(jnp.broadcast_to(share[None], parts.shape), ALL_AXES, 0, 0)
    return parts.reshape(values.shape)


def body(
    patches,
    visible,
    recon_cotangent,
    embed_weight,
    embed_bias,
    position_table,
    attn_norm_gain,
    attn_norm_bias,
    qkv_weight,
    qkv_bias,
    proj_weight,
    proj_bias,
    mlp_norm_gain,
    mlp_norm_bias,
    up_weight,
    up_bias,
    down_weight,
    down_bias,
    head_weight,
    head_bias,
):
    my_group = lax.axis_index(VARS_AXES)
    me = my_group.astype(jnp.int32).reshape(1)
    batch_items = patches.shape[0]
    patch_count = patches.shape[2]

    def exchange(rows):
        return lax.all_to_all(rows, VARS_AXES, 0, 0)

    def partners(blocks):
        swap = [(0, 1), (1, 0)]
        return [
            blocks[0],
            lax.ppermute(blocks[1], "core", swap),
            lax.ppermute(blocks[2], "yhi", swap),
            lax.ppermute(blocks[3], ("yhi", "core"), [(i, 3 - i) for i in range(4)]),
        ]

    items_visible = visible.reshape(GROUPS, OWN_ITEMS, ITEM_ROWS // 2)
    to_embed, to_head, head_sum = pick(
        me,
        jnp.swapaxes(patches, 2, 3).reshape(GROUPS, OWN_ITEMS, 2, WIDTH, patch_count),
        items_visible,
        jnp.swapaxes(recon_cotangent, 1, 2).reshape(GROUPS, OWN_ITEMS, WIDTH, ITEM_ROWS),
        embed_weight,
        head_weight.T,
        head_bias[None],
    )
    for_embed = partners(to_embed)
    for_head = partners([tie(block, for_embed) for block in to_head])
    own_visible = lax.dynamic_slice_in_dim(visible, my_group * OWN_ITEMS, OWN_ITEMS, 0)
    position = jnp.concatenate([own_visible, own_visible + patch_count], axis=1)
    zero = jnp.zeros((D,), BF16)
    small = jnp.stack(
        [
            embed_bias,
            attn_norm_gain,
            attn_norm_bias,
            proj_bias,
            mlp_norm_gain,
            mlp_norm_bias,
            down_bias,
            zero,
        ]
    ).astype(F32)
    joined_bias = jnp.concatenate([qkv_bias[0], zero, qkv_bias[1]]).astype(F32)[None]

    (
        embedded,
        flipped_one,
        qkv,
        probs,
        flipped_attended,
        residual,
        normed_two,
        flipped_two,
    ) = attention_forward(
        *for_embed,
        position.reshape(ROWS, 1),
        position_table,
        small,
        qkv_weight,
        joined_bias,
        proj_weight,
    )
    slope, down_grad, recon, head_grad, grad_out, down_low = mlp_forward(
        me,
        normed_two,
        residual,
        up_weight,
        up_bias.astype(F32)[None],
        down_weight,
        small,
        head_sum,
        *for_head,
    )
    recon = exchange(recon)
    up_grad, up_sum, grad_normed = mlp_backward(
        down_low, slope, flipped_two, down_weight, up_weight
    )
    grads, grad_res, sums = attention_backward(
        tie(grad_normed, recon), grad_out, residual, small, proj_weight, qkv, probs
    )
    mixed_grad = weight_gradients(grads, flipped_one, flipped_attended)
    rest, grad_inputs = embed_backward(
        me,
        grads,
        qkv_weight,
        embedded,
        grad_res,
        small,
        *for_embed,
        position.reshape(1, ROWS),
        up_sum,
        sums,
        head_grad,
    )
    down_grad, up_grad, mixed_grad = lax.psum((down_grad, up_grad, mixed_grad), ALL_AXES)
    rest = sum_over_devices(rest)
    placed = exchange(tie(grad_inputs, rest))
    patch_grad = put(items_visible, placed).reshape(batch_items, 2, WIDTH, patch_count)
    patch_grad = jnp.swapaxes(patch_grad, 2, 3)
    down_grad, up_grad, qkv_grad, proj_grad = widen(down_grad, up_grad, mixed_grad)
    rest = rest[: SUMS_AT + 16].astype(F32)
    embed_grad = lax.dynamic_slice_in_dim(rest, EMBED_AT + my_group * WIDTH, WIDTH, 0)
    total = rest[SUMS_AT : SUMS_AT + 16]
    early = rest[SUMS_AT - 16 : SUMS_AT]
    head_shift = lax.dynamic_index_in_dim(early, 1 + my_group, 0, False)[:WIDTH]
    head_grad = lax.dynamic_slice_in_dim(rest, HEAD_AT + my_group * WIDTH, WIDTH, 0).T
    return (
        jnp.swapaxes(recon.reshape(batch_items, WIDTH, ITEM_ROWS), 1, 2),
        patch_grad,
        embed_grad,
        total[2],
        rest[:SLOTS],
        total[0],
        total[1],
        qkv_grad,
        total[6:8],
        proj_grad,
        total[5],
        total[3],
        total[4],
        up_grad,
        total[8:12].reshape(FF),
        down_grad,
        early[0],
        head_grad,
        head_shift,
    )


def solution(mesh):
    items, groups = ITEMS_AXES, VARS_AXES
    fine = Mesh(mesh.devices.reshape(4, 2, 4, 2, 2), ALL_AXES)
    in_specs = (
        P(items, None, None, groups),
        P(items, None),
        P(items, None, groups),
        P(groups, None),
        *[P()] * 14,
        P(None, groups),
        P(groups),
    )
    out_specs = (
        P(items, None, groups),
        P(items, None, None, groups),
        P(groups, None),
        *[P()] * 14,
        P(None, groups),
        P(groups),
    )
    return jax.shard_map(body, mesh=fine, in_specs=in_specs, out_specs=out_specs, check_vma=False)
```

```python
import functools

import jax
import jax.numpy as jnp
from jax import lax
from jax.experimental import pallas as pl
from jax.experimental.pallas import tpu as pltpu
from jax.sharding import Mesh
from jax.sharding import PartitionSpec as P

HEADS = 12
HEAD_DIM = 64
D = 768
FF = 3072
ITEM_ROWS = 128
OWN_ITEMS = 6
ROWS = OWN_ITEMS * ITEM_ROWS
GROUPS = 4
WIDTH = 80
PAIRS = HEADS // 2
SLOTS = 512
FF_TILE = 768
CUT = 384
REST = 1280
CHUNK = 256
F32 = jnp.float32
BF16 = jnp.bfloat16
VMEM_LIMIT = 58 * 1024 * 1024

ITEMS_AXES = ("z", "ylo", "x")
VARS_AXES = ("yhi", "core")
ALL_AXES = ITEMS_AXES + VARS_AXES


def dot(left, right):
    return jnp.dot(left, right, preferred_element_type=F32)


def dot_nt(left, right):
    return lax.dot_general(left, right, (((1,), (1,)), ((), ())), preferred_element_type=F32)


def dot_tn(left, right):
    return lax.dot_general(left, right, (((0,), (0,)), ((), ())), preferred_element_type=F32)


def normalise(values):
    centre = values - jnp.mean(values, axis=-1, keepdims=True)
    scale = lax.rsqrt(jnp.mean(centre * centre, axis=-1, keepdims=True) + 1e-06)
    return centre * scale, scale


def norm_back(grad, unit, scale, gain):
    wide = grad * gain
    first = jnp.mean(wide, axis=-1, keepdims=True)
    second = jnp.mean(wide * unit, axis=-1, keepdims=True)
    return scale * (wide - first - unit * second)


def column_sum(values):
    return jnp.sum(values, axis=0, keepdims=True)


def low_half():
    return lax.broadcasted_iota(jnp.int32, (ITEM_ROWS, ITEM_ROWS), 1) < HEAD_DIM


def stack_heads(block, first):
    zero = jnp.zeros_like(block)
    return jnp.concatenate([jnp.where(first, block, zero), jnp.where(first, zero, block)], axis=0)


def join_heads(both, first):
    return jnp.where(first, both[:ITEM_ROWS], both[ITEM_ROWS:])


def call(kernel, out_shape, **kwargs):
    return pl.pallas_call(
        kernel,
        out_shape=out_shape,
        compiler_params=pltpu.CompilerParams(vmem_limit_bytes=VMEM_LIMIT),
        cost_estimate=pl.CostEstimate(flops=1_000_000, bytes_accessed=10_000, transcendentals=0),
        **kwargs,
    )


def shape(*dims, dtype=F32):
    return jax.ShapeDtypeStruct(dims, dtype)


def by_partner(*dims):
    return pl.BlockSpec((1,) + dims, lambda step, me: (me[0] ^ step,) + (0,) * len(dims))


def throughout(*dims):
    return pl.BlockSpec(dims, lambda step, me: (0,) * len(dims))


def pick_kernel(me, patches, visible, *outs):
    step = pl.program_id(0)
    numbers = lax.broadcasted_iota(jnp.int32, (SLOTS // 2, ITEM_ROWS // 2), 0)
    first = (me[0] ^ step) * OWN_ITEMS
    picked = []
    for item in range(OWN_ITEMS):
        hot = (visible[pl.ds(first + item, 1), :] == numbers).astype(BF16)
        rows = [dot(patches[0, item, time], hot) for time in range(2)]
        picked.append(jnp.concatenate(rows, axis=1).astype(BF16))
    for index, out in enumerate(outs):

        @pl.when(step == index)
        def _():
            for item in range(OWN_ITEMS):
                out[:, item * ITEM_ROWS : (item + 1) * ITEM_ROWS] = picked[item]


def pick(me, patches, visible):
    return call(
        pick_kernel,
        [shape(WIDTH, D, dtype=BF16)] * 4,
        grid_spec=pltpu.PrefetchScalarGridSpec(
            num_scalar_prefetch=1,
            grid=(GROUPS,),
            in_specs=[
                by_partner(OWN_ITEMS, 2, WIDTH, SLOTS // 2),
                throughout(GROUPS * OWN_ITEMS, ITEM_ROWS // 2),
            ],
            out_specs=[throughout(WIDTH, D)] * 4,
        ),
    )(me, patches, visible)


def turn_kernel(me, cotangent, head_rows, head_bias, *outs):
    step = pl.program_id(0)
    head_sum = outs[4]

    @pl.when(step == 0)
    def _():
        head_sum[...] = jnp.zeros_like(head_sum)

    total = jnp.zeros((WIDTH, ITEM_ROWS), F32)
    for item in range(OWN_ITEMS):
        total += cotangent[0, item].astype(F32)
    head_sum[...] += total
    for index, out in enumerate(outs[:4]):

        @pl.when(step == index)
        def _():
            for item in range(OWN_ITEMS):
                out[0:WIDTH, item * ITEM_ROWS : (item + 1) * ITEM_ROWS] = cotangent[0, item]
            out[WIDTH : 2 * WIDTH, :] = head_rows[...]
            out[2 * WIDTH :, :] = jnp.zeros((16, D), BF16)
            rows = lax.broadcasted_iota(jnp.int32, (16, WIDTH), 0)
            bias = jnp.where(rows == 0, head_bias[...].astype(F32), 0.0)
            out[2 * WIDTH :, 0:WIDTH] = bias.astype(BF16)


def turn(me, cotangent, head_rows, head_bias):
    outs = call(
        turn_kernel,
        [shape(2 * WIDTH + 16, D, dtype=BF16)] * 4 + [shape(WIDTH, ITEM_ROWS)],
        grid_spec=pltpu.PrefetchScalarGridSpec(
            num_scalar_prefetch=1,
            grid=(GROUPS,),
            in_specs=[
                by_partner(OWN_ITEMS, WIDTH, ITEM_ROWS),
                throughout(WIDTH, D),
                throughout(1, WIDTH),
            ],
            out_specs=[throughout(2 * WIDTH + 16, D)] * 4 + [throughout(WIDTH, ITEM_ROWS)],
        ),
    )(me, cotangent, head_rows, head_bias)
    return outs[:4], outs[4]


def put_kernel(visible, rows, out):
    numbers = lax.broadcasted_iota(jnp.int32, (SLOTS // 2, ITEM_ROWS // 2), 0)
    cut = ITEM_ROWS // 2
    for item in range(OWN_ITEMS):
        hot = (visible[0, item : item + 1, :] == numbers).astype(BF16)
        for time in range(2):
            block = rows[0, item, :, time * cut : (time + 1) * cut]
            out[0, item, time] = dot_nt(block, hot).astype(BF16)


def put(visible, rows):
    def part(*dims):
        return pl.BlockSpec((1,) + dims, lambda step: (step,) + (0,) * len(dims))

    return call(
        put_kernel,
        shape(GROUPS, OWN_ITEMS, 2, WIDTH, SLOTS // 2, dtype=BF16),
        grid=(GROUPS,),
        in_specs=[part(OWN_ITEMS, ITEM_ROWS // 2), part(OWN_ITEMS, WIDTH, ITEM_ROWS)],
        out_specs=part(OWN_ITEMS, 2, WIDTH, SLOTS // 2),
    )(visible, rows)


EMBED_BIAS, GAIN_ONE, SHIFT_ONE, PROJ_BIAS, GAIN_TWO, SHIFT_TWO, DOWN_BIAS, HEAD_BIAS = range(8)


PARTS = ROWS // CHUNK
CHUNK_ITEMS = CHUNK // ITEM_ROWS
TILES = FF // FF_TILE


def whole(*dims):
    return pl.BlockSpec(dims, lambda *step: (0,) * len(dims), pipeline_mode=pl.Buffered(1))


def held(*dims):
    return pl.BlockSpec(dims, lambda *step: (0,) * len(dims))


def rows_at(first, rows, width, count):
    return pl.BlockSpec((rows, width), lambda step, *_: (jnp.clip(step - first, 0, count - 1), 0))


def columns_at(first, rows, width, count):
    return pl.BlockSpec((rows, width), lambda step, *_: (0, jnp.clip(step - first, 0, count - 1)))


def attention_kernel(
    first_in, second_in, third_in, fourth_in, first_weight, second_weight, third_weight, fourth_weight,
    position, table, small, qkv_far, qkv_bias, proj_far,
    unit_one, scale_one, flipped_one, qkv, probs, flipped_attended, residual, unit_two, scale_two,
    normed_two, flipped_two,
    embedded, attended, qkv_weight, proj_weight, arrivals,
):
    step = pl.program_id(0)
    first = low_half()
    picked = (first_in, second_in, third_in, fourth_in)
    embeds = (first_weight, second_weight, third_weight, fourth_weight)
    qkv_copy = pltpu.make_async_copy(qkv_far, qkv_weight, arrivals.at[0])
    proj_copy = pltpu.make_async_copy(proj_far, proj_weight, arrivals.at[1])

    @pl.when(step == 0)
    def _():
        qkv_copy.start()
        proj_copy.start()

    here = pl.ds(pl.multiple_of(step * CHUNK, CHUNK), CHUNK)
    slots = lax.broadcasted_iota(jnp.int32, (CHUNK, SLOTS), 1)
    hot = (position[...] == slots).astype(BF16)
    values = dot(hot, table[...]) + small[EMBED_BIAS : EMBED_BIAS + 1, :]
    for source, weight in zip(picked, embeds):
        values += dot_tn(source[:, here], weight[...])
    embedded[...] = values
    unit, scale = normalise(values)
    unit_one[...] = unit.astype(BF16)
    scale_one[...] = jnp.broadcast_to(scale, (CHUNK, ITEM_ROWS))
    normed = unit * small[GAIN_ONE : GAIN_ONE + 1, :] + small[SHIFT_ONE : SHIFT_ONE + 1, :]
    normed = normed.astype(BF16)
    flipped_one[...] = normed.T
    pl.when(step == 0)(qkv_copy.wait)
    for part in range(3):
        columns = slice(part * D, (part + 1) * D)
        mixed = dot(normed, qkv_weight[:, columns]) + qkv_bias[:, columns]
        qkv[:, columns] = mixed.astype(BF16)
    for item in range(CHUNK_ITEMS):
        rows = slice(item * ITEM_ROWS, (item + 1) * ITEM_ROWS)
        for pair in range(PAIRS):
            lanes = [
                slice(part * D + pair * ITEM_ROWS, part * D + (pair + 1) * ITEM_ROWS)
                for part in range(3)
            ]
            queries = qkv[rows, lanes[0]] * jnp.asarray(HEAD_DIM**-0.5, BF16)
            scores = dot_nt(stack_heads(queries, first), qkv[rows, lanes[1]])
            weights = jnp.exp(scores - jnp.max(scores, axis=-1, keepdims=True))
            weights = weights * (1.0 / jnp.sum(weights, axis=-1, keepdims=True))
            weights = weights.astype(BF16)
            spot = (item * PAIRS + pair) * CHUNK
            probs[spot : spot + CHUNK, :] = weights
            made = join_heads(dot(weights, qkv[rows, lanes[2]]), first)
            attended[rows, lanes[0]] = made.astype(BF16)
    mixed = attended[...]
    flipped_attended[...] = mixed.T
    pl.when(step == 0)(proj_copy.wait)
    values = embedded[...] + dot(mixed, proj_weight[...]) + small[PROJ_BIAS : PROJ_BIAS + 1, :]
    residual[...] = values + small[DOWN_BIAS : DOWN_BIAS + 1, :]
    unit, scale = normalise(values)
    unit_two[...] = unit.astype(BF16)
    scale_two[...] = jnp.broadcast_to(scale, (CHUNK, ITEM_ROWS))
    normed = unit * small[GAIN_TWO : GAIN_TWO + 1, :] + small[SHIFT_TWO : SHIFT_TWO + 1, :]
    normed = normed.astype(BF16)
    normed_two[...] = normed
    flipped_two[...] = normed.T


def attention(*operands):
    far = pl.BlockSpec(memory_space=pl.ANY)
    return call(
        attention_kernel,
        (
            shape(ROWS, D, dtype=BF16),
            shape(ROWS, ITEM_ROWS),
            shape(D, ROWS, dtype=BF16),
            shape(ROWS, 3 * D, dtype=BF16),
            shape(OWN_ITEMS * PAIRS * CHUNK, ITEM_ROWS, dtype=BF16),
            shape(D, ROWS, dtype=BF16),
            shape(ROWS, D),
            shape(ROWS, D, dtype=BF16),
            shape(ROWS, ITEM_ROWS),
            shape(ROWS, D, dtype=BF16),
            shape(D, ROWS, dtype=BF16),
        ),
        grid=(PARTS,),
        in_specs=[whole(WIDTH, D)] * 8
        + [
            rows_at(0, CHUNK, 1, PARTS),
            whole(SLOTS, D),
            whole(8, D),
            far,
            whole(1, 3 * D),
            far,
        ],
        out_specs=[
            rows_at(0, CHUNK, D, PARTS),
            rows_at(0, CHUNK, ITEM_ROWS, PARTS),
            columns_at(0, D, CHUNK, PARTS),
            rows_at(0, CHUNK, 3 * D, PARTS),
            rows_at(0, CHUNK_ITEMS * PAIRS * CHUNK, ITEM_ROWS, PARTS),
            columns_at(0, D, CHUNK, PARTS),
            rows_at(0, CHUNK, D, PARTS),
            rows_at(0, CHUNK, D, PARTS),
            rows_at(0, CHUNK, ITEM_ROWS, PARTS),
            rows_at(0, CHUNK, D, PARTS),
            columns_at(0, D, CHUNK, PARTS),
        ],
        scratch_shapes=[
            pltpu.VMEM((CHUNK, D), F32),
            pltpu.VMEM((CHUNK, D), BF16),
            pltpu.VMEM((D, 3 * D), BF16),
            pltpu.VMEM((D, D), BF16),
            pltpu.SemaphoreType.DMA((2,)),
        ],
    )(*operands)


BACK = TILES
LAST = BACK + TILES + PARTS


def block_kernel(
    me, normed_two, residual_far, up_weight, up_bias, down_weight, head_sum, first_cot, second_cot, third_cot,
    fourth_cot, flipped_two_far, unit_two, scale_two, small, proj_far, qkv, probs, flipped_one_far,
    flipped_attended_far,
    down_grad, recon, head_grad, up_grad, up_sum, grad_qkv, grad_res, sums, mixed_grad,
    total, activated, slope, down_low, attn_grad, residual, flipped_two, proj_weight, flipped_one,
    flipped_attended, arrivals,
):
    step = pl.program_id(0)
    first = low_half()
    pairs = (
        (residual_far, residual),
        (flipped_two_far, flipped_two),
        (proj_far, proj_weight),
        (flipped_one_far, flipped_one),
        (flipped_attended_far, flipped_attended),
    )
    copies = [
        pltpu.make_async_copy(source, target, arrivals.at[index])
        for index, (source, target) in enumerate(pairs)
    ]
    residual_copy, flipped_two_copy, proj_copy, flipped_one_copy, flipped_attended_copy = copies

    @pl.when(step == 0)
    def _():
        for copy in copies:
            copy.start()
        for start in range(0, ROWS, CHUNK):
            rows = slice(start, start + CHUNK)
            grad = jnp.zeros((CHUNK, D), F32)
            for source in (first_cot, second_cot, third_cot, fourth_cot):
                grad += dot_tn(source[0:WIDTH, rows], source[WIDTH : 2 * WIDTH, :])
            down_low[rows, :] = grad.astype(BF16)
            line = column_sum(grad)
            if start:
                line += head_grad[GROUPS * WIDTH : GROUPS * WIDTH + 1, :]
            head_grad[GROUPS * WIDTH : GROUPS * WIDTH + 1, :] = line
        head_grad[GROUPS * WIDTH + 1 :, :] = jnp.zeros((15, D), F32)

    @pl.when(step < TILES)
    def _():
        bias = up_bias[...]
        tile = pl.ds(pl.multiple_of(step * FF_TILE, FF_TILE), FF_TILE)
        for start in range(0, ROWS, CHUNK):
            rows = slice(start, start + CHUNK)
            hidden = dot(normed_two[rows, :], up_weight[...]) + bias
            square = hidden * hidden
            inner = 0.7978845608028654 + (0.7978845608028654 * 0.044715) * square
            curve = jnp.tanh(hidden * inner)
            half = 0.5 + 0.5 * curve
            made = hidden * half
            low = made.astype(BF16)
            activated[rows, :] = low
            rise = 0.7978845608028654 + (0.7978845608028654 * 3 * 0.044715) * square
            slope[rows, tile] = (half + made * (rise - rise * curve)).astype(BF16)
            made = dot(low, down_weight[...])
            total[rows, :] = jnp.where(step == 0, made, total[rows, :] + made)
        down_grad[...] = dot_tn(activated[...], down_low[...]).astype(BF16)

    @pl.when(step == TILES - 1)
    def _():
        residual_copy.wait()
        low = (total[...] + residual[...]).astype(BF16)
        for index, source in enumerate((first_cot, second_cot, third_cot, fourth_cot)):
            group = me[0] ^ index
            column = source[2 * WIDTH :, 0:ITEM_ROWS].astype(F32).T[0:WIDTH, 0:1]
            made = (dot_nt(source[WIDTH : 2 * WIDTH, :], low) + column).astype(BF16)
            for item in range(OWN_ITEMS):
                block = made[:, item * ITEM_ROWS : (item + 1) * ITEM_ROWS]
                recon[pl.ds(group, 1), item] = block[None]
            rows = pl.ds(pl.multiple_of(group * WIDTH, 16), WIDTH)
            head_grad[rows, :] = dot(source[0:WIDTH, :], low)
        rows = lax.broadcasted_iota(jnp.int32, (16, D), 0)
        padded = jnp.concatenate([head_sum[...], jnp.zeros((ITEM_ROWS - WIDTH, ITEM_ROWS), F32)], axis=0)
        line = column_sum(padded.T)
        line = jnp.concatenate([line, jnp.zeros((1, D - ITEM_ROWS), F32)], axis=1)
        head_grad[GROUPS * WIDTH :, :] += jnp.where(rows == 1 + me[0], line, 0.0)
        sums[...] = jnp.zeros_like(sums)

    @pl.when(jnp.logical_and(step >= BACK, step < BACK + TILES))
    def _():
        tile = pl.ds(pl.multiple_of((step - BACK) * FF_TILE, FF_TILE), FF_TILE)
        grad = dot_nt(down_low[...], down_weight[...]) * slope[:, tile].astype(F32)
        hidden_low = grad.astype(BF16)
        pl.when(step == BACK)(flipped_two_copy.wait)
        up_sum[...] = column_sum(hidden_low.astype(F32))
        up_grad[...] = dot(flipped_two[...], hidden_low).astype(BF16)
        made = dot_nt(hidden_low, up_weight[...])
        total[...] = jnp.where(step == BACK, made, total[...] + made)

    @pl.when(jnp.logical_and(step >= BACK + TILES, step < LAST))
    def _():
        part = step - BACK - TILES
        pl.when(step == BACK + TILES)(proj_copy.wait)
        here = pl.ds(pl.multiple_of(part * CHUNK, CHUNK), CHUNK)
        unit = unit_two[...].astype(F32)
        grad = total[here, :]
        back = norm_back(grad, unit, scale_two[:, 0:1], small[GAIN_TWO : GAIN_TWO + 1, :])
        back += down_low[here, :].astype(F32)
        grad_res[...] = back
        low = back.astype(BF16)
        slope[here, 3 * D :] = low
        attn_grad[...] = dot_nt(low, proj_weight[...]).astype(BF16)
        sums[0:1, :] += column_sum(grad * unit)
        sums[1:2, :] += column_sum(grad)
        sums[2:3, :] += column_sum(back)
        scaling = jnp.asarray(HEAD_DIM**-0.5, F32)
        for item in range(CHUNK_ITEMS):
            rows = slice(item * ITEM_ROWS, (item + 1) * ITEM_ROWS)
            for pair in range(PAIRS):
                lanes = [
                    slice(kind * D + pair * ITEM_ROWS, kind * D + (pair + 1) * ITEM_ROWS)
                    for kind in range(3)
                ]
                queries = stack_heads(qkv[rows, lanes[0]], first)
                cot = stack_heads(attn_grad[rows, lanes[0]], first)
                spot = (item * PAIRS + pair) * CHUNK
                low = probs[spot : spot + CHUNK, :]
                wide = low.astype(F32)
                grad_probs = dot_nt(cot, qkv[rows, lanes[2]])
                grad_qkv[rows, lanes[2]] = dot_tn(low, cot).astype(BF16)
                centre = jnp.sum(wide * grad_probs, axis=-1, keepdims=True)
                scores_low = (wide * (grad_probs - centre)).astype(BF16)
                made = join_heads(dot(scores_low, qkv[rows, lanes[1]]), first)
                grad_qkv[rows, lanes[0]] = (made * scaling).astype(BF16)
                made = dot_tn(scores_low, queries) * scaling
                grad_qkv[rows, lanes[1]] = made.astype(BF16)
        slope[here, : 3 * D] = grad_qkv[...]
        sums[3:4, :] += column_sum(grad_qkv[:, :D].astype(F32))
        sums[4:5, :] += column_sum(grad_qkv[:, 2 * D :].astype(F32))

    for tile in range(4):

        @pl.when(step == LAST + tile)
        def _():
            if tile == 0:
                flipped_one_copy.wait()
            if tile == 3:
                flipped_attended_copy.wait()
            left = flipped_one if tile < 3 else flipped_attended
            made = dot(left[...], slope[:, tile * D : (tile + 1) * D])
            mixed_grad[...] = made.astype(BF16)


def block(me, *operands):
    def again(step):
        return jnp.where(step < BACK, step, jnp.clip(step - BACK, 0, TILES - 1))

    far = pl.BlockSpec(memory_space=pl.ANY)
    return call(
        block_kernel,
        (
            shape(FF, D, dtype=BF16),
            shape(GROUPS, OWN_ITEMS, WIDTH, ITEM_ROWS, dtype=BF16),
            shape(GROUPS * WIDTH + 16, D),
            shape(FF, D, dtype=BF16),
            shape(1, FF),
            shape(ROWS, 3 * D, dtype=BF16),
            shape(ROWS, D),
            shape(8, D),
            shape(4 * D, D, dtype=BF16),
        ),
        grid_spec=pltpu.PrefetchScalarGridSpec(
            num_scalar_prefetch=1,
            grid=(LAST + 4,),
            in_specs=[
                whole(ROWS, D),
                far,
                pl.BlockSpec((D, FF_TILE), lambda step, me: (0, again(step))),
                columns_at(0, 1, FF_TILE, TILES),
                pl.BlockSpec((FF_TILE, D), lambda step, me: (again(step), 0)),
                whole(WIDTH, ITEM_ROWS),
            ]
            + [whole(2 * WIDTH + 16, D)] * 4
            + [
                far,
                rows_at(BACK + TILES, CHUNK, D, PARTS),
                rows_at(BACK + TILES, CHUNK, ITEM_ROWS, PARTS),
                whole(8, D),
                far,
                rows_at(BACK + TILES, CHUNK, 3 * D, PARTS),
                rows_at(BACK + TILES, CHUNK_ITEMS * PAIRS * CHUNK, ITEM_ROWS, PARTS),
                far,
                far,
            ],
            out_specs=[
                rows_at(0, FF_TILE, D, TILES),
                held(GROUPS, OWN_ITEMS, WIDTH, ITEM_ROWS),
                held(GROUPS * WIDTH + 16, D),
                rows_at(BACK, FF_TILE, D, TILES),
                columns_at(BACK, 1, FF_TILE, TILES),
                rows_at(BACK + TILES, CHUNK, 3 * D, PARTS),
                rows_at(BACK + TILES, CHUNK, D, PARTS),
                held(8, D),
                rows_at(LAST, D, D, 4),
            ],
            scratch_shapes=[
                pltpu.VMEM((ROWS, D), F32),
                pltpu.VMEM((ROWS, FF_TILE), BF16),
                pltpu.VMEM((ROWS, FF), BF16),
                pltpu.VMEM((ROWS, D), BF16),
                pltpu.VMEM((CHUNK, D), BF16),
                pltpu.VMEM((ROWS, D), F32),
                pltpu.VMEM((D, ROWS), BF16),
                pltpu.VMEM((D, D), BF16),
                pltpu.VMEM((D, ROWS), BF16),
                pltpu.VMEM((D, ROWS), BF16),
                pltpu.SemaphoreType.DMA((5,)),
            ],
        ),
    )(me, *operands)


EMBED_AT = SLOTS
HEAD_AT = EMBED_AT + GROUPS * WIDTH
SUMS_AT = HEAD_AT + GROUPS * WIDTH + 16


def embed_back_kernel(
    place, grads, qkv_weight, unit_one, scale_one, grad_res, small, first_in, second_in, third_in, fourth_in,
    first_weight, second_weight, third_weight, fourth_weight, position, up_sum, sums, head_grad,
    out, grad_inputs, embedded_low, rest,
):
    gain_one = small[GAIN_ONE : GAIN_ONE + 1, :]
    me = place[0]
    sources = (first_in, second_in, third_in, fourth_in)

    def first_norm(step, carry):
        rows = pl.ds(pl.multiple_of(step * CHUNK, CHUNK), CHUNK)
        grad = dot_nt(grads[rows, :], qkv_weight[...])
        unit = unit_one[rows, :].astype(F32)
        total = grad_res[rows, :] + norm_back(grad, unit, scale_one[rows, 0:1], gain_one)
        low = total.astype(BF16)
        embedded_low[rows, :] = low
        for index, weight in enumerate((first_weight, second_weight, third_weight, fourth_weight)):
            made = dot_nt(weight[...], low).astype(BF16)
            for part in range(CHUNK // ITEM_ROWS):
                block = made[:, part * ITEM_ROWS : (part + 1) * ITEM_ROWS]
                item = step * (CHUNK // ITEM_ROWS) + part
                grad_inputs[pl.ds(me ^ index, 1), pl.ds(item, 1)] = block[None, None]
        gain, shift, bias = carry
        return gain + column_sum(grad * unit), shift + column_sum(grad), bias + column_sum(total)

    none = jnp.zeros((1, D), F32)
    gain, shift, bias = lax.fori_loop(0, ROWS // CHUNK, first_norm, (none, none, none))
    slots = lax.broadcasted_iota(jnp.int32, (SLOTS, ROWS), 0)
    hot = (position[...] == slots).astype(BF16)
    rest[0:SLOTS, :] = dot(hot, embedded_low[...])
    for index, source in enumerate(sources):
        rows = pl.ds(pl.multiple_of(EMBED_AT + (me ^ index) * WIDTH, 16), WIDTH)
        rest[rows, :] = dot(source[...], embedded_low[...])
    rest[HEAD_AT:SUMS_AT, :] = head_grad[...]
    rest[SUMS_AT:, :] = jnp.zeros((REST - SUMS_AT, D), F32)
    for row, value in enumerate((gain, shift, bias)):
        rest[SUMS_AT + row : SUMS_AT + row + 1, :] = value
    rest[SUMS_AT + 3 : SUMS_AT + 8, :] = sums[0:5, :]
    for row in range(FF // D):
        at = SUMS_AT + 8 + row
        rest[at : at + 1, :] = up_sum[:, row * D : (row + 1) * D]
    out[...] = rest[...].astype(BF16)


def embed_backward(place, *operands):
    vmem = pl.BlockSpec(memory_space=pltpu.VMEM)
    return call(
        embed_back_kernel,
        (
            shape(REST, D, dtype=BF16),
            shape(GROUPS, OWN_ITEMS, WIDTH, ITEM_ROWS, dtype=BF16),
        ),
        in_specs=[pl.BlockSpec(memory_space=pltpu.SMEM)] + [vmem] * len(operands),
        out_specs=[vmem] * 2,
        scratch_shapes=[pltpu.VMEM((ROWS, D), BF16), pltpu.VMEM((REST, D), F32)],
    )(place, *operands)


WIDEN_STEPS = 6


def widen_kernel(down, up, mixed, down_out, up_out, qkv_out, proj_out):
    down_out[...] = down[...].astype(F32)
    for tile in range(4):
        lanes = slice(tile * D, (tile + 1) * D)
        up_out[:, lanes] = up[tile].astype(F32)
        if tile < 3:
            qkv_out[:, lanes] = mixed[tile].astype(F32)
    proj_out[...] = mixed[3].astype(F32)


def widen(down, up, mixed):
    rows = D // WIDEN_STEPS
    tiles = pl.BlockSpec((4, rows, D), lambda step: (0, step, 0))
    block = lambda rows, width: pl.BlockSpec((rows, width), lambda step: (step, 0))
    return call(
        widen_kernel,
        (shape(FF, D), shape(D, FF), shape(D, 3 * D), shape(D, D)),
        grid=(WIDEN_STEPS,),
        in_specs=[block(4 * rows, D), tiles, tiles],
        out_specs=[block(4 * rows, D), block(rows, FF), block(rows, 3 * D), block(rows, D)],
    )(down, up.reshape(4, D, D), mixed.reshape(4, D, D))


def tie(value, *tokens):
    return lax.optimization_barrier((value, tokens))[0]


def sum_over_devices(values):
    plane = ("z", "ylo", "yhi")
    core, place = lax.axis_index("core"), lax.axis_index("x")
    swap = [(0, 1), (1, 0)]
    rows, width = values.shape
    cut, quarter = width // 2, rows // 4

    def shift(value, distance):
        return lax.ppermute(value, "x", [(i, (i + distance) % 4) for i in range(4)])

    send = lax.dynamic_slice_in_dim(values, (1 - core) * cut, cut, 1)
    own = lax.dynamic_slice_in_dim(values, core * cut, cut, 1).astype(F32)
    own = (own + lax.ppermute(send, "core", swap).astype(F32)).astype(BF16)
    part = lambda step: lax.dynamic_slice_in_dim(own, ((place + step) % 4) * quarter, quarter, 0)
    total = part(0).astype(F32)
    for distance in (1, 3, 2):
        total += shift(part(distance), distance).astype(F32)
    parts = total.astype(BF16).reshape(16, -1, ITEM_ROWS)
    parts = lax.all_to_all(parts, plane, 0, 0)
    share = jnp.sum(parts.astype(F32), axis=0).astype(BF16)
    parts = lax.all_to_all(jnp.broadcast_to(share[None], parts.shape), plane, 0, 0)
    own = parts.reshape(quarter, cut)
    turned = [own, shift(own, 3), shift(own, 2), shift(own, 1)]
    turned = jnp.concatenate(turned + turned[:3], axis=0)
    own = lax.dynamic_slice_in_dim(turned, ((4 - place) % 4) * quarter, rows, 0)
    other = lax.ppermute(own, "core", swap)
    first = core == 0
    return jnp.concatenate([jnp.where(first, own, other), jnp.where(first, other, own)], axis=1)


def body(
    patches,
    visible,
    recon_cotangent,
    embed_weight,
    embed_bias,
    position_table,
    attn_norm_gain,
    attn_norm_bias,
    qkv_weight,
    qkv_bias,
    proj_weight,
    proj_bias,
    mlp_norm_gain,
    mlp_norm_bias,
    up_weight,
    up_bias,
    down_weight,
    down_bias,
    head_weight,
    head_bias,
):
    my_group = lax.axis_index(VARS_AXES)
    me = my_group.astype(jnp.int32).reshape(1)
    batch_items = patches.shape[0]
    patch_count = patches.shape[2]

    def exchange(rows):
        return lax.all_to_all(rows, VARS_AXES, 0, 0)

    def partners(blocks):
        swap = [(0, 1), (1, 0)]
        return [
            blocks[0],
            lax.ppermute(blocks[1], "core", swap),
            lax.ppermute(blocks[2], "yhi", swap),
            lax.ppermute(blocks[3], ("yhi", "core"), [(i, 3 - i) for i in range(4)]),
        ]

    items_visible = visible.reshape(GROUPS, OWN_ITEMS, ITEM_ROWS // 2)
    swap = [(0, 1), (1, 0)]
    far_embed = lax.ppermute(embed_weight, "yhi", swap)
    near_embed = lax.ppermute(embed_weight, "core", swap)
    to_embed = pick(
        me, jnp.swapaxes(patches, 2, 3).reshape(GROUPS, OWN_ITEMS, 2, WIDTH, patch_count), visible
    )
    picked = partners(to_embed)
    embeds = [embed_weight, near_embed, far_embed, lax.ppermute(far_embed, "core", swap)]
    for_embed = [*picked, *embeds]
    to_head, head_sum = turn(
        me,
        jnp.swapaxes(recon_cotangent, 1, 2).reshape(GROUPS, OWN_ITEMS, WIDTH, ITEM_ROWS),
        head_weight.T,
        tie(head_bias[None], picked[1]),
    )
    for_head = partners(to_head)
    own_visible = lax.dynamic_slice_in_dim(visible, my_group * OWN_ITEMS, OWN_ITEMS, 0)
    position = jnp.concatenate([own_visible, own_visible + patch_count], axis=1)
    zero = jnp.zeros((D,), BF16)
    small = jnp.stack(
        [
            embed_bias,
            attn_norm_gain,
            attn_norm_bias,
            proj_bias,
            mlp_norm_gain,
            mlp_norm_bias,
            down_bias,
            zero,
        ]
    ).astype(F32)
    joined_bias = jnp.concatenate([qkv_bias[0], zero, qkv_bias[1]]).astype(F32)[None]

    (
        unit_one,
        scale_one,
        flipped_one,
        qkv,
        probs,
        flipped_attended,
        residual,
        unit_two,
        scale_two,
        normed_two,
        flipped_two,
    ) = attention(
        *for_embed,
        position.reshape(ROWS, 1),
        position_table,
        small,
        qkv_weight,
        joined_bias,
        proj_weight,
    )
    down_grad, recon, head_grad, up_grad, up_sum, grad_qkv, grad_res, sums, mixed_grad = block(
        me,
        normed_two,
        residual,
        up_weight,
        up_bias.astype(F32)[None],
        down_weight,
        head_sum,
        *for_head,
        flipped_two,
        unit_two,
        scale_two,
        small,
        proj_weight,
        qkv,
        probs,
        flipped_one,
        flipped_attended,
    )
    rest, grad_inputs = embed_backward(
        me,
        grad_qkv,
        qkv_weight,
        unit_one,
        scale_one,
        grad_res,
        small,
        *for_embed,
        position.reshape(1, ROWS),
        up_sum,
        sums,
        head_grad,
    )
    down_grad, up_grad, mixed_grad = lax.psum((down_grad, up_grad, mixed_grad), ALL_AXES)
    rest = sum_over_devices(rest)
    recon = exchange(tie(recon, rest))
    placed = exchange(tie(grad_inputs, recon))
    patch_grad = put(items_visible, placed).reshape(batch_items, 2, WIDTH, patch_count)
    patch_grad = jnp.swapaxes(patch_grad, 2, 3)
    down_grad, up_grad, qkv_grad, proj_grad = widen(down_grad, up_grad, mixed_grad)
    rest = rest[: SUMS_AT + 16].astype(F32)
    embed_grad = lax.dynamic_slice_in_dim(rest, EMBED_AT + my_group * WIDTH, WIDTH, 0)
    total = rest[SUMS_AT : SUMS_AT + 16]
    early = rest[SUMS_AT - 16 : SUMS_AT]
    head_shift = lax.dynamic_index_in_dim(early, 1 + my_group, 0, False)[:WIDTH]
    head_grad = lax.dynamic_slice_in_dim(rest, HEAD_AT + my_group * WIDTH, WIDTH, 0).T
    return (
        jnp.swapaxes(recon.reshape(batch_items, WIDTH, ITEM_ROWS), 1, 2),
        patch_grad,
        embed_grad,
        total[2],
        rest[:SLOTS],
        total[0],
        total[1],
        qkv_grad,
        total[6:8],
        proj_grad,
        total[5],
        total[3],
        total[4],
        up_grad,
        total[8:12].reshape(FF),
        down_grad,
        early[0],
        head_grad,
        head_shift,
    )


def solution(mesh):
    items, groups = ITEMS_AXES, VARS_AXES
    fine = Mesh(mesh.devices.reshape(4, 2, 4, 2, 2), ALL_AXES)
    in_specs = (
        P(items, None, None, groups),
        P(items, None),
        P(items, None, groups),
        P(groups, None),
        *[P()] * 14,
        P(None, groups),
        P(groups),
    )
    out_specs = (
        P(items, None, groups),
        P(items, None, None, groups),
        P(groups, None),
        *[P()] * 14,
        P(None, groups),
        P(groups),
    )
    return jax.shard_map(body, mesh=fine, in_specs=in_specs, out_specs=out_specs, check_vma=False)
```

```python
import functools

import jax
import jax.numpy as jnp
from jax import lax
from jax.experimental import pallas as pl
from jax.experimental.pallas import tpu as pltpu
from jax.sharding import Mesh
from jax.sharding import PartitionSpec as P

HEADS = 12
HEAD_DIM = 64
D = 768
FF = 3072
ITEM_ROWS = 128
OWN_ITEMS = 6
ROWS = OWN_ITEMS * ITEM_ROWS
GROUPS = 4
WIDTH = 80
PAIRS = HEADS // 2
SLOTS = 512
FF_TILE = 768
CUT = 384
REST = 1280
CHUNK = 256
F32 = jnp.float32
BF16 = jnp.bfloat16
VMEM_LIMIT = 58 * 1024 * 1024

ITEMS_AXES = ("z", "ylo", "x")
VARS_AXES = ("yhi", "core")
ALL_AXES = ITEMS_AXES + VARS_AXES


def dot(left, right):
    return jnp.dot(left, right, preferred_element_type=F32)


def dot_nt(left, right):
    return lax.dot_general(left, right, (((1,), (1,)), ((), ())), preferred_element_type=F32)


def dot_tn(left, right):
    return lax.dot_general(left, right, (((0,), (0,)), ((), ())), preferred_element_type=F32)


def normalise(values):
    centre = values - jnp.mean(values, axis=-1, keepdims=True)
    scale = lax.rsqrt(jnp.mean(centre * centre, axis=-1, keepdims=True) + 1e-06)
    return centre * scale, scale


def norm_back(grad, unit, scale, gain):
    wide = grad * gain
    first = jnp.mean(wide, axis=-1, keepdims=True)
    second = jnp.mean(wide * unit, axis=-1, keepdims=True)
    return scale * (wide - first - unit * second)


def column_sum(values):
    return jnp.sum(values, axis=0, keepdims=True)


def low_half():
    return lax.broadcasted_iota(jnp.int32, (ITEM_ROWS, ITEM_ROWS), 1) < HEAD_DIM


def stack_heads(block, first):
    zero = jnp.zeros_like(block)
    return jnp.concatenate([jnp.where(first, block, zero), jnp.where(first, zero, block)], axis=0)


def join_heads(both, first):
    return jnp.where(first, both[:ITEM_ROWS], both[ITEM_ROWS:])


def call(kernel, out_shape, **kwargs):
    return pl.pallas_call(
        kernel,
        out_shape=out_shape,
        compiler_params=pltpu.CompilerParams(vmem_limit_bytes=VMEM_LIMIT),
        cost_estimate=pl.CostEstimate(flops=1_000_000, bytes_accessed=10_000, transcendentals=0),
        **kwargs,
    )


def shape(*dims, dtype=F32):
    return jax.ShapeDtypeStruct(dims, dtype)


def by_partner(*dims):
    return pl.BlockSpec((1,) + dims, lambda step, me: (me[0] ^ step,) + (0,) * len(dims))


def throughout(*dims):
    return pl.BlockSpec(dims, lambda step, me: (0,) * len(dims))


def pick_kernel(me, patches, visible, cotangent, head_rows, head_bias, *outs):
    step = pl.program_id(0)
    head_sum = outs[8]
    numbers = lax.broadcasted_iota(jnp.int32, (SLOTS // 2, ITEM_ROWS // 2), 0)
    first = (me[0] ^ step) * OWN_ITEMS
    picked = []
    total = jnp.zeros((WIDTH, ITEM_ROWS), F32)
    for item in range(OWN_ITEMS):
        hot = (visible[pl.ds(first + item, 1), :] == numbers).astype(BF16)
        rows = [dot(patches[0, item, time], hot) for time in range(2)]
        picked.append(jnp.concatenate(rows, axis=1).astype(BF16))
        total += cotangent[0, item].astype(F32)
    head_sum[...] = jnp.where(step == 0, total, head_sum[...] + total)
    for index in range(GROUPS):

        @pl.when(step == index)
        def _():
            out, cot_out = outs[index], outs[GROUPS + index]
            for item in range(OWN_ITEMS):
                lanes = slice(item * ITEM_ROWS, (item + 1) * ITEM_ROWS)
                out[:, lanes] = picked[item]
                cot_out[0:WIDTH, lanes] = cotangent[0, item]
            cot_out[WIDTH : 2 * WIDTH, :] = head_rows[...]
            cot_out[2 * WIDTH :, :] = jnp.zeros((16, D), BF16)
            rows = lax.broadcasted_iota(jnp.int32, (16, WIDTH), 0)
            bias = jnp.where(rows == 0, head_bias[...].astype(F32), 0.0)
            cot_out[2 * WIDTH :, 0:WIDTH] = bias.astype(BF16)


def pick(me, patches, visible, cotangent, head_rows, head_bias):
    outs = call(
        pick_kernel,
        [shape(WIDTH, D, dtype=BF16)] * 4
        + [shape(2 * WIDTH + 16, D, dtype=BF16)] * 4
        + [shape(WIDTH, ITEM_ROWS)],
        grid_spec=pltpu.PrefetchScalarGridSpec(
            num_scalar_prefetch=1,
            grid=(GROUPS,),
            in_specs=[
                by_partner(OWN_ITEMS, 2, WIDTH, SLOTS // 2),
                throughout(GROUPS * OWN_ITEMS, ITEM_ROWS // 2),
                by_partner(OWN_ITEMS, WIDTH, ITEM_ROWS),
                throughout(WIDTH, D),
                throughout(1, WIDTH),
            ],
            out_specs=[throughout(WIDTH, D)] * 4
            + [throughout(2 * WIDTH + 16, D)] * 4
            + [throughout(WIDTH, ITEM_ROWS)],
        ),
    )(me, patches, visible, cotangent, head_rows, head_bias)
    return outs[:4], outs[4:8], outs[8]


def put_kernel(visible, rows, out):
    numbers = lax.broadcasted_iota(jnp.int32, (SLOTS // 2, ITEM_ROWS // 2), 0)
    cut = ITEM_ROWS // 2
    for item in range(OWN_ITEMS):
        hot = (visible[0, item : item + 1, :] == numbers).astype(BF16)
        for time in range(2):
            block = rows[0, item, :, time * cut : (time + 1) * cut]
            out[0, item, time] = dot_nt(block, hot).astype(BF16)


def put(visible, rows):
    def part(*dims):
        return pl.BlockSpec((1,) + dims, lambda step: (step,) + (0,) * len(dims))

    return call(
        put_kernel,
        shape(GROUPS, OWN_ITEMS, 2, WIDTH, SLOTS // 2, dtype=BF16),
        grid=(GROUPS,),
        in_specs=[part(OWN_ITEMS, ITEM_ROWS // 2), part(OWN_ITEMS, WIDTH, ITEM_ROWS)],
        out_specs=part(OWN_ITEMS, 2, WIDTH, SLOTS // 2),
    )(visible, rows)


EMBED_BIAS, GAIN_ONE, SHIFT_ONE, PROJ_BIAS, GAIN_TWO, SHIFT_TWO, DOWN_BIAS, HEAD_BIAS = range(8)


PARTS = ROWS // CHUNK
CHUNK_ITEMS = CHUNK // ITEM_ROWS
TILES = FF // FF_TILE


def whole(*dims):
    return pl.BlockSpec(dims, lambda *step: (0,) * len(dims), pipeline_mode=pl.Buffered(1))


def held(*dims):
    return pl.BlockSpec(dims, lambda *step: (0,) * len(dims))


def rows_at(first, rows, width, count):
    return pl.BlockSpec((rows, width), lambda step, *_: (jnp.clip(step - first, 0, count - 1), 0))


def columns_at(first, rows, width, count):
    return pl.BlockSpec((rows, width), lambda step, *_: (0, jnp.clip(step - first, 0, count - 1)))


def attention_kernel(
    first_in, second_in, third_in, fourth_in, first_weight, second_weight, third_weight, fourth_weight,
    position, table, small, qkv_far, qkv_bias, proj_far,
    unit_one, scale_one, flipped_one, qkv, probs, flipped_attended, residual, unit_two, scale_two,
    normed_two, flipped_two,
    embedded, attended, qkv_weight, proj_weight, arrivals,
):
    step = pl.program_id(0)
    first = low_half()
    picked = (first_in, second_in, third_in, fourth_in)
    embeds = (first_weight, second_weight, third_weight, fourth_weight)
    qkv_copy = pltpu.make_async_copy(qkv_far, qkv_weight, arrivals.at[0])
    proj_copy = pltpu.make_async_copy(proj_far, proj_weight, arrivals.at[1])

    @pl.when(step == 0)
    def _():
        qkv_copy.start()
        proj_copy.start()

    here = pl.ds(pl.multiple_of(step * CHUNK, CHUNK), CHUNK)
    slots = lax.broadcasted_iota(jnp.int32, (CHUNK, SLOTS), 1)
    hot = (position[...] == slots).astype(BF16)
    values = dot(hot, table[...]) + small[EMBED_BIAS : EMBED_BIAS + 1, :]
    for source, weight in zip(picked, embeds):
        values += dot_tn(source[:, here], weight[...])
    embedded[...] = values
    unit, scale = normalise(values)
    unit_one[...] = unit.astype(BF16)
    scale_one[...] = jnp.broadcast_to(scale, (CHUNK, ITEM_ROWS))
    normed = unit * small[GAIN_ONE : GAIN_ONE + 1, :] + small[SHIFT_ONE : SHIFT_ONE + 1, :]
    normed = normed.astype(BF16)
    flipped_one[...] = normed.T
    pl.when(step == 0)(qkv_copy.wait)
    for part in range(3):
        columns = slice(part * D, (part + 1) * D)
        mixed = dot(normed, qkv_weight[:, columns]) + qkv_bias[:, columns]
        qkv[:, columns] = mixed.astype(BF16)
    for item in range(CHUNK_ITEMS):
        rows = slice(item * ITEM_ROWS, (item + 1) * ITEM_ROWS)
        for pair in range(PAIRS):
            lanes = [
                slice(part * D + pair * ITEM_ROWS, part * D + (pair + 1) * ITEM_ROWS)
                for part in range(3)
            ]
            queries = qkv[rows, lanes[0]] * jnp.asarray(HEAD_DIM**-0.5, BF16)
            scores = dot_nt(stack_heads(queries, first), qkv[rows, lanes[1]])
            weights = jnp.exp(scores - jnp.max(scores, axis=-1, keepdims=True))
            weights = weights * (1.0 / jnp.sum(weights, axis=-1, keepdims=True))
            weights = weights.astype(BF16)
            spot = (item * PAIRS + pair) * CHUNK
            probs[spot : spot + CHUNK, :] = weights
            made = join_heads(dot(weights, qkv[rows, lanes[2]]), first)
            attended[rows, lanes[0]] = made.astype(BF16)
    mixed = attended[...]
    flipped_attended[...] = mixed.T
    pl.when(step == 0)(proj_copy.wait)
    values = embedded[...] + dot(mixed, proj_weight[...]) + small[PROJ_BIAS : PROJ_BIAS + 1, :]
    residual[...] = values + small[DOWN_BIAS : DOWN_BIAS + 1, :]
    unit, scale = normalise(values)
    unit_two[...] = unit.astype(BF16)
    scale_two[...] = jnp.broadcast_to(scale, (CHUNK, ITEM_ROWS))
    normed = unit * small[GAIN_TWO : GAIN_TWO + 1, :] + small[SHIFT_TWO : SHIFT_TWO + 1, :]
    normed = normed.astype(BF16)
    normed_two[...] = normed
    flipped_two[...] = normed.T


def attention(*operands):
    far = pl.BlockSpec(memory_space=pl.ANY)
    return call(
        attention_kernel,
        (
            shape(ROWS, D, dtype=BF16),
            shape(ROWS, ITEM_ROWS),
            shape(D, ROWS, dtype=BF16),
            shape(ROWS, 3 * D, dtype=BF16),
            shape(OWN_ITEMS * PAIRS * CHUNK, ITEM_ROWS, dtype=BF16),
            shape(D, ROWS, dtype=BF16),
            shape(ROWS, D),
            shape(ROWS, D, dtype=BF16),
            shape(ROWS, ITEM_ROWS),
            shape(ROWS, D, dtype=BF16),
            shape(D, ROWS, dtype=BF16),
        ),
        grid=(PARTS,),
        in_specs=[whole(WIDTH, D)] * 8
        + [
            rows_at(0, CHUNK, 1, PARTS),
            whole(SLOTS, D),
            whole(8, D),
            far,
            whole(1, 3 * D),
            far,
        ],
        out_specs=[
            rows_at(0, CHUNK, D, PARTS),
            rows_at(0, CHUNK, ITEM_ROWS, PARTS),
            columns_at(0, D, CHUNK, PARTS),
            rows_at(0, CHUNK, 3 * D, PARTS),
            rows_at(0, CHUNK_ITEMS * PAIRS * CHUNK, ITEM_ROWS, PARTS),
            columns_at(0, D, CHUNK, PARTS),
            rows_at(0, CHUNK, D, PARTS),
            rows_at(0, CHUNK, D, PARTS),
            rows_at(0, CHUNK, ITEM_ROWS, PARTS),
            rows_at(0, CHUNK, D, PARTS),
            columns_at(0, D, CHUNK, PARTS),
        ],
        scratch_shapes=[
            pltpu.VMEM((CHUNK, D), F32),
            pltpu.VMEM((CHUNK, D), BF16),
            pltpu.VMEM((D, 3 * D), BF16),
            pltpu.VMEM((D, D), BF16),
            pltpu.SemaphoreType.DMA((2,)),
        ],
    )(*operands)


def feed_forward_kernel(
    me, normed_two, residual_far, up_weight, up_bias, down_weight, head_sum, first_cot, second_cot, third_cot,
    fourth_cot, flipped_far,
    down_grad, recon, head_grad, up_grad, up_sum, down_low, total,
    activated, slope, residual, flipped, arrivals,
):
    step = pl.program_id(0)
    residual_copy = pltpu.make_async_copy(residual_far, residual, arrivals.at[0])
    flipped_copy = pltpu.make_async_copy(flipped_far, flipped, arrivals.at[1])

    @pl.when(step == 0)
    def _():
        residual_copy.start()
        flipped_copy.start()
        for start in range(0, ROWS, CHUNK):
            rows = slice(start, start + CHUNK)
            grad = jnp.zeros((CHUNK, D), F32)
            for source in (first_cot, second_cot, third_cot, fourth_cot):
                grad += dot_tn(source[0:WIDTH, rows], source[WIDTH : 2 * WIDTH, :])
            down_low[rows, :] = grad.astype(BF16)
            line = column_sum(grad)
            if start:
                line += head_grad[GROUPS * WIDTH : GROUPS * WIDTH + 1, :]
            head_grad[GROUPS * WIDTH : GROUPS * WIDTH + 1, :] = line
        head_grad[GROUPS * WIDTH + 1 :, :] = jnp.zeros((15, D), F32)

    @pl.when(step < TILES)
    def _():
        bias = up_bias[...]
        tile = pl.ds(pl.multiple_of(step * FF_TILE, FF_TILE), FF_TILE)
        for start in range(0, ROWS, CHUNK):
            rows = slice(start, start + CHUNK)
            hidden = dot(normed_two[rows, :], up_weight[...]) + bias
            square = hidden * hidden
            inner = 0.7978845608028654 + (0.7978845608028654 * 0.044715) * square
            curve = jnp.tanh(hidden * inner)
            half = 0.5 + 0.5 * curve
            made = hidden * half
            low = made.astype(BF16)
            activated[rows, :] = low
            rise = 0.7978845608028654 + (0.7978845608028654 * 3 * 0.044715) * square
            slope[rows, tile] = (half + made * (rise - rise * curve)).astype(BF16)
            made = dot(low, down_weight[...])
            total[rows, :] = jnp.where(step == 0, made, total[rows, :] + made)
        down_grad[...] = dot_tn(activated[...], down_low[...]).astype(BF16)

    @pl.when(step == TILES - 1)
    def _():
        residual_copy.wait()
        low = (total[...] + residual[...]).astype(BF16)
        for index, source in enumerate((first_cot, second_cot, third_cot, fourth_cot)):
            group = me[0] ^ index
            column = source[2 * WIDTH :, 0:ITEM_ROWS].astype(F32).T[0:WIDTH, 0:1]
            made = (dot_nt(source[WIDTH : 2 * WIDTH, :], low) + column).astype(BF16)
            for item in range(OWN_ITEMS):
                block = made[:, item * ITEM_ROWS : (item + 1) * ITEM_ROWS]
                recon[pl.ds(group, 1), item] = block[None]
            rows = pl.ds(pl.multiple_of(group * WIDTH, 16), WIDTH)
            head_grad[rows, :] = dot(source[0:WIDTH, :], low)
        rows = lax.broadcasted_iota(jnp.int32, (16, D), 0)
        padded = jnp.concatenate([head_sum[...], jnp.zeros((ITEM_ROWS - WIDTH, ITEM_ROWS), F32)], axis=0)
        line = column_sum(padded.T)
        line = jnp.concatenate([line, jnp.zeros((1, D - ITEM_ROWS), F32)], axis=1)
        head_grad[GROUPS * WIDTH :, :] += jnp.where(rows == 1 + me[0], line, 0.0)

    @pl.when(step >= TILES)
    def _():
        tile = pl.ds(pl.multiple_of((step - TILES) * FF_TILE, FF_TILE), FF_TILE)
        grad = dot_nt(down_low[...], down_weight[...]) * slope[:, tile].astype(F32)
        hidden_low = grad.astype(BF16)
        pl.when(step == TILES)(flipped_copy.wait)
        up_sum[...] = column_sum(hidden_low.astype(F32))
        up_grad[...] = dot(flipped[...], hidden_low).astype(BF16)
        made = dot_nt(hidden_low, up_weight[...])
        total[...] = jnp.where(step == TILES, made, total[...] + made)


def feed_forward(me, *operands):
    again = lambda step: step % TILES
    far = pl.BlockSpec(memory_space=pl.ANY)
    return call(
        feed_forward_kernel,
        (
            shape(FF, D, dtype=BF16),
            shape(GROUPS, OWN_ITEMS, WIDTH, ITEM_ROWS, dtype=BF16),
            shape(GROUPS * WIDTH + 16, D),
            shape(FF, D, dtype=BF16),
            shape(1, FF),
            shape(ROWS, D, dtype=BF16),
            shape(ROWS, D),
        ),
        grid_spec=pltpu.PrefetchScalarGridSpec(
            num_scalar_prefetch=1,
            grid=(2 * TILES,),
            in_specs=[
                whole(ROWS, D),
                far,
                pl.BlockSpec((D, FF_TILE), lambda step, me: (0, again(step))),
                columns_at(0, 1, FF_TILE, TILES),
                pl.BlockSpec((FF_TILE, D), lambda step, me: (again(step), 0)),
                whole(WIDTH, ITEM_ROWS),
            ]
            + [whole(2 * WIDTH + 16, D)] * 4
            + [far],
            out_specs=[
                rows_at(0, FF_TILE, D, TILES),
                held(GROUPS, OWN_ITEMS, WIDTH, ITEM_ROWS),
                held(GROUPS * WIDTH + 16, D),
                rows_at(TILES, FF_TILE, D, TILES),
                columns_at(TILES, 1, FF_TILE, TILES),
                held(ROWS, D),
                held(ROWS, D),
            ],
            scratch_shapes=[
                pltpu.VMEM((ROWS, FF_TILE), BF16),
                pltpu.VMEM((ROWS, FF), BF16),
                pltpu.VMEM((ROWS, D), F32),
                pltpu.VMEM((D, ROWS), BF16),
                pltpu.SemaphoreType.DMA((2,)),
            ],
        ),
    )(me, *operands)


def attention_back_kernel(
    grad_normed, down_low, unit_two, scale_two, small, proj_weight, qkv, probs, flipped_one_far,
    flipped_attended_far,
    grad_qkv, grad_res, sums, mixed_grad,
    grads, attn_grad, flipped_one, flipped_attended, arrivals,
):
    step = pl.program_id(0)
    first = low_half()
    flipped_one_copy = pltpu.make_async_copy(flipped_one_far, flipped_one, arrivals.at[0])
    flipped_attended_copy = pltpu.make_async_copy(
        flipped_attended_far, flipped_attended, arrivals.at[1]
    )

    @pl.when(step == 0)
    def _():
        flipped_one_copy.start()
        flipped_attended_copy.start()
        sums[...] = jnp.zeros_like(sums)

    @pl.when(step < PARTS)
    def _():
        here = pl.ds(pl.multiple_of(step * CHUNK, CHUNK), CHUNK)
        unit = unit_two[...].astype(F32)
        grad = grad_normed[...]
        back = norm_back(grad, unit, scale_two[:, 0:1], small[GAIN_TWO : GAIN_TWO + 1, :])
        back += down_low[...].astype(F32)
        grad_res[...] = back
        low = back.astype(BF16)
        grads[here, 3 * D :] = low
        attn_grad[...] = dot_nt(low, proj_weight[...]).astype(BF16)
        sums[0:1, :] += column_sum(grad * unit)
        sums[1:2, :] += column_sum(grad)
        sums[2:3, :] += column_sum(back)
        scaling = jnp.asarray(HEAD_DIM**-0.5, F32)
        for item in range(CHUNK_ITEMS):
            rows = slice(item * ITEM_ROWS, (item + 1) * ITEM_ROWS)
            for pair in range(PAIRS):
                lanes = [
                    slice(kind * D + pair * ITEM_ROWS, kind * D + (pair + 1) * ITEM_ROWS)
                    for kind in range(3)
                ]
                queries = stack_heads(qkv[rows, lanes[0]], first)
                cot = stack_heads(attn_grad[rows, lanes[0]], first)
                spot = (item * PAIRS + pair) * CHUNK
                low = probs[spot : spot + CHUNK, :]
                wide = low.astype(F32)
                grad_probs = dot_nt(cot, qkv[rows, lanes[2]])
                grad_qkv[rows, lanes[2]] = dot_tn(low, cot).astype(BF16)
                centre = jnp.sum(wide * grad_probs, axis=-1, keepdims=True)
                scores_low = (wide * (grad_probs - centre)).astype(BF16)
                made = join_heads(dot(scores_low, qkv[rows, lanes[1]]), first)
                grad_qkv[rows, lanes[0]] = (made * scaling).astype(BF16)
                made = dot_tn(scores_low, queries) * scaling
                grad_qkv[rows, lanes[1]] = made.astype(BF16)
        grads[here, : 3 * D] = grad_qkv[...]
        sums[3:4, :] += column_sum(grad_qkv[:, :D].astype(F32))
        sums[4:5, :] += column_sum(grad_qkv[:, 2 * D :].astype(F32))

    for tile in range(4):

        @pl.when(step == PARTS + tile)
        def _():
            if tile == 0:
                flipped_one_copy.wait()
            if tile == 3:
                flipped_attended_copy.wait()
            left = flipped_one if tile < 3 else flipped_attended
            made = dot(left[...], grads[:, tile * D : (tile + 1) * D])
            mixed_grad[...] = made.astype(BF16)


def attention_backward(*operands):
    far = pl.BlockSpec(memory_space=pl.ANY)
    return call(
        attention_back_kernel,
        (
            shape(ROWS, 3 * D, dtype=BF16),
            shape(ROWS, D),
            shape(8, D),
            shape(4 * D, D, dtype=BF16),
        ),
        grid=(PARTS + 4,),
        in_specs=[
            rows_at(0, CHUNK, D, PARTS),
            rows_at(0, CHUNK, D, PARTS),
            rows_at(0, CHUNK, D, PARTS),
            rows_at(0, CHUNK, ITEM_ROWS, PARTS),
            whole(8, D),
            whole(D, D),
            rows_at(0, CHUNK, 3 * D, PARTS),
            rows_at(0, CHUNK_ITEMS * PAIRS * CHUNK, ITEM_ROWS, PARTS),
            far,
            far,
        ],
        out_specs=[
            rows_at(0, CHUNK, 3 * D, PARTS),
            rows_at(0, CHUNK, D, PARTS),
            held(8, D),
            rows_at(PARTS, D, D, 4),
        ],
        scratch_shapes=[
            pltpu.VMEM((ROWS, 4 * D), BF16),
            pltpu.VMEM((CHUNK, D), BF16),
            pltpu.VMEM((D, ROWS), BF16),
            pltpu.VMEM((D, ROWS), BF16),
            pltpu.SemaphoreType.DMA((2,)),
        ],
    )(*operands)


EMBED_AT = SLOTS
HEAD_AT = EMBED_AT + GROUPS * WIDTH
SUMS_AT = HEAD_AT + GROUPS * WIDTH + 16


def embed_back_kernel(
    place, grads, qkv_weight, unit_one, scale_one, grad_res, small, first_in, second_in, third_in, fourth_in,
    first_weight, second_weight, third_weight, fourth_weight, position, up_sum, sums, head_grad,
    out, grad_inputs, embedded_low, rest,
):
    gain_one = small[GAIN_ONE : GAIN_ONE + 1, :]
    me = place[0]
    sources = (first_in, second_in, third_in, fourth_in)

    def first_norm(step, carry):
        rows = pl.ds(pl.multiple_of(step * CHUNK, CHUNK), CHUNK)
        grad = dot_nt(grads[rows, :], qkv_weight[...])
        unit = unit_one[rows, :].astype(F32)
        total = grad_res[rows, :] + norm_back(grad, unit, scale_one[rows, 0:1], gain_one)
        low = total.astype(BF16)
        embedded_low[rows, :] = low
        for index, weight in enumerate((first_weight, second_weight, third_weight, fourth_weight)):
            made = dot_nt(weight[...], low).astype(BF16)
            for part in range(CHUNK // ITEM_ROWS):
                block = made[:, part * ITEM_ROWS : (part + 1) * ITEM_ROWS]
                item = step * (CHUNK // ITEM_ROWS) + part
                grad_inputs[pl.ds(me ^ index, 1), pl.ds(item, 1)] = block[None, None]
        gain, shift, bias = carry
        return gain + column_sum(grad * unit), shift + column_sum(grad), bias + column_sum(total)

    none = jnp.zeros((1, D), F32)
    gain, shift, bias = lax.fori_loop(0, ROWS // CHUNK, first_norm, (none, none, none))
    slots = lax.broadcasted_iota(jnp.int32, (SLOTS, ROWS), 0)
    hot = (position[...] == slots).astype(BF16)
    rest[0:SLOTS, :] = dot(hot, embedded_low[...])
    for index, source in enumerate(sources):
        rows = pl.ds(pl.multiple_of(EMBED_AT + (me ^ index) * WIDTH, 16), WIDTH)
        rest[rows, :] = dot(source[...], embedded_low[...])
    rest[HEAD_AT:SUMS_AT, :] = head_grad[...]
    rest[SUMS_AT:, :] = jnp.zeros((REST - SUMS_AT, D), F32)
    for row, value in enumerate((gain, shift, bias)):
        rest[SUMS_AT + row : SUMS_AT + row + 1, :] = value
    rest[SUMS_AT + 3 : SUMS_AT + 8, :] = sums[0:5, :]
    for row in range(FF // D):
        at = SUMS_AT + 8 + row
        rest[at : at + 1, :] = up_sum[:, row * D : (row + 1) * D]
    out[...] = rest[...].astype(BF16)


def embed_backward(place, *operands):
    vmem = pl.BlockSpec(memory_space=pltpu.VMEM)
    return call(
        embed_back_kernel,
        (
            shape(REST, D, dtype=BF16),
            shape(GROUPS, OWN_ITEMS, WIDTH, ITEM_ROWS, dtype=BF16),
        ),
        in_specs=[pl.BlockSpec(memory_space=pltpu.SMEM)] + [vmem] * len(operands),
        out_specs=[vmem] * 2,
        scratch_shapes=[pltpu.VMEM((ROWS, D), BF16), pltpu.VMEM((REST, D), F32)],
    )(place, *operands)


WIDEN_STEPS = 6


def widen_kernel(down, up, down_out, up_out):
    down_out[...] = down[...].astype(F32)
    for tile in range(4):
        up_out[:, tile * D : (tile + 1) * D] = up[tile].astype(F32)


def widen_mixed_kernel(mixed, qkv_out, proj_out):
    for tile in range(3):
        qkv_out[:, tile * D : (tile + 1) * D] = mixed[tile].astype(F32)
    proj_out[...] = mixed[3].astype(F32)


def row_blocks(count, width):
    return pl.BlockSpec((count * D // WIDEN_STEPS, width), lambda step: (step, 0))


def tile_rows():
    return pl.BlockSpec((4, D // WIDEN_STEPS, D), lambda step: (0, step, 0))


def widen(down, up):
    return call(
        widen_kernel,
        (shape(FF, D), shape(D, FF)),
        grid=(WIDEN_STEPS,),
        in_specs=[row_blocks(4, D), tile_rows()],
        out_specs=[row_blocks(4, D), row_blocks(1, FF)],
    )(down, up.reshape(4, D, D))


def widen_mixed(mixed):
    return call(
        widen_mixed_kernel,
        (shape(D, 3 * D), shape(D, D)),
        grid=(WIDEN_STEPS,),
        in_specs=[tile_rows()],
        out_specs=[row_blocks(1, 3 * D), row_blocks(1, D)],
    )(mixed.reshape(4, D, D))


def tie(value, *tokens):
    return lax.optimization_barrier((value, tokens))[0]


def sum_over_devices(values, axis, plane):
    core, place = lax.axis_index("core"), lax.axis_index(axis)
    swap = [(0, 1), (1, 0)]
    rows, width = values.shape
    cut, quarter = width // 2, rows // 4

    def shift(value, distance):
        return lax.ppermute(value, axis, [(i, (i + distance) % 4) for i in range(4)])

    send = lax.dynamic_slice_in_dim(values, (1 - core) * cut, cut, 1)
    own = lax.dynamic_slice_in_dim(values, core * cut, cut, 1).astype(F32)
    own = (own + lax.ppermute(send, "core", swap).astype(F32)).astype(BF16)
    part = lambda step: lax.dynamic_slice_in_dim(own, ((place + step) % 4) * quarter, quarter, 0)
    total = part(0).astype(F32)
    for distance in (1, 3, 2):
        total += shift(part(distance), distance).astype(F32)
    lanes = cut if quarter % 128 == 0 else ITEM_ROWS
    parts = total.astype(BF16).reshape(16, -1, lanes)
    parts = lax.all_to_all(parts, plane, 0, 0)
    share = jnp.sum(parts.astype(F32), axis=0).astype(BF16)
    parts = lax.all_to_all(jnp.broadcast_to(share[None], parts.shape), plane, 0, 0)
    own = parts.reshape(quarter, cut)
    turned = [own, shift(own, 3), shift(own, 2), shift(own, 1)]
    turned = jnp.concatenate(turned + turned[:3], axis=0)
    own = lax.dynamic_slice_in_dim(turned, ((4 - place) % 4) * quarter, rows, 0)
    other = lax.ppermute(own, "core", swap)
    first = core == 0
    return jnp.concatenate([jnp.where(first, own, other), jnp.where(first, other, own)], axis=1)


def body(
    patches,
    visible,
    recon_cotangent,
    embed_weight,
    embed_bias,
    position_table,
    attn_norm_gain,
    attn_norm_bias,
    qkv_weight,
    qkv_bias,
    proj_weight,
    proj_bias,
    mlp_norm_gain,
    mlp_norm_bias,
    up_weight,
    up_bias,
    down_weight,
    down_bias,
    head_weight,
    head_bias,
):
    my_group = lax.axis_index(VARS_AXES)
    me = my_group.astype(jnp.int32).reshape(1)
    batch_items = patches.shape[0]
    patch_count = patches.shape[2]

    def exchange(rows):
        return lax.all_to_all(rows, VARS_AXES, 0, 0)

    def partners(blocks):
        swap = [(0, 1), (1, 0)]
        return [
            blocks[0],
            lax.ppermute(blocks[1], "core", swap),
            lax.ppermute(blocks[2], "yhi", swap),
            lax.ppermute(blocks[3], ("yhi", "core"), [(i, 3 - i) for i in range(4)]),
        ]

    items_visible = visible.reshape(GROUPS, OWN_ITEMS, ITEM_ROWS // 2)
    swap = [(0, 1), (1, 0)]
    far_embed = lax.ppermute(embed_weight, "yhi", swap)
    near_embed = lax.ppermute(embed_weight, "core", swap)
    to_embed, to_head, head_sum = pick(
        me,
        jnp.swapaxes(patches, 2, 3).reshape(GROUPS, OWN_ITEMS, 2, WIDTH, patch_count),
        visible,
        jnp.swapaxes(recon_cotangent, 1, 2).reshape(GROUPS, OWN_ITEMS, WIDTH, ITEM_ROWS),
        head_weight.T,
        head_bias[None],
    )
    picked = partners(to_embed)
    embeds = [embed_weight, near_embed, far_embed, lax.ppermute(far_embed, "core", swap)]
    for_embed = [*picked, *embeds]
    for_head = partners(to_head)
    own_visible = lax.dynamic_slice_in_dim(visible, my_group * OWN_ITEMS, OWN_ITEMS, 0)
    position = jnp.concatenate([own_visible, own_visible + patch_count], axis=1)
    zero = jnp.zeros((D,), BF16)
    small = jnp.stack(
        [
            embed_bias,
            attn_norm_gain,
            attn_norm_bias,
            proj_bias,
            mlp_norm_gain,
            mlp_norm_bias,
            down_bias,
            zero,
        ]
    ).astype(F32)
    joined_bias = jnp.concatenate([qkv_bias[0], zero, qkv_bias[1]]).astype(F32)[None]

    (
        unit_one,
        scale_one,
        flipped_one,
        qkv,
        probs,
        flipped_attended,
        residual,
        unit_two,
        scale_two,
        normed_two,
        flipped_two,
    ) = attention(
        *for_embed,
        position.reshape(ROWS, 1),
        position_table,
        small,
        qkv_weight,
        joined_bias,
        proj_weight,
    )
    down_grad, recon, head_grad, up_grad, up_sum, down_low, grad_normed = feed_forward(
        me,
        normed_two,
        residual,
        up_weight,
        up_bias.astype(F32)[None],
        down_weight,
        head_sum,
        *for_head,
        flipped_two,
    )
    down_grad, up_grad = lax.psum((down_grad, up_grad), ALL_AXES)
    grad_qkv, grad_res, sums, mixed_grad = attention_backward(
        grad_normed,
        down_low,
        unit_two,
        scale_two,
        small,
        proj_weight,
        qkv,
        probs,
        flipped_one,
        flipped_attended,
    )
    rest, grad_inputs = embed_backward(
        me,
        grad_qkv,
        qkv_weight,
        unit_one,
        scale_one,
        grad_res,
        small,
        *for_embed,
        position.reshape(1, ROWS),
        up_sum,
        sums,
        head_grad,
    )
    mixed_grad = sum_over_devices(mixed_grad, "z", ("ylo", "x", "yhi"))
    rest = sum_over_devices(rest, "x", ("z", "ylo", "yhi"))
    recon = exchange(tie(recon, rest))
    placed = exchange(tie(grad_inputs, recon))
    patch_grad = put(items_visible, placed).reshape(batch_items, 2, WIDTH, patch_count)
    patch_grad = jnp.swapaxes(patch_grad, 2, 3)
    qkv_grad, proj_grad = widen_mixed(mixed_grad)
    down_grad, up_grad = widen(down_grad, up_grad)
    rest = rest[: SUMS_AT + 16].astype(F32)
    embed_grad = lax.dynamic_slice_in_dim(rest, EMBED_AT + my_group * WIDTH, WIDTH, 0)
    total = rest[SUMS_AT : SUMS_AT + 16]
    early = rest[SUMS_AT - 16 : SUMS_AT]
    head_shift = lax.dynamic_index_in_dim(early, 1 + my_group, 0, False)[:WIDTH]
    head_grad = lax.dynamic_slice_in_dim(rest, HEAD_AT + my_group * WIDTH, WIDTH, 0).T
    return (
        jnp.swapaxes(recon.reshape(batch_items, WIDTH, ITEM_ROWS), 1, 2),
        patch_grad,
        embed_grad,
        total[2],
        rest[:SLOTS],
        total[0],
        total[1],
        qkv_grad,
        total[6:8],
        proj_grad,
        total[5],
        total[3],
        total[4],
        up_grad,
        total[8:12].reshape(FF),
        down_grad,
        early[0],
        head_grad,
        head_shift,
    )


def solution(mesh):
    items, groups = ITEMS_AXES, VARS_AXES
    fine = Mesh(mesh.devices.reshape(4, 2, 4, 2, 2), ALL_AXES)
    in_specs = (
        P(items, None, None, groups),
        P(items, None),
        P(items, None, groups),
        P(groups, None),
        *[P()] * 14,
        P(None, groups),
        P(groups),
    )
    out_specs = (
        P(items, None, groups),
        P(items, None, None, groups),
        P(groups, None),
        *[P()] * 14,
        P(None, groups),
        P(groups),
    )
    return jax.shard_map(body, mesh=fine, in_specs=in_specs, out_specs=out_specs, check_vma=False)
```

```python
import functools

import jax
import jax.numpy as jnp
from jax import lax
from jax.experimental import pallas as pl
from jax.experimental.pallas import tpu as pltpu
from jax.sharding import Mesh
from jax.sharding import PartitionSpec as P

HEADS = 12
HEAD_DIM = 64
D = 768
FF = 3072
ITEM_ROWS = 128
OWN_ITEMS = 6
ROWS = OWN_ITEMS * ITEM_ROWS
GROUPS = 4
WIDTH = 80
PAIRS = HEADS // 2
SLOTS = 512
FF_TILE = 768
CUT = 384
REST = 1280
CHUNK = 256
F32 = jnp.float32
BF16 = jnp.bfloat16
VMEM_LIMIT = 58 * 1024 * 1024

ITEMS_AXES = ("z", "ylo", "x")
VARS_AXES = ("yhi", "core")
ALL_AXES = ITEMS_AXES + VARS_AXES


def dot(left, right):
    return jnp.dot(left, right, preferred_element_type=F32)


def dot_nt(left, right):
    return lax.dot_general(left, right, (((1,), (1,)), ((), ())), preferred_element_type=F32)


def dot_tn(left, right):
    return lax.dot_general(left, right, (((0,), (0,)), ((), ())), preferred_element_type=F32)


def normalise(values):
    centre = values - jnp.mean(values, axis=-1, keepdims=True)
    scale = lax.rsqrt(jnp.mean(centre * centre, axis=-1, keepdims=True) + 1e-06)
    return centre * scale, scale


def norm_back(grad, unit, scale, gain):
    wide = grad * gain
    first = jnp.mean(wide, axis=-1, keepdims=True)
    second = jnp.mean(wide * unit, axis=-1, keepdims=True)
    return scale * (wide - first - unit * second)


def column_sum(values):
    return jnp.sum(values, axis=0, keepdims=True)


def low_half():
    return lax.broadcasted_iota(jnp.int32, (ITEM_ROWS, ITEM_ROWS), 1) < HEAD_DIM


def stack_heads(block, first):
    zero = jnp.zeros_like(block)
    return jnp.concatenate([jnp.where(first, block, zero), jnp.where(first, zero, block)], axis=0)


def join_heads(both, first):
    return jnp.where(first, both[:ITEM_ROWS], both[ITEM_ROWS:])


def call(kernel, out_shape, **kwargs):
    return pl.pallas_call(
        kernel,
        out_shape=out_shape,
        compiler_params=pltpu.CompilerParams(vmem_limit_bytes=VMEM_LIMIT),
        cost_estimate=pl.CostEstimate(flops=1_000_000, bytes_accessed=10_000, transcendentals=0),
        **kwargs,
    )


def shape(*dims, dtype=F32):
    return jax.ShapeDtypeStruct(dims, dtype)


def by_partner(*dims):
    return pl.BlockSpec((1,) + dims, lambda step, me: (me[0] ^ step,) + (0,) * len(dims))


def throughout(*dims):
    return pl.BlockSpec(dims, lambda step, me: (0,) * len(dims))


def pick_kernel(me, patches, visible, cotangent, head_rows, head_bias, *outs):
    step = pl.program_id(0)
    head_sum = outs[8]
    numbers = lax.broadcasted_iota(jnp.int32, (SLOTS // 2, ITEM_ROWS // 2), 0)
    first = (me[0] ^ step) * OWN_ITEMS
    picked = []
    total = jnp.zeros((WIDTH, ITEM_ROWS), F32)
    for item in range(OWN_ITEMS):
        hot = (visible[pl.ds(first + item, 1), :] == numbers).astype(BF16)
        rows = [dot(patches[0, item, time], hot) for time in range(2)]
        picked.append(jnp.concatenate(rows, axis=1).astype(BF16))
        total += cotangent[0, item].astype(F32)
    head_sum[...] = jnp.where(step == 0, total, head_sum[...] + total)
    for index in range(GROUPS):

        @pl.when(step == index)
        def _():
            out, cot_out = outs[index], outs[GROUPS + index]
            for item in range(OWN_ITEMS):
                lanes = slice(item * ITEM_ROWS, (item + 1) * ITEM_ROWS)
                out[:, lanes] = picked[item]
                cot_out[0:WIDTH, lanes] = cotangent[0, item]
            cot_out[WIDTH : 2 * WIDTH, :] = head_rows[...]
            cot_out[2 * WIDTH :, :] = jnp.zeros((16, D), BF16)
            rows = lax.broadcasted_iota(jnp.int32, (16, WIDTH), 0)
            bias = jnp.where(rows == 0, head_bias[...].astype(F32), 0.0)
            cot_out[2 * WIDTH :, 0:WIDTH] = bias.astype(BF16)


def pick(me, patches, visible, cotangent, head_rows, head_bias):
    outs = call(
        pick_kernel,
        [shape(WIDTH, D, dtype=BF16)] * 4
        + [shape(2 * WIDTH + 16, D, dtype=BF16)] * 4
        + [shape(WIDTH, ITEM_ROWS)],
        grid_spec=pltpu.PrefetchScalarGridSpec(
            num_scalar_prefetch=1,
            grid=(GROUPS,),
            in_specs=[
                by_partner(OWN_ITEMS, 2, WIDTH, SLOTS // 2),
                throughout(GROUPS * OWN_ITEMS, ITEM_ROWS // 2),
                by_partner(OWN_ITEMS, WIDTH, ITEM_ROWS),
                throughout(WIDTH, D),
                throughout(1, WIDTH),
            ],
            out_specs=[throughout(WIDTH, D)] * 4
            + [throughout(2 * WIDTH + 16, D)] * 4
            + [throughout(WIDTH, ITEM_ROWS)],
        ),
    )(me, patches, visible, cotangent, head_rows, head_bias)
    return outs[:4], outs[4:8], outs[8]


def put_kernel(me, visible, first_rows, second_rows, third_rows, fourth_rows, out):
    step = pl.program_id(0)
    numbers = lax.broadcasted_iota(jnp.int32, (SLOTS // 2, ITEM_ROWS // 2), 0)
    cut = ITEM_ROWS // 2
    for index, rows in enumerate((first_rows, second_rows, third_rows, fourth_rows)):

        @pl.when(step == index)
        def _():
            for item in range(OWN_ITEMS):
                hot = (visible[0, item : item + 1, :] == numbers).astype(BF16)
                for time in range(2):
                    block = rows[item, :, time * cut : (time + 1) * cut]
                    out[0, item, time] = dot_nt(block, hot).astype(BF16)


def put(me, visible, blocks):
    return call(
        put_kernel,
        shape(GROUPS, OWN_ITEMS, 2, WIDTH, SLOTS // 2, dtype=BF16),
        grid_spec=pltpu.PrefetchScalarGridSpec(
            num_scalar_prefetch=1,
            grid=(GROUPS,),
            in_specs=[by_partner(OWN_ITEMS, ITEM_ROWS // 2)]
            + [throughout(OWN_ITEMS, WIDTH, ITEM_ROWS)] * 4,
            out_specs=by_partner(OWN_ITEMS, 2, WIDTH, SLOTS // 2),
        ),
    )(me, visible, *blocks)


EMBED_BIAS, GAIN_ONE, SHIFT_ONE, PROJ_BIAS, GAIN_TWO, SHIFT_TWO, DOWN_BIAS, HEAD_BIAS = range(8)


PARTS = ROWS // CHUNK
CHUNK_ITEMS = CHUNK // ITEM_ROWS
TILES = FF // FF_TILE


def whole(*dims):
    return pl.BlockSpec(dims, lambda *step: (0,) * len(dims), pipeline_mode=pl.Buffered(1))


def held(*dims):
    return pl.BlockSpec(dims, lambda *step: (0,) * len(dims))


def rows_at(first, rows, width, count):
    return pl.BlockSpec((rows, width), lambda step, *_: (jnp.clip(step - first, 0, count - 1), 0))


def columns_at(first, rows, width, count):
    return pl.BlockSpec((rows, width), lambda step, *_: (0, jnp.clip(step - first, 0, count - 1)))


def attention_kernel(
    first_in, second_in, third_in, fourth_in, first_weight, second_weight, third_weight, fourth_weight,
    position, table, small, qkv_far, qkv_bias, proj_far,
    unit_one, scale_one, flipped_one, qkv, probs, flipped_attended, residual, unit_two, scale_two,
    normed_two, flipped_two,
    embedded, attended, qkv_weight, proj_weight, arrivals,
):
    step = pl.program_id(0)
    first = low_half()
    picked = (first_in, second_in, third_in, fourth_in)
    embeds = (first_weight, second_weight, third_weight, fourth_weight)
    qkv_copy = pltpu.make_async_copy(qkv_far, qkv_weight, arrivals.at[0])
    proj_copy = pltpu.make_async_copy(proj_far, proj_weight, arrivals.at[1])

    @pl.when(step == 0)
    def _():
        qkv_copy.start()
        proj_copy.start()

    here = pl.ds(pl.multiple_of(step * CHUNK, CHUNK), CHUNK)
    slots = lax.broadcasted_iota(jnp.int32, (CHUNK, SLOTS), 1)
    hot = (position[...] == slots).astype(BF16)
    values = dot(hot, table[...]) + small[EMBED_BIAS : EMBED_BIAS + 1, :]
    for source, weight in zip(picked, embeds):
        values += dot_tn(source[:, here], weight[...])
    embedded[...] = values
    unit, scale = normalise(values)
    unit_one[...] = unit.astype(BF16)
    scale_one[...] = jnp.broadcast_to(scale, (CHUNK, ITEM_ROWS))
    normed = unit * small[GAIN_ONE : GAIN_ONE + 1, :] + small[SHIFT_ONE : SHIFT_ONE + 1, :]
    normed = normed.astype(BF16)
    flipped_one[...] = normed.T
    pl.when(step == 0)(qkv_copy.wait)
    for part in range(3):
        columns = slice(part * D, (part + 1) * D)
        mixed = dot(normed, qkv_weight[:, columns]) + qkv_bias[:, columns]
        qkv[:, columns] = mixed.astype(BF16)
    for item in range(CHUNK_ITEMS):
        rows = slice(item * ITEM_ROWS, (item + 1) * ITEM_ROWS)
        for pair in range(PAIRS):
            lanes = [
                slice(part * D + pair * ITEM_ROWS, part * D + (pair + 1) * ITEM_ROWS)
                for part in range(3)
            ]
            queries = qkv[rows, lanes[0]] * jnp.asarray(HEAD_DIM**-0.5, BF16)
            scores = dot_nt(stack_heads(queries, first), qkv[rows, lanes[1]])
            weights = jnp.exp(scores - jnp.max(scores, axis=-1, keepdims=True))
            weights = weights * (1.0 / jnp.sum(weights, axis=-1, keepdims=True))
            weights = weights.astype(BF16)
            spot = (item * PAIRS + pair) * CHUNK
            probs[spot : spot + CHUNK, :] = weights
            made = join_heads(dot(weights, qkv[rows, lanes[2]]), first)
            attended[rows, lanes[0]] = made.astype(BF16)
    mixed = attended[...]
    flipped_attended[...] = mixed.T
    pl.when(step == 0)(proj_copy.wait)
    values = embedded[...] + dot(mixed, proj_weight[...]) + small[PROJ_BIAS : PROJ_BIAS + 1, :]
    residual[...] = values + small[DOWN_BIAS : DOWN_BIAS + 1, :]
    unit, scale = normalise(values)
    unit_two[...] = unit.astype(BF16)
    scale_two[...] = jnp.broadcast_to(scale, (CHUNK, ITEM_ROWS))
    normed = unit * small[GAIN_TWO : GAIN_TWO + 1, :] + small[SHIFT_TWO : SHIFT_TWO + 1, :]
    normed = normed.astype(BF16)
    normed_two[...] = normed
    flipped_two[...] = normed.T


def attention(*operands):
    far = pl.BlockSpec(memory_space=pl.ANY)
    return call(
        attention_kernel,
        (
            shape(ROWS, D, dtype=BF16),
            shape(ROWS, ITEM_ROWS),
            shape(D, ROWS, dtype=BF16),
            shape(ROWS, 3 * D, dtype=BF16),
            shape(OWN_ITEMS * PAIRS * CHUNK, ITEM_ROWS, dtype=BF16),
            shape(D, ROWS, dtype=BF16),
            shape(ROWS, D),
            shape(ROWS, D, dtype=BF16),
            shape(ROWS, ITEM_ROWS),
            shape(ROWS, D, dtype=BF16),
            shape(D, ROWS, dtype=BF16),
        ),
        grid=(PARTS,),
        in_specs=[whole(WIDTH, D)] * 8
        + [
            rows_at(0, CHUNK, 1, PARTS),
            whole(SLOTS, D),
            whole(8, D),
            far,
            whole(1, 3 * D),
            far,
        ],
        out_specs=[
            rows_at(0, CHUNK, D, PARTS),
            rows_at(0, CHUNK, ITEM_ROWS, PARTS),
            columns_at(0, D, CHUNK, PARTS),
            rows_at(0, CHUNK, 3 * D, PARTS),
            rows_at(0, CHUNK_ITEMS * PAIRS * CHUNK, ITEM_ROWS, PARTS),
            columns_at(0, D, CHUNK, PARTS),
            rows_at(0, CHUNK, D, PARTS),
            rows_at(0, CHUNK, D, PARTS),
            rows_at(0, CHUNK, ITEM_ROWS, PARTS),
            rows_at(0, CHUNK, D, PARTS),
            columns_at(0, D, CHUNK, PARTS),
        ],
        scratch_shapes=[
            pltpu.VMEM((CHUNK, D), F32),
            pltpu.VMEM((CHUNK, D), BF16),
            pltpu.VMEM((D, 3 * D), BF16),
            pltpu.VMEM((D, D), BF16),
            pltpu.SemaphoreType.DMA((2,)),
        ],
    )(*operands)


def feed_forward_kernel(
    me, normed_two, residual_far, up_weight, up_bias, down_weight, head_sum, first_cot, second_cot, third_cot,
    fourth_cot, flipped_far,
    down_grad, recon, head_grad, up_grad, up_sum, down_low, total,
    activated, slope, residual, flipped, arrivals,
):
    step = pl.program_id(0)
    residual_copy = pltpu.make_async_copy(residual_far, residual, arrivals.at[0])
    flipped_copy = pltpu.make_async_copy(flipped_far, flipped, arrivals.at[1])

    @pl.when(step == 0)
    def _():
        residual_copy.start()
        flipped_copy.start()
        for start in range(0, ROWS, CHUNK):
            rows = slice(start, start + CHUNK)
            grad = jnp.zeros((CHUNK, D), F32)
            for source in (first_cot, second_cot, third_cot, fourth_cot):
                grad += dot_tn(source[0:WIDTH, rows], source[WIDTH : 2 * WIDTH, :])
            down_low[rows, :] = grad.astype(BF16)
            line = column_sum(grad)
            if start:
                line += head_grad[GROUPS * WIDTH : GROUPS * WIDTH + 1, :]
            head_grad[GROUPS * WIDTH : GROUPS * WIDTH + 1, :] = line
        head_grad[GROUPS * WIDTH + 1 :, :] = jnp.zeros((15, D), F32)

    @pl.when(step < TILES)
    def _():
        bias = up_bias[...]
        tile = pl.ds(pl.multiple_of(step * FF_TILE, FF_TILE), FF_TILE)
        for start in range(0, ROWS, CHUNK):
            rows = slice(start, start + CHUNK)
            hidden = dot(normed_two[rows, :], up_weight[...]) + bias
            square = hidden * hidden
            inner = 0.7978845608028654 + (0.7978845608028654 * 0.044715) * square
            curve = jnp.tanh(hidden * inner)
            half = 0.5 + 0.5 * curve
            made = hidden * half
            low = made.astype(BF16)
            activated[rows, :] = low
            rise = 0.7978845608028654 + (0.7978845608028654 * 3 * 0.044715) * square
            slope[rows, tile] = (half + made * (rise - rise * curve)).astype(BF16)
            made = dot(low, down_weight[...])
            total[rows, :] = jnp.where(step == 0, made, total[rows, :] + made)
        down_grad[...] = dot_tn(activated[...], down_low[...]).astype(BF16)

    @pl.when(step == TILES - 1)
    def _():
        residual_copy.wait()
        low = (total[...] + residual[...]).astype(BF16)
        for index, source in enumerate((first_cot, second_cot, third_cot, fourth_cot)):
            group = me[0] ^ index
            column = source[2 * WIDTH :, 0:ITEM_ROWS].astype(F32).T[0:WIDTH, 0:1]
            made = (dot_nt(source[WIDTH : 2 * WIDTH, :], low) + column).astype(BF16)
            for item in range(OWN_ITEMS):
                block = made[:, item * ITEM_ROWS : (item + 1) * ITEM_ROWS]
                recon[index, item] = block
            rows = pl.ds(pl.multiple_of(group * WIDTH, 16), WIDTH)
            head_grad[rows, :] = dot(source[0:WIDTH, :], low)
        rows = lax.broadcasted_iota(jnp.int32, (16, D), 0)
        padded = jnp.concatenate([head_sum[...], jnp.zeros((ITEM_ROWS - WIDTH, ITEM_ROWS), F32)], axis=0)
        line = column_sum(padded.T)
        line = jnp.concatenate([line, jnp.zeros((1, D - ITEM_ROWS), F32)], axis=1)
        head_grad[GROUPS * WIDTH :, :] += jnp.where(rows == 1 + me[0], line, 0.0)

    @pl.when(step >= TILES)
    def _():
        tile = pl.ds(pl.multiple_of((step - TILES) * FF_TILE, FF_TILE), FF_TILE)
        grad = dot_nt(down_low[...], down_weight[...]) * slope[:, tile].astype(F32)
        hidden_low = grad.astype(BF16)
        pl.when(step == TILES)(flipped_copy.wait)
        up_sum[...] = column_sum(hidden_low.astype(F32))
        up_grad[...] = dot(flipped[...], hidden_low).astype(BF16)
        made = dot_nt(hidden_low, up_weight[...])
        total[...] = jnp.where(step == TILES, made, total[...] + made)


def feed_forward(me, *operands):
    again = lambda step: step % TILES
    far = pl.BlockSpec(memory_space=pl.ANY)
    return call(
        feed_forward_kernel,
        (
            shape(FF, D, dtype=BF16),
            shape(GROUPS, OWN_ITEMS, WIDTH, ITEM_ROWS, dtype=BF16),
            shape(GROUPS * WIDTH + 16, D),
            shape(FF, D, dtype=BF16),
            shape(1, FF),
            shape(ROWS, D, dtype=BF16),
            shape(ROWS, D),
        ),
        grid_spec=pltpu.PrefetchScalarGridSpec(
            num_scalar_prefetch=1,
            grid=(2 * TILES,),
            in_specs=[
                whole(ROWS, D),
                far,
                pl.BlockSpec((D, FF_TILE), lambda step, me: (0, again(step))),
                columns_at(0, 1, FF_TILE, TILES),
                pl.BlockSpec((FF_TILE, D), lambda step, me: (again(step), 0)),
                whole(WIDTH, ITEM_ROWS),
            ]
            + [whole(2 * WIDTH + 16, D)] * 4
            + [far],
            out_specs=[
                rows_at(0, FF_TILE, D, TILES),
                held(GROUPS, OWN_ITEMS, WIDTH, ITEM_ROWS),
                held(GROUPS * WIDTH + 16, D),
                rows_at(TILES, FF_TILE, D, TILES),
                columns_at(TILES, 1, FF_TILE, TILES),
                held(ROWS, D),
                held(ROWS, D),
            ],
            scratch_shapes=[
                pltpu.VMEM((ROWS, FF_TILE), BF16),
                pltpu.VMEM((ROWS, FF), BF16),
                pltpu.VMEM((ROWS, D), F32),
                pltpu.VMEM((D, ROWS), BF16),
                pltpu.SemaphoreType.DMA((2,)),
            ],
        ),
    )(me, *operands)


def write_halves(core, values, send, keep):
    left, right = values[:, :CUT], values[:, CUT:]

    @pl.when(core == 0)
    def _():
        keep[...] = left
        send[...] = right

    @pl.when(core != 0)
    def _():
        keep[...] = right
        send[...] = left


def attention_back_kernel(
    core, grad_normed, down_low, unit_two, scale_two, small, proj_weight, qkv, probs, flipped_one_far,
    flipped_attended_far,
    grad_qkv, grad_res, sums, send, keep,
    grads, attn_grad, flipped_one, flipped_attended, arrivals,
):
    step = pl.program_id(0)
    first = low_half()
    flipped_one_copy = pltpu.make_async_copy(flipped_one_far, flipped_one, arrivals.at[0])
    flipped_attended_copy = pltpu.make_async_copy(
        flipped_attended_far, flipped_attended, arrivals.at[1]
    )

    @pl.when(step == 0)
    def _():
        flipped_one_copy.start()
        flipped_attended_copy.start()
        sums[...] = jnp.zeros_like(sums)

    @pl.when(step < PARTS)
    def _():
        here = pl.ds(pl.multiple_of(step * CHUNK, CHUNK), CHUNK)
        unit = unit_two[...].astype(F32)
        grad = grad_normed[...]
        back = norm_back(grad, unit, scale_two[:, 0:1], small[GAIN_TWO : GAIN_TWO + 1, :])
        back += down_low[...].astype(F32)
        grad_res[...] = back
        low = back.astype(BF16)
        grads[here, 3 * D :] = low
        attn_grad[...] = dot_nt(low, proj_weight[...]).astype(BF16)
        sums[0:1, :] += column_sum(grad * unit)
        sums[1:2, :] += column_sum(grad)
        sums[2:3, :] += column_sum(back)
        scaling = jnp.asarray(HEAD_DIM**-0.5, F32)
        for item in range(CHUNK_ITEMS):
            rows = slice(item * ITEM_ROWS, (item + 1) * ITEM_ROWS)
            for pair in range(PAIRS):
                lanes = [
                    slice(kind * D + pair * ITEM_ROWS, kind * D + (pair + 1) * ITEM_ROWS)
                    for kind in range(3)
                ]
                queries = stack_heads(qkv[rows, lanes[0]], first)
                cot = stack_heads(attn_grad[rows, lanes[0]], first)
                spot = (item * PAIRS + pair) * CHUNK
                low = probs[spot : spot + CHUNK, :]
                wide = low.astype(F32)
                grad_probs = dot_nt(cot, qkv[rows, lanes[2]])
                grad_qkv[rows, lanes[2]] = dot_tn(low, cot).astype(BF16)
                centre = jnp.sum(wide * grad_probs, axis=-1, keepdims=True)
                scores_low = (wide * (grad_probs - centre)).astype(BF16)
                made = join_heads(dot(scores_low, qkv[rows, lanes[1]]), first)
                grad_qkv[rows, lanes[0]] = (made * scaling).astype(BF16)
                made = dot_tn(scores_low, queries) * scaling
                grad_qkv[rows, lanes[1]] = made.astype(BF16)
        grads[here, : 3 * D] = grad_qkv[...]
        sums[3:4, :] += column_sum(grad_qkv[:, :D].astype(F32))
        sums[4:5, :] += column_sum(grad_qkv[:, 2 * D :].astype(F32))

    for tile in range(4):

        @pl.when(step == PARTS + tile)
        def _():
            if tile == 0:
                flipped_one_copy.wait()
            if tile == 3:
                flipped_attended_copy.wait()
            left = flipped_one if tile < 3 else flipped_attended
            made = dot(left[...], grads[:, tile * D : (tile + 1) * D])
            write_halves(core[0], made.astype(BF16), send, keep)


def attention_backward(*operands):
    far = pl.BlockSpec(memory_space=pl.ANY)
    return call(
        attention_back_kernel,
        (
            shape(ROWS, 3 * D, dtype=BF16),
            shape(ROWS, D),
            shape(8, D),
            shape(4 * D, CUT, dtype=BF16),
            shape(4 * D, CUT, dtype=BF16),
        ),
        grid=(PARTS + 4,),
        in_specs=[
            pl.BlockSpec(memory_space=pltpu.SMEM),
            rows_at(0, CHUNK, D, PARTS),
            rows_at(0, CHUNK, D, PARTS),
            rows_at(0, CHUNK, D, PARTS),
            rows_at(0, CHUNK, ITEM_ROWS, PARTS),
            whole(8, D),
            whole(D, D),
            rows_at(0, CHUNK, 3 * D, PARTS),
            rows_at(0, CHUNK_ITEMS * PAIRS * CHUNK, ITEM_ROWS, PARTS),
            far,
            far,
        ],
        out_specs=[
            rows_at(0, CHUNK, 3 * D, PARTS),
            rows_at(0, CHUNK, D, PARTS),
            held(8, D),
            rows_at(PARTS, D, CUT, 4),
            rows_at(PARTS, D, CUT, 4),
        ],
        scratch_shapes=[
            pltpu.VMEM((ROWS, 4 * D), BF16),
            pltpu.VMEM((CHUNK, D), BF16),
            pltpu.VMEM((D, ROWS), BF16),
            pltpu.VMEM((D, ROWS), BF16),
            pltpu.SemaphoreType.DMA((2,)),
        ],
    )(*operands)


EMBED_AT = SLOTS
HEAD_AT = EMBED_AT + GROUPS * WIDTH
SUMS_AT = HEAD_AT + GROUPS * WIDTH + 16


def embed_back_kernel(
    place, grads, qkv_weight, unit_one, scale_one, grad_res, small, first_in, second_in, third_in, fourth_in,
    first_weight, second_weight, third_weight, fourth_weight, position, up_sum, sums, head_grad,
    send, keep, grad_inputs, embedded_low, rest,
):
    gain_one = small[GAIN_ONE : GAIN_ONE + 1, :]
    me = place[0]
    sources = (first_in, second_in, third_in, fourth_in)

    def first_norm(step, carry):
        rows = pl.ds(pl.multiple_of(step * CHUNK, CHUNK), CHUNK)
        grad = dot_nt(grads[rows, :], qkv_weight[...])
        unit = unit_one[rows, :].astype(F32)
        total = grad_res[rows, :] + norm_back(grad, unit, scale_one[rows, 0:1], gain_one)
        low = total.astype(BF16)
        embedded_low[rows, :] = low
        for index, weight in enumerate((first_weight, second_weight, third_weight, fourth_weight)):
            made = dot_nt(weight[...], low).astype(BF16)
            for part in range(CHUNK // ITEM_ROWS):
                block = made[:, part * ITEM_ROWS : (part + 1) * ITEM_ROWS]
                item = step * (CHUNK // ITEM_ROWS) + part
                grad_inputs[index, pl.ds(item, 1)] = block[None]
        gain, shift, bias = carry
        return gain + column_sum(grad * unit), shift + column_sum(grad), bias + column_sum(total)

    none = jnp.zeros((1, D), F32)
    gain, shift, bias = lax.fori_loop(0, ROWS // CHUNK, first_norm, (none, none, none))
    slots = lax.broadcasted_iota(jnp.int32, (SLOTS, ROWS), 0)
    hot = (position[...] == slots).astype(BF16)
    rest[0:SLOTS, :] = dot(hot, embedded_low[...])
    for index, source in enumerate(sources):
        rows = pl.ds(pl.multiple_of(EMBED_AT + (me ^ index) * WIDTH, 16), WIDTH)
        rest[rows, :] = dot(source[...], embedded_low[...])
    rest[HEAD_AT:SUMS_AT, :] = head_grad[...]
    rest[SUMS_AT:, :] = jnp.zeros((REST - SUMS_AT, D), F32)
    for row, value in enumerate((gain, shift, bias)):
        rest[SUMS_AT + row : SUMS_AT + row + 1, :] = value
    rest[SUMS_AT + 3 : SUMS_AT + 8, :] = sums[0:5, :]
    for row in range(FF // D):
        at = SUMS_AT + 8 + row
        rest[at : at + 1, :] = up_sum[:, row * D : (row + 1) * D]
    write_halves(lax.rem(me, 2), rest[...].astype(BF16), send, keep)


def embed_backward(place, *operands):
    vmem = pl.BlockSpec(memory_space=pltpu.VMEM)
    return call(
        embed_back_kernel,
        (
            shape(REST, CUT, dtype=BF16),
            shape(REST, CUT, dtype=BF16),
            shape(GROUPS, OWN_ITEMS, WIDTH, ITEM_ROWS, dtype=BF16),
        ),
        in_specs=[pl.BlockSpec(memory_space=pltpu.SMEM)] + [vmem] * len(operands),
        out_specs=[vmem] * 3,
        scratch_shapes=[pltpu.VMEM((ROWS, D), BF16), pltpu.VMEM((REST, D), F32)],
    )(place, *operands)


WIDEN_STEPS = 6


def widen_kernel(down, up, down_out, up_out):
    down_out[...] = down[...].astype(F32)
    for tile in range(4):
        up_out[:, tile * D : (tile + 1) * D] = up[tile].astype(F32)


def widen_mixed_kernel(core, own, other, qkv_out, proj_out):
    def write(left, right):
        for tile in range(4):
            out, start = (qkv_out, tile * D) if tile < 3 else (proj_out, 0)
            out[:, start : start + CUT] = left[tile].astype(F32)
            out[:, start + CUT : start + D] = right[tile].astype(F32)

    pl.when(core[0] == 0)(lambda: write(own, other))
    pl.when(core[0] != 0)(lambda: write(other, own))


def row_blocks(count, width):
    return pl.BlockSpec((count * D // WIDEN_STEPS, width), lambda step: (step, 0))


def tile_rows():
    return pl.BlockSpec((4, D // WIDEN_STEPS, D), lambda step: (0, step, 0))


def widen(down, up):
    return call(
        widen_kernel,
        (shape(FF, D), shape(D, FF)),
        grid=(WIDEN_STEPS,),
        in_specs=[row_blocks(4, D), tile_rows()],
        out_specs=[row_blocks(4, D), row_blocks(1, FF)],
    )(down, up.reshape(4, D, D))


def widen_mixed(core, own, other):
    halves = pl.BlockSpec((4, D // WIDEN_STEPS, CUT), lambda step: (0, step, 0))
    return call(
        widen_mixed_kernel,
        (shape(D, 3 * D), shape(D, D)),
        grid=(WIDEN_STEPS,),
        in_specs=[pl.BlockSpec(memory_space=pltpu.SMEM), halves, halves],
        out_specs=[row_blocks(1, 3 * D), row_blocks(1, D)],
    )(core, own.reshape(4, D, CUT), other.reshape(4, D, CUT))


def tie(value, *tokens):
    return lax.optimization_barrier((value, tokens))[0]


SWAP = [(0, 1), (1, 0)]
PLANES = {"x": ("z", "ylo", "yhi"), "z": ("ylo", "x", "yhi")}


def other_core(value):
    return lax.ppermute(value, "core", SWAP)


def shift(value, axis, distance):
    return lax.ppermute(value, axis, [(i, (i + distance) % 4) for i in range(4)])


def quarters(keep, arrived, axis):
    own = (keep.astype(F32) + arrived.astype(F32)).astype(BF16)
    rows = own.shape[0] // 4
    place = lax.axis_index(axis)
    return [
        lax.dynamic_slice_in_dim(own, ((place + step) % 4) * rows, rows, 0) for step in range(4)
    ]


def sum_quarter(parts, axis):
    total = parts[0].astype(F32)
    for distance in (1, 3, 2):
        total += shift(parts[distance], axis, distance).astype(F32)
    return total.astype(BF16)


def split_plane(block, axis):
    lanes = block.shape[1] if block.shape[0] % 128 == 0 else ITEM_ROWS
    return lax.all_to_all(block.reshape(16, -1, lanes), PLANES[axis], 0, 0)


def join_plane(parts, axis):
    share = jnp.sum(parts.astype(F32), axis=0).astype(BF16)
    parts = lax.all_to_all(jnp.broadcast_to(share[None], parts.shape), PLANES[axis], 0, 0)
    return parts.reshape(-1, CUT)


def join_quarters(own, axis):
    turned = [own, shift(own, axis, 3), shift(own, axis, 2), shift(own, axis, 1)]
    turned = jnp.concatenate(turned + turned[:3], axis=0)
    start = ((4 - lax.axis_index(axis)) % 4) * own.shape[0]
    return lax.dynamic_slice_in_dim(turned, start, 4 * own.shape[0], 0)


def body(
    patches,
    visible,
    recon_cotangent,
    embed_weight,
    embed_bias,
    position_table,
    attn_norm_gain,
    attn_norm_bias,
    qkv_weight,
    qkv_bias,
    proj_weight,
    proj_bias,
    mlp_norm_gain,
    mlp_norm_bias,
    up_weight,
    up_bias,
    down_weight,
    down_bias,
    head_weight,
    head_bias,
):
    my_group = lax.axis_index(VARS_AXES)
    me = my_group.astype(jnp.int32).reshape(1)
    batch_items = patches.shape[0]
    patch_count = patches.shape[2]

    def partners(blocks):
        return [
            blocks[0],
            other_core(blocks[1]),
            lax.ppermute(blocks[2], "yhi", SWAP),
            lax.ppermute(blocks[3], ("yhi", "core"), [(i, 3 - i) for i in range(4)]),
        ]

    items_visible = visible.reshape(GROUPS, OWN_ITEMS, ITEM_ROWS // 2)
    far_embed = lax.ppermute(embed_weight, "yhi", SWAP)
    near_embed = other_core(embed_weight)
    to_embed, to_head, head_sum = pick(
        me,
        jnp.swapaxes(patches, 2, 3).reshape(GROUPS, OWN_ITEMS, 2, WIDTH, patch_count),
        visible,
        jnp.swapaxes(recon_cotangent, 1, 2).reshape(GROUPS, OWN_ITEMS, WIDTH, ITEM_ROWS),
        head_weight.T,
        head_bias[None],
    )
    picked = partners(to_embed)
    embeds = [embed_weight, near_embed, far_embed, other_core(far_embed)]
    for_embed = [*picked, *embeds]
    for_head = partners(to_head)
    own_visible = lax.dynamic_slice_in_dim(visible, my_group * OWN_ITEMS, OWN_ITEMS, 0)
    position = jnp.concatenate([own_visible, own_visible + patch_count], axis=1)
    zero = jnp.zeros((D,), BF16)
    small = jnp.stack(
        [
            embed_bias,
            attn_norm_gain,
            attn_norm_bias,
            proj_bias,
            mlp_norm_gain,
            mlp_norm_bias,
            down_bias,
            zero,
        ]
    ).astype(F32)
    joined_bias = jnp.concatenate([qkv_bias[0], zero, qkv_bias[1]]).astype(F32)[None]

    (
        unit_one,
        scale_one,
        flipped_one,
        qkv,
        probs,
        flipped_attended,
        residual,
        unit_two,
        scale_two,
        normed_two,
        flipped_two,
    ) = attention(
        *for_embed,
        position.reshape(ROWS, 1),
        position_table,
        small,
        qkv_weight,
        joined_bias,
        proj_weight,
    )
    down_grad, recon, head_grad, up_grad, up_sum, down_low, grad_normed = feed_forward(
        me,
        normed_two,
        residual,
        up_weight,
        up_bias.astype(F32)[None],
        down_weight,
        head_sum,
        *for_head,
        flipped_two,
    )
    down_grad, up_grad = lax.psum((down_grad, up_grad), ALL_AXES)

    def second_half(grad_normed):
        core = lax.axis_index("core").astype(jnp.int32).reshape(1)
        grad_qkv, grad_res, sums, qkv_send, qkv_keep = attention_backward(
            core,
            grad_normed,
            down_low,
            unit_two,
            scale_two,
            small,
            proj_weight,
            qkv,
            probs,
            flipped_one,
            flipped_attended,
        )
        qkv_parts = quarters(qkv_keep, other_core(qkv_send), "z")
        recon_blocks = partners([tie(recon[index], qkv_parts) for index in range(GROUPS)])
        rest_send, rest_keep, grad_inputs = embed_backward(
            me,
            tie(grad_qkv, recon_blocks),
            qkv_weight,
            unit_one,
            scale_one,
            grad_res,
            small,
            *for_embed,
            position.reshape(1, ROWS),
            up_sum,
            sums,
            head_grad,
        )
        rest_parts = quarters(rest_keep, other_core(tie(rest_send, qkv_parts)), "x")
        input_blocks = partners([tie(grad_inputs[index], qkv_parts) for index in range(GROUPS)])
        qkv_total = sum_quarter(qkv_parts, "z")
        rest_total = sum_quarter(rest_parts, "x")
        qkv_plane = split_plane(tie(qkv_total, input_blocks), "z")
        rest_plane = split_plane(tie(rest_total, qkv_plane), "x")
        patch_grad = put(me, items_visible, input_blocks)
        qkv_block = join_plane(tie(qkv_plane, rest_plane, patch_grad), "z")
        rest_block = join_plane(tie(rest_plane, qkv_block), "x")
        qkv_own = join_quarters(qkv_block, "z")
        qkv_other = other_core(qkv_own)
        rest_own = join_quarters(rest_block, "x")
        rest_other = other_core(rest_own)
        first = core[0] == 0
        rest = jnp.concatenate(
            [jnp.where(first, rest_own, rest_other), jnp.where(first, rest_other, rest_own)], axis=1
        )
        recon_all = jnp.stack(recon_blocks)
        by_group = [
            lax.dynamic_index_in_dim(recon_all, my_group ^ group, 0, False) for group in range(GROUPS)
        ]
        return (rest, jnp.stack(by_group), patch_grad, *widen_mixed(core, qkv_own, qkv_other))

    def skipped(grad_normed):
        kept = jax.eval_shape(second_half, grad_normed)
        return tuple(jnp.zeros(part.shape, part.dtype) for part in kept)

    rest, recon, patch_grad, qkv_grad, proj_grad = lax.cond(
        visible[0, 0] >= 0, second_half, skipped, grad_normed
    )
    patch_grad = patch_grad.reshape(batch_items, 2, WIDTH, patch_count)
    patch_grad = jnp.swapaxes(patch_grad, 2, 3)
    down_grad, up_grad = widen(down_grad, up_grad)
    rest = rest[: SUMS_AT + 16].astype(F32)
    embed_grad = lax.dynamic_slice_in_dim(rest, EMBED_AT + my_group * WIDTH, WIDTH, 0)
    total = rest[SUMS_AT : SUMS_AT + 16]
    early = rest[SUMS_AT - 16 : SUMS_AT]
    head_shift = lax.dynamic_index_in_dim(early, 1 + my_group, 0, False)[:WIDTH]
    head_grad = lax.dynamic_slice_in_dim(rest, HEAD_AT + my_group * WIDTH, WIDTH, 0).T
    return (
        jnp.swapaxes(recon.reshape(batch_items, WIDTH, ITEM_ROWS), 1, 2),
        patch_grad,
        embed_grad,
        total[2],
        rest[:SLOTS],
        total[0],
        total[1],
        qkv_grad,
        total[6:8],
        proj_grad,
        total[5],
        total[3],
        total[4],
        up_grad,
        total[8:12].reshape(FF),
        down_grad,
        early[0],
        head_grad,
        head_shift,
    )


def solution(mesh):
    items, groups = ITEMS_AXES, VARS_AXES
    fine = Mesh(mesh.devices.reshape(4, 2, 4, 2, 2), ALL_AXES)
    in_specs = (
        P(items, None, None, groups),
        P(items, None),
        P(items, None, groups),
        P(groups, None),
        *[P()] * 14,
        P(None, groups),
        P(groups),
    )
    out_specs = (
        P(items, None, groups),
        P(items, None, None, groups),
        P(groups, None),
        *[P()] * 14,
        P(None, groups),
        P(groups),
    )
    return jax.shard_map(body, mesh=fine, in_specs=in_specs, out_specs=out_specs, check_vma=False)
```

```python
import functools

import jax
import jax.numpy as jnp
from jax import lax
from jax.experimental import pallas as pl
from jax.experimental.pallas import tpu as pltpu
from jax.sharding import Mesh
from jax.sharding import PartitionSpec as P

HEADS = 12
HEAD_DIM = 64
D = 768
FF = 3072
ITEM_ROWS = 128
OWN_ITEMS = 6
ROWS = OWN_ITEMS * ITEM_ROWS
GROUPS = 4
WIDTH = 80
PAIRS = HEADS // 2
SLOTS = 512
FF_TILE = 768
CUT = 384
REST = 1280
CHUNK = 256
F32 = jnp.float32
BF16 = jnp.bfloat16
VMEM_LIMIT = 58 * 1024 * 1024

ITEMS_AXES = ("z", "ylo", "x")
VARS_AXES = ("yhi", "core")
ALL_AXES = ITEMS_AXES + VARS_AXES


def dot(left, right):
    return jnp.dot(left, right, preferred_element_type=F32)


def dot_nt(left, right):
    return lax.dot_general(left, right, (((1,), (1,)), ((), ())), preferred_element_type=F32)


def dot_tn(left, right):
    return lax.dot_general(left, right, (((0,), (0,)), ((), ())), preferred_element_type=F32)


def normalise(values):
    centre = values - jnp.mean(values, axis=-1, keepdims=True)
    scale = lax.rsqrt(jnp.mean(centre * centre, axis=-1, keepdims=True) + 1e-06)
    return centre * scale, scale


def norm_back(grad, unit, scale, gain):
    wide = grad * gain
    first = jnp.mean(wide, axis=-1, keepdims=True)
    second = jnp.mean(wide * unit, axis=-1, keepdims=True)
    return scale * (wide - first - unit * second)


def column_sum(values):
    return jnp.sum(values, axis=0, keepdims=True)


def low_half():
    return lax.broadcasted_iota(jnp.int32, (ITEM_ROWS, ITEM_ROWS), 1) < HEAD_DIM


def stack_heads(block, first):
    zero = jnp.zeros_like(block)
    return jnp.concatenate([jnp.where(first, block, zero), jnp.where(first, zero, block)], axis=0)


def join_heads(both, first):
    return jnp.where(first, both[:ITEM_ROWS], both[ITEM_ROWS:])


def call(kernel, out_shape, **kwargs):
    return pl.pallas_call(
        kernel,
        out_shape=out_shape,
        compiler_params=pltpu.CompilerParams(vmem_limit_bytes=VMEM_LIMIT),
        cost_estimate=pl.CostEstimate(flops=1_000_000, bytes_accessed=10_000, transcendentals=0),
        **kwargs,
    )


def shape(*dims, dtype=F32):
    return jax.ShapeDtypeStruct(dims, dtype)


def by_partner(*dims):
    return pl.BlockSpec((1,) + dims, lambda step, me: (me[0] ^ step,) + (0,) * len(dims))


def throughout(*dims):
    return pl.BlockSpec(dims, lambda step, me: (0,) * len(dims))


def pick_kernel(me, patches, visible, cotangent, head_rows, head_bias, *outs):
    step = pl.program_id(0)
    head_sum = outs[8]
    numbers = lax.broadcasted_iota(jnp.int32, (SLOTS // 2, ITEM_ROWS // 2), 0)
    first = (me[0] ^ step) * OWN_ITEMS
    picked = []
    total = jnp.zeros((WIDTH, ITEM_ROWS), F32)
    for item in range(OWN_ITEMS):
        hot = (visible[pl.ds(first + item, 1), :] == numbers).astype(BF16)
        rows = [dot(patches[0, item, time], hot) for time in range(2)]
        picked.append(jnp.concatenate(rows, axis=1).astype(BF16))
        total += cotangent[0, item].astype(F32)
    head_sum[...] = jnp.where(step == 0, total, head_sum[...] + total)
    for index in range(GROUPS):

        @pl.when(step == index)
        def _():
            out, cot_out = outs[index], outs[GROUPS + index]
            for item in range(OWN_ITEMS):
                lanes = slice(item * ITEM_ROWS, (item + 1) * ITEM_ROWS)
                out[:, lanes] = picked[item]
                cot_out[0:WIDTH, lanes] = cotangent[0, item]
            cot_out[WIDTH : 2 * WIDTH, :] = head_rows[...]
            cot_out[2 * WIDTH :, :] = jnp.zeros((16, D), BF16)
            rows = lax.broadcasted_iota(jnp.int32, (16, WIDTH), 0)
            bias = jnp.where(rows == 0, head_bias[...].astype(F32), 0.0)
            cot_out[2 * WIDTH :, 0:WIDTH] = bias.astype(BF16)


def pick(me, patches, visible, cotangent, head_rows, head_bias):
    outs = call(
        pick_kernel,
        [shape(WIDTH, D, dtype=BF16)] * 4
        + [shape(2 * WIDTH + 16, D, dtype=BF16)] * 4
        + [shape(WIDTH, ITEM_ROWS)],
        grid_spec=pltpu.PrefetchScalarGridSpec(
            num_scalar_prefetch=1,
            grid=(GROUPS,),
            in_specs=[
                by_partner(OWN_ITEMS, 2, WIDTH, SLOTS // 2),
                throughout(GROUPS * OWN_ITEMS, ITEM_ROWS // 2),
                by_partner(OWN_ITEMS, WIDTH, ITEM_ROWS),
                throughout(WIDTH, D),
                throughout(1, WIDTH),
            ],
            out_specs=[throughout(WIDTH, D)] * 4
            + [throughout(2 * WIDTH + 16, D)] * 4
            + [throughout(WIDTH, ITEM_ROWS)],
        ),
    )(me, patches, visible, cotangent, head_rows, head_bias)
    return outs[:4], outs[4:8], outs[8]


def put_kernel(me, visible, first_rows, second_rows, third_rows, fourth_rows, out, recon):
    step = pl.program_id(0)
    numbers = lax.broadcasted_iota(jnp.int32, (SLOTS // 2, ITEM_ROWS // 2), 0)
    cut = ITEM_ROWS // 2
    for index, rows in enumerate((first_rows, second_rows, third_rows, fourth_rows)):

        @pl.when(step == index)
        def _():
            recon[0] = rows[OWN_ITEMS:]
            for item in range(OWN_ITEMS):
                hot = (visible[0, item : item + 1, :] == numbers).astype(BF16)
                for time in range(2):
                    block = rows[item, :, time * cut : (time + 1) * cut]
                    out[0, item, time] = dot_nt(block, hot).astype(BF16)


def put(me, visible, blocks):
    return call(
        put_kernel,
        (
            shape(GROUPS, OWN_ITEMS, 2, WIDTH, SLOTS // 2, dtype=BF16),
            shape(GROUPS, OWN_ITEMS, WIDTH, ITEM_ROWS, dtype=BF16),
        ),
        grid_spec=pltpu.PrefetchScalarGridSpec(
            num_scalar_prefetch=1,
            grid=(GROUPS,),
            in_specs=[by_partner(OWN_ITEMS, ITEM_ROWS // 2)]
            + [throughout(2 * OWN_ITEMS, WIDTH, ITEM_ROWS)] * 4,
            out_specs=[
                by_partner(OWN_ITEMS, 2, WIDTH, SLOTS // 2),
                by_partner(OWN_ITEMS, WIDTH, ITEM_ROWS),
            ],
        ),
    )(me, visible, *blocks)


EMBED_BIAS, GAIN_ONE, SHIFT_ONE, PROJ_BIAS, GAIN_TWO, SHIFT_TWO, DOWN_BIAS, HEAD_BIAS = range(8)


PARTS = ROWS // CHUNK
CHUNK_ITEMS = CHUNK // ITEM_ROWS
TILES = FF // FF_TILE


def whole(*dims):
    return pl.BlockSpec(dims, lambda *step: (0,) * len(dims), pipeline_mode=pl.Buffered(1))


def held(*dims):
    return pl.BlockSpec(dims, lambda *step: (0,) * len(dims))


def rows_at(first, rows, width, count):
    return pl.BlockSpec((rows, width), lambda step, *_: (jnp.clip(step - first, 0, count - 1), 0))


def columns_at(first, rows, width, count):
    return pl.BlockSpec((rows, width), lambda step, *_: (0, jnp.clip(step - first, 0, count - 1)))


def attention_kernel(
    first_in, second_in, third_in, fourth_in, first_weight, second_weight, third_weight, fourth_weight,
    position, table, small, qkv_far, qkv_bias, proj_far,
    unit_one, scale_one, flipped_one, qkv, probs, flipped_attended, residual, unit_two, scale_two,
    normed_two, flipped_two,
    embedded, attended, qkv_weight, proj_weight, arrivals,
):
    step = pl.program_id(0)
    first = low_half()
    picked = (first_in, second_in, third_in, fourth_in)
    embeds = (first_weight, second_weight, third_weight, fourth_weight)
    qkv_copy = pltpu.make_async_copy(qkv_far, qkv_weight, arrivals.at[0])
    proj_copy = pltpu.make_async_copy(proj_far, proj_weight, arrivals.at[1])

    @pl.when(step == 0)
    def _():
        qkv_copy.start()
        proj_copy.start()

    here = pl.ds(pl.multiple_of(step * CHUNK, CHUNK), CHUNK)
    slots = lax.broadcasted_iota(jnp.int32, (CHUNK, SLOTS), 1)
    hot = (position[...] == slots).astype(BF16)
    values = dot(hot, table[...]) + small[EMBED_BIAS : EMBED_BIAS + 1, :]
    for source, weight in zip(picked, embeds):
        values += dot_tn(source[:, here], weight[...])
    embedded[...] = values
    unit, scale = normalise(values)
    unit_one[...] = unit.astype(BF16)
    scale_one[...] = jnp.broadcast_to(scale, (CHUNK, ITEM_ROWS))
    normed = unit * small[GAIN_ONE : GAIN_ONE + 1, :] + small[SHIFT_ONE : SHIFT_ONE + 1, :]
    normed = normed.astype(BF16)
    flipped_one[...] = normed.T
    pl.when(step == 0)(qkv_copy.wait)
    for part in range(3):
        columns = slice(part * D, (part + 1) * D)
        mixed = dot(normed, qkv_weight[:, columns]) + qkv_bias[:, columns]
        qkv[:, columns] = mixed.astype(BF16)
    for item in range(CHUNK_ITEMS):
        rows = slice(item * ITEM_ROWS, (item + 1) * ITEM_ROWS)
        for pair in range(PAIRS):
            lanes = [
                slice(part * D + pair * ITEM_ROWS, part * D + (pair + 1) * ITEM_ROWS)
                for part in range(3)
            ]
            queries = qkv[rows, lanes[0]] * jnp.asarray(HEAD_DIM**-0.5, BF16)
            scores = dot_nt(stack_heads(queries, first), qkv[rows, lanes[1]])
            weights = jnp.exp(scores - jnp.max(scores, axis=-1, keepdims=True))
            weights = weights * (1.0 / jnp.sum(weights, axis=-1, keepdims=True))
            weights = weights.astype(BF16)
            spot = (item * PAIRS + pair) * CHUNK
            probs[spot : spot + CHUNK, :] = weights
            made = join_heads(dot(weights, qkv[rows, lanes[2]]), first)
            attended[rows, lanes[0]] = made.astype(BF16)
    mixed = attended[...]
    flipped_attended[...] = mixed.T
    pl.when(step == 0)(proj_copy.wait)
    values = embedded[...] + dot(mixed, proj_weight[...]) + small[PROJ_BIAS : PROJ_BIAS + 1, :]
    residual[...] = values + small[DOWN_BIAS : DOWN_BIAS + 1, :]
    unit, scale = normalise(values)
    unit_two[...] = unit.astype(BF16)
    scale_two[...] = jnp.broadcast_to(scale, (CHUNK, ITEM_ROWS))
    normed = unit * small[GAIN_TWO : GAIN_TWO + 1, :] + small[SHIFT_TWO : SHIFT_TWO + 1, :]
    normed = normed.astype(BF16)
    normed_two[...] = normed
    flipped_two[...] = normed.T


def attention(*operands):
    far = pl.BlockSpec(memory_space=pl.ANY)
    return call(
        attention_kernel,
        (
            shape(ROWS, D, dtype=BF16),
            shape(ROWS, ITEM_ROWS),
            shape(D, ROWS, dtype=BF16),
            shape(ROWS, 3 * D, dtype=BF16),
            shape(OWN_ITEMS * PAIRS * CHUNK, ITEM_ROWS, dtype=BF16),
            shape(D, ROWS, dtype=BF16),
            shape(ROWS, D),
            shape(ROWS, D, dtype=BF16),
            shape(ROWS, ITEM_ROWS),
            shape(ROWS, D, dtype=BF16),
            shape(D, ROWS, dtype=BF16),
        ),
        grid=(PARTS,),
        in_specs=[whole(WIDTH, D)] * 8
        + [
            rows_at(0, CHUNK, 1, PARTS),
            whole(SLOTS, D),
            whole(8, D),
            far,
            whole(1, 3 * D),
            far,
        ],
        out_specs=[
            rows_at(0, CHUNK, D, PARTS),
            rows_at(0, CHUNK, ITEM_ROWS, PARTS),
            columns_at(0, D, CHUNK, PARTS),
            rows_at(0, CHUNK, 3 * D, PARTS),
            rows_at(0, CHUNK_ITEMS * PAIRS * CHUNK, ITEM_ROWS, PARTS),
            columns_at(0, D, CHUNK, PARTS),
            rows_at(0, CHUNK, D, PARTS),
            rows_at(0, CHUNK, D, PARTS),
            rows_at(0, CHUNK, ITEM_ROWS, PARTS),
            rows_at(0, CHUNK, D, PARTS),
            columns_at(0, D, CHUNK, PARTS),
        ],
        scratch_shapes=[
            pltpu.VMEM((CHUNK, D), F32),
            pltpu.VMEM((CHUNK, D), BF16),
            pltpu.VMEM((D, 3 * D), BF16),
            pltpu.VMEM((D, D), BF16),
            pltpu.SemaphoreType.DMA((2,)),
        ],
    )(*operands)


def feed_forward_kernel(
    me, normed_two, residual_far, up_weight, up_bias, down_weight, head_sum, first_cot, second_cot, third_cot,
    fourth_cot, flipped_far,
    down_grad, recon, head_grad, up_grad, up_sum, down_low, total,
    activated, slope, residual, flipped, arrivals,
):
    step = pl.program_id(0)
    residual_copy = pltpu.make_async_copy(residual_far, residual, arrivals.at[0])
    flipped_copy = pltpu.make_async_copy(flipped_far, flipped, arrivals.at[1])

    @pl.when(step == 0)
    def _():
        residual_copy.start()
        flipped_copy.start()
        for start in range(0, ROWS, CHUNK):
            rows = slice(start, start + CHUNK)
            grad = jnp.zeros((CHUNK, D), F32)
            for source in (first_cot, second_cot, third_cot, fourth_cot):
                grad += dot_tn(source[0:WIDTH, rows], source[WIDTH : 2 * WIDTH, :])
            down_low[rows, :] = grad.astype(BF16)
            line = column_sum(grad)
            if start:
                line += head_grad[GROUPS * WIDTH : GROUPS * WIDTH + 1, :]
            head_grad[GROUPS * WIDTH : GROUPS * WIDTH + 1, :] = line
        head_grad[GROUPS * WIDTH + 1 :, :] = jnp.zeros((15, D), F32)

    @pl.when(step < TILES)
    def _():
        bias = up_bias[...]
        tile = pl.ds(pl.multiple_of(step * FF_TILE, FF_TILE), FF_TILE)
        for start in range(0, ROWS, CHUNK):
            rows = slice(start, start + CHUNK)
            hidden = dot(normed_two[rows, :], up_weight[...]) + bias
            square = hidden * hidden
            inner = 0.7978845608028654 + (0.7978845608028654 * 0.044715) * square
            curve = jnp.tanh(hidden * inner)
            half = 0.5 + 0.5 * curve
            made = hidden * half
            low = made.astype(BF16)
            activated[rows, :] = low
            rise = 0.7978845608028654 + (0.7978845608028654 * 3 * 0.044715) * square
            slope[rows, tile] = (half + made * (rise - rise * curve)).astype(BF16)
            made = dot(low, down_weight[...])
            total[rows, :] = jnp.where(step == 0, made, total[rows, :] + made)
        down_grad[...] = dot_tn(activated[...], down_low[...]).astype(BF16)

    @pl.when(step == TILES - 1)
    def _():
        residual_copy.wait()
        low = (total[...] + residual[...]).astype(BF16)
        for index, source in enumerate((first_cot, second_cot, third_cot, fourth_cot)):
            group = me[0] ^ index
            column = source[2 * WIDTH :, 0:ITEM_ROWS].astype(F32).T[0:WIDTH, 0:1]
            made = (dot_nt(source[WIDTH : 2 * WIDTH, :], low) + column).astype(BF16)
            for item in range(OWN_ITEMS):
                block = made[:, item * ITEM_ROWS : (item + 1) * ITEM_ROWS]
                recon[index, item] = block
            rows = pl.ds(pl.multiple_of(group * WIDTH, 16), WIDTH)
            head_grad[rows, :] = dot(source[0:WIDTH, :], low)
        rows = lax.broadcasted_iota(jnp.int32, (16, D), 0)
        padded = jnp.concatenate([head_sum[...], jnp.zeros((ITEM_ROWS - WIDTH, ITEM_ROWS), F32)], axis=0)
        line = column_sum(padded.T)
        line = jnp.concatenate([line, jnp.zeros((1, D - ITEM_ROWS), F32)], axis=1)
        head_grad[GROUPS * WIDTH :, :] += jnp.where(rows == 1 + me[0], line, 0.0)

    @pl.when(step >= TILES)
    def _():
        tile = pl.ds(pl.multiple_of((step - TILES) * FF_TILE, FF_TILE), FF_TILE)
        grad = dot_nt(down_low[...], down_weight[...]) * slope[:, tile].astype(F32)
        hidden_low = grad.astype(BF16)
        pl.when(step == TILES)(flipped_copy.wait)
        up_sum[...] = column_sum(hidden_low.astype(F32))
        up_grad[...] = dot(flipped[...], hidden_low).astype(BF16)
        made = dot_nt(hidden_low, up_weight[...])
        total[...] = jnp.where(step == TILES, made, total[...] + made)


def feed_forward(me, *operands):
    again = lambda step: step % TILES
    far = pl.BlockSpec(memory_space=pl.ANY)
    return call(
        feed_forward_kernel,
        (
            shape(FF, D, dtype=BF16),
            shape(GROUPS, OWN_ITEMS, WIDTH, ITEM_ROWS, dtype=BF16),
            shape(GROUPS * WIDTH + 16, D),
            shape(FF, D, dtype=BF16),
            shape(1, FF),
            shape(ROWS, D, dtype=BF16),
            shape(ROWS, D),
        ),
        grid_spec=pltpu.PrefetchScalarGridSpec(
            num_scalar_prefetch=1,
            grid=(2 * TILES,),
            in_specs=[
                whole(ROWS, D),
                far,
                pl.BlockSpec((D, FF_TILE), lambda step, me: (0, again(step))),
                columns_at(0, 1, FF_TILE, TILES),
                pl.BlockSpec((FF_TILE, D), lambda step, me: (again(step), 0)),
                whole(WIDTH, ITEM_ROWS),
            ]
            + [whole(2 * WIDTH + 16, D)] * 4
            + [far],
            out_specs=[
                rows_at(0, FF_TILE, D, TILES),
                held(GROUPS, OWN_ITEMS, WIDTH, ITEM_ROWS),
                held(GROUPS * WIDTH + 16, D),
                rows_at(TILES, FF_TILE, D, TILES),
                columns_at(TILES, 1, FF_TILE, TILES),
                held(ROWS, D),
                held(ROWS, D),
            ],
            scratch_shapes=[
                pltpu.VMEM((ROWS, FF_TILE), BF16),
                pltpu.VMEM((ROWS, FF), BF16),
                pltpu.VMEM((ROWS, D), F32),
                pltpu.VMEM((D, ROWS), BF16),
                pltpu.SemaphoreType.DMA((2,)),
            ],
        ),
    )(me, *operands)


def write_halves(core, values, send, keep):
    left, right = values[:, :CUT], values[:, CUT:]

    @pl.when(core == 0)
    def _():
        keep[...] = left
        send[...] = right

    @pl.when(core != 0)
    def _():
        keep[...] = right
        send[...] = left


def attention_back_kernel(
    core, grad_normed, down_low, unit_two, scale_two, small, proj_weight, qkv, probs, flipped_one_far,
    flipped_attended_far,
    grad_qkv, grad_res, sums, send, keep,
    grads, attn_grad, flipped_one, flipped_attended, arrivals,
):
    step = pl.program_id(0)
    first = low_half()
    flipped_one_copy = pltpu.make_async_copy(flipped_one_far, flipped_one, arrivals.at[0])
    flipped_attended_copy = pltpu.make_async_copy(
        flipped_attended_far, flipped_attended, arrivals.at[1]
    )

    @pl.when(step == 0)
    def _():
        flipped_one_copy.start()
        flipped_attended_copy.start()
        sums[...] = jnp.zeros_like(sums)

    @pl.when(step < PARTS)
    def _():
        here = pl.ds(pl.multiple_of(step * CHUNK, CHUNK), CHUNK)
        unit = unit_two[...].astype(F32)
        grad = grad_normed[...]
        back = norm_back(grad, unit, scale_two[:, 0:1], small[GAIN_TWO : GAIN_TWO + 1, :])
        back += down_low[...].astype(F32)
        grad_res[...] = back
        low = back.astype(BF16)
        grads[here, 3 * D :] = low
        attn_grad[...] = dot_nt(low, proj_weight[...]).astype(BF16)
        sums[0:1, :] += column_sum(grad * unit)
        sums[1:2, :] += column_sum(grad)
        sums[2:3, :] += column_sum(back)
        scaling = jnp.asarray(HEAD_DIM**-0.5, F32)
        for item in range(CHUNK_ITEMS):
            rows = slice(item * ITEM_ROWS, (item + 1) * ITEM_ROWS)
            for pair in range(PAIRS):
                lanes = [
                    slice(kind * D + pair * ITEM_ROWS, kind * D + (pair + 1) * ITEM_ROWS)
                    for kind in range(3)
                ]
                queries = stack_heads(qkv[rows, lanes[0]], first)
                cot = stack_heads(attn_grad[rows, lanes[0]], first)
                spot = (item * PAIRS + pair) * CHUNK
                low = probs[spot : spot + CHUNK, :]
                wide = low.astype(F32)
                grad_probs = dot_nt(cot, qkv[rows, lanes[2]])
                grad_qkv[rows, lanes[2]] = dot_tn(low, cot).astype(BF16)
                centre = jnp.sum(wide * grad_probs, axis=-1, keepdims=True)
                scores_low = (wide * (grad_probs - centre)).astype(BF16)
                made = join_heads(dot(scores_low, qkv[rows, lanes[1]]), first)
                grad_qkv[rows, lanes[0]] = (made * scaling).astype(BF16)
                made = dot_tn(scores_low, queries) * scaling
                grad_qkv[rows, lanes[1]] = made.astype(BF16)
        grads[here, : 3 * D] = grad_qkv[...]
        sums[3:4, :] += column_sum(grad_qkv[:, :D].astype(F32))
        sums[4:5, :] += column_sum(grad_qkv[:, 2 * D :].astype(F32))

    for tile in range(4):

        @pl.when(step == PARTS + tile)
        def _():
            if tile == 0:
                flipped_one_copy.wait()
            if tile == 3:
                flipped_attended_copy.wait()
            left = flipped_one if tile < 3 else flipped_attended
            made = dot(left[...], grads[:, tile * D : (tile + 1) * D])
            write_halves(core[0], made.astype(BF16), send, keep)


def attention_backward(*operands):
    far = pl.BlockSpec(memory_space=pl.ANY)
    return call(
        attention_back_kernel,
        (
            shape(ROWS, 3 * D, dtype=BF16),
            shape(ROWS, D),
            shape(8, D),
            shape(4 * D, CUT, dtype=BF16),
            shape(4 * D, CUT, dtype=BF16),
        ),
        grid=(PARTS + 4,),
        in_specs=[
            pl.BlockSpec(memory_space=pltpu.SMEM),
            rows_at(0, CHUNK, D, PARTS),
            rows_at(0, CHUNK, D, PARTS),
            rows_at(0, CHUNK, D, PARTS),
            rows_at(0, CHUNK, ITEM_ROWS, PARTS),
            whole(8, D),
            whole(D, D),
            rows_at(0, CHUNK, 3 * D, PARTS),
            rows_at(0, CHUNK_ITEMS * PAIRS * CHUNK, ITEM_ROWS, PARTS),
            far,
            far,
        ],
        out_specs=[
            rows_at(0, CHUNK, 3 * D, PARTS),
            rows_at(0, CHUNK, D, PARTS),
            held(8, D),
            rows_at(PARTS, D, CUT, 4),
            rows_at(PARTS, D, CUT, 4),
        ],
        scratch_shapes=[
            pltpu.VMEM((ROWS, 4 * D), BF16),
            pltpu.VMEM((CHUNK, D), BF16),
            pltpu.VMEM((D, ROWS), BF16),
            pltpu.VMEM((D, ROWS), BF16),
            pltpu.SemaphoreType.DMA((2,)),
        ],
    )(*operands)


EMBED_AT = SLOTS
HEAD_AT = EMBED_AT + GROUPS * WIDTH
SUMS_AT = HEAD_AT + GROUPS * WIDTH + 16


def embed_back_kernel(
    place, grads, qkv_weight, unit_one, scale_one, grad_res, small, first_in, second_in, third_in, fourth_in,
    first_weight, second_weight, third_weight, fourth_weight, position, up_sum, sums, head_grad, recon,
    send, keep, first_out, second_out, third_out, fourth_out, embedded_low, rest,
):
    gain_one = small[GAIN_ONE : GAIN_ONE + 1, :]
    me = place[0]
    sources = (first_in, second_in, third_in, fourth_in)
    outs = (first_out, second_out, third_out, fourth_out)
    for index, out in enumerate(outs):
        out[OWN_ITEMS:] = recon[index]

    def first_norm(step, carry):
        rows = pl.ds(pl.multiple_of(step * CHUNK, CHUNK), CHUNK)
        grad = dot_nt(grads[rows, :], qkv_weight[...])
        unit = unit_one[rows, :].astype(F32)
        total = grad_res[rows, :] + norm_back(grad, unit, scale_one[rows, 0:1], gain_one)
        low = total.astype(BF16)
        embedded_low[rows, :] = low
        for index, weight in enumerate((first_weight, second_weight, third_weight, fourth_weight)):
            made = dot_nt(weight[...], low).astype(BF16)
            for part in range(CHUNK // ITEM_ROWS):
                block = made[:, part * ITEM_ROWS : (part + 1) * ITEM_ROWS]
                item = step * (CHUNK // ITEM_ROWS) + part
                outs[index][pl.ds(item, 1)] = block[None]
        gain, shift, bias = carry
        return gain + column_sum(grad * unit), shift + column_sum(grad), bias + column_sum(total)

    none = jnp.zeros((1, D), F32)
    gain, shift, bias = lax.fori_loop(0, ROWS // CHUNK, first_norm, (none, none, none))
    slots = lax.broadcasted_iota(jnp.int32, (SLOTS, ROWS), 0)
    hot = (position[...] == slots).astype(BF16)
    rest[0:SLOTS, :] = dot(hot, embedded_low[...])
    for index, source in enumerate(sources):
        rows = pl.ds(pl.multiple_of(EMBED_AT + (me ^ index) * WIDTH, 16), WIDTH)
        rest[rows, :] = dot(source[...], embedded_low[...])
    rest[HEAD_AT:SUMS_AT, :] = head_grad[...]
    rest[SUMS_AT:, :] = jnp.zeros((REST - SUMS_AT, D), F32)
    for row, value in enumerate((gain, shift, bias)):
        rest[SUMS_AT + row : SUMS_AT + row + 1, :] = value
    rest[SUMS_AT + 3 : SUMS_AT + 8, :] = sums[0:5, :]
    for row in range(FF // D):
        at = SUMS_AT + 8 + row
        rest[at : at + 1, :] = up_sum[:, row * D : (row + 1) * D]
    write_halves(lax.rem(me, 2), rest[...].astype(BF16), send, keep)


def embed_backward(place, *operands):
    vmem = pl.BlockSpec(memory_space=pltpu.VMEM)
    return call(
        embed_back_kernel,
        (
            shape(REST, CUT, dtype=BF16),
            shape(REST, CUT, dtype=BF16),
        )
        + (shape(2 * OWN_ITEMS, WIDTH, ITEM_ROWS, dtype=BF16),) * 4,
        in_specs=[pl.BlockSpec(memory_space=pltpu.SMEM)] + [vmem] * len(operands),
        out_specs=[vmem] * 6,
        scratch_shapes=[pltpu.VMEM((ROWS, D), BF16), pltpu.VMEM((REST, D), F32)],
    )(place, *operands)


WIDEN_STEPS = 6


def widen_kernel(down, up, down_out, up_out):
    down_out[...] = down[...].astype(F32)
    for tile in range(4):
        up_out[:, tile * D : (tile + 1) * D] = up[tile].astype(F32)


def widen_mixed_kernel(core, own, other, qkv_out, proj_out):
    def write(left, right):
        for tile in range(4):
            out, start = (qkv_out, tile * D) if tile < 3 else (proj_out, 0)
            out[:, start : start + CUT] = left[tile].astype(F32)
            out[:, start + CUT : start + D] = right[tile].astype(F32)

    pl.when(core[0] == 0)(lambda: write(own, other))
    pl.when(core[0] != 0)(lambda: write(other, own))


def row_blocks(count, width):
    return pl.BlockSpec((count * D // WIDEN_STEPS, width), lambda step: (step, 0))


def tile_rows():
    return pl.BlockSpec((4, D // WIDEN_STEPS, D), lambda step: (0, step, 0))


def widen(down, up):
    return call(
        widen_kernel,
        (shape(FF, D), shape(D, FF)),
        grid=(WIDEN_STEPS,),
        in_specs=[row_blocks(4, D), tile_rows()],
        out_specs=[row_blocks(4, D), row_blocks(1, FF)],
    )(down, up.reshape(4, D, D))


def widen_mixed(core, own, other):
    halves = pl.BlockSpec((4, D // WIDEN_STEPS, CUT), lambda step: (0, step, 0))
    return call(
        widen_mixed_kernel,
        (shape(D, 3 * D), shape(D, D)),
        grid=(WIDEN_STEPS,),
        in_specs=[pl.BlockSpec(memory_space=pltpu.SMEM), halves, halves],
        out_specs=[row_blocks(1, 3 * D), row_blocks(1, D)],
    )(core, own.reshape(4, D, CUT), other.reshape(4, D, CUT))


def extract_kernel(place, own, other, position_out, embed_out, head_out, totals_out):
    group = place[0]
    parts = (
        (position_out, 0),
        (embed_out, pl.multiple_of(EMBED_AT + group * WIDTH, 16)),
        (head_out, pl.multiple_of(HEAD_AT + group * WIDTH, 16)),
        (totals_out, SUMS_AT - 16),
    )

    def write(left, right):
        for out, start in parts:
            rows = pl.ds(start, out.shape[0])
            out[:, :CUT] = left[rows, :].astype(F32)
            out[:, CUT:] = right[rows, :].astype(F32)

    pl.when(lax.rem(group, 2) == 0)(lambda: write(own, other))
    pl.when(lax.rem(group, 2) != 0)(lambda: write(other, own))


def extract(me, own, other):
    vmem = pl.BlockSpec(memory_space=pltpu.VMEM)
    return call(
        extract_kernel,
        (shape(SLOTS, D), shape(WIDTH, D), shape(WIDTH, D), shape(32, D)),
        in_specs=[pl.BlockSpec(memory_space=pltpu.SMEM), vmem, vmem],
        out_specs=[vmem] * 4,
    )(me, own, other)


def tie(value, *tokens):
    return lax.optimization_barrier((value, tokens))[0]


SWAP = [(0, 1), (1, 0)]
PLANES = {"x": ("z", "ylo", "yhi"), "z": ("ylo", "x", "yhi")}


def other_core(value):
    return lax.ppermute(value, "core", SWAP)


def shift(value, axis, distance):
    return lax.ppermute(value, axis, [(i, (i + distance) % 4) for i in range(4)])


def quarters(keep, arrived, axis):
    own = (keep.astype(F32) + arrived.astype(F32)).astype(BF16)
    rows = own.shape[0] // 4
    place = lax.axis_index(axis)
    return [
        lax.dynamic_slice_in_dim(own, ((place + step) % 4) * rows, rows, 0) for step in range(4)
    ]


def sum_quarter(parts, axis):
    total = parts[0].astype(F32)
    for distance in (1, 3, 2):
        total += shift(parts[distance], axis, distance).astype(F32)
    return total.astype(BF16)


def split_plane(block, axis):
    lanes = block.shape[1] if block.shape[0] % 128 == 0 else ITEM_ROWS
    return lax.all_to_all(block.reshape(16, -1, lanes), PLANES[axis], 0, 0)


def join_plane(parts, axis):
    share = jnp.sum(parts.astype(F32), axis=0).astype(BF16)
    parts = lax.all_to_all(jnp.broadcast_to(share[None], parts.shape), PLANES[axis], 0, 0)
    return parts.reshape(-1, CUT)


def join_quarters(own, axis):
    turned = [own, shift(own, axis, 3), shift(own, axis, 2), shift(own, axis, 1)]
    turned = jnp.concatenate(turned + turned[:3], axis=0)
    start = ((4 - lax.axis_index(axis)) % 4) * own.shape[0]
    return lax.dynamic_slice_in_dim(turned, start, 4 * own.shape[0], 0)


def body(
    patches,
    visible,
    recon_cotangent,
    embed_weight,
    embed_bias,
    position_table,
    attn_norm_gain,
    attn_norm_bias,
    qkv_weight,
    qkv_bias,
    proj_weight,
    proj_bias,
    mlp_norm_gain,
    mlp_norm_bias,
    up_weight,
    up_bias,
    down_weight,
    down_bias,
    head_weight,
    head_bias,
):
    my_group = lax.axis_index(VARS_AXES)
    me = my_group.astype(jnp.int32).reshape(1)
    batch_items = patches.shape[0]
    patch_count = patches.shape[2]

    def partners(blocks):
        return [
            blocks[0],
            other_core(blocks[1]),
            lax.ppermute(blocks[2], "yhi", SWAP),
            lax.ppermute(blocks[3], ("yhi", "core"), [(i, 3 - i) for i in range(4)]),
        ]

    items_visible = visible.reshape(GROUPS, OWN_ITEMS, ITEM_ROWS // 2)
    far_embed = lax.ppermute(embed_weight, "yhi", SWAP)
    near_embed = other_core(embed_weight)
    to_embed, to_head, head_sum = pick(
        me,
        jnp.swapaxes(patches, 2, 3).reshape(GROUPS, OWN_ITEMS, 2, WIDTH, patch_count),
        visible,
        jnp.swapaxes(recon_cotangent, 1, 2).reshape(GROUPS, OWN_ITEMS, WIDTH, ITEM_ROWS),
        head_weight.T,
        head_bias[None],
    )
    picked = partners(to_embed)
    embeds = [embed_weight, near_embed, far_embed, other_core(far_embed)]
    for_embed = [*picked, *embeds]
    for_head = partners(to_head)
    own_visible = lax.dynamic_slice_in_dim(visible, my_group * OWN_ITEMS, OWN_ITEMS, 0)
    position = jnp.concatenate([own_visible, own_visible + patch_count], axis=1)
    zero = jnp.zeros((D,), BF16)
    small = jnp.stack(
        [
            embed_bias,
            attn_norm_gain,
            attn_norm_bias,
            proj_bias,
            mlp_norm_gain,
            mlp_norm_bias,
            down_bias,
            zero,
        ]
    ).astype(F32)
    joined_bias = jnp.concatenate([qkv_bias[0], zero, qkv_bias[1]]).astype(F32)[None]

    (
        unit_one,
        scale_one,
        flipped_one,
        qkv,
        probs,
        flipped_attended,
        residual,
        unit_two,
        scale_two,
        normed_two,
        flipped_two,
    ) = attention(
        *for_embed,
        position.reshape(ROWS, 1),
        position_table,
        small,
        qkv_weight,
        joined_bias,
        proj_weight,
    )
    down_grad, recon, head_grad, up_grad, up_sum, down_low, grad_normed = feed_forward(
        me,
        normed_two,
        residual,
        up_weight,
        up_bias.astype(F32)[None],
        down_weight,
        head_sum,
        *for_head,
        flipped_two,
    )
    down_grad, up_grad = lax.psum((down_grad, up_grad), ALL_AXES)

    def second_half(grad_normed):
        core = lax.axis_index("core").astype(jnp.int32).reshape(1)
        grad_qkv, grad_res, sums, qkv_send, qkv_keep = attention_backward(
            core,
            grad_normed,
            down_low,
            unit_two,
            scale_two,
            small,
            proj_weight,
            qkv,
            probs,
            flipped_one,
            flipped_attended,
        )
        qkv_parts = quarters(qkv_keep, other_core(qkv_send), "z")
        rest_send, rest_keep, *blocks = embed_backward(
            me,
            grad_qkv,
            qkv_weight,
            unit_one,
            scale_one,
            grad_res,
            small,
            *for_embed,
            position.reshape(1, ROWS),
            up_sum,
            sums,
            head_grad,
            recon,
        )
        rest_parts = quarters(rest_keep, other_core(tie(rest_send, qkv_parts)), "x")
        qkv_plane = split_plane(sum_quarter(qkv_parts, "z"), "z")
        rest_block = sum_quarter(rest_parts, "x")
        blocks = partners([tie(block, qkv_plane) for block in blocks])
        qkv_block = join_plane(qkv_plane, "z")
        rest_plane = split_plane(tie(rest_block, qkv_block), "x")
        patch_grad, rows = put(me, items_visible, blocks)
        rest_block = join_plane(tie(rest_plane, blocks), "x")
        qkv_own = join_quarters(qkv_block, "z")
        qkv_other = other_core(tie(qkv_own, patch_grad))
        rest_own = join_quarters(rest_block, "x")
        rest_other = other_core(rest_own)
        return (
            rows,
            patch_grad,
            *extract(me, rest_own, rest_other),
            *widen_mixed(core, qkv_own, qkv_other),
        )

    def skipped(grad_normed):
        kept = jax.eval_shape(second_half, grad_normed)
        return tuple(jnp.zeros(part.shape, part.dtype) for part in kept)

    recon, patch_grad, position_grad, embed_grad, head_grad, total, qkv_grad, proj_grad = lax.cond(
        visible[0, 0] >= 0, second_half, skipped, grad_normed
    )
    patch_grad = patch_grad.reshape(batch_items, 2, WIDTH, patch_count)
    patch_grad = jnp.swapaxes(patch_grad, 2, 3)
    down_grad, up_grad = widen(down_grad, up_grad)
    head_shift = lax.dynamic_index_in_dim(total, 1 + my_group, 0, False)[:WIDTH]
    early, total = total[0], total[16:]
    return (
        jnp.swapaxes(recon.reshape(batch_items, WIDTH, ITEM_ROWS), 1, 2),
        patch_grad,
        embed_grad,
        total[2],
        position_grad,
        total[0],
        total[1],
        qkv_grad,
        total[6:8],
        proj_grad,
        total[5],
        total[3],
        total[4],
        up_grad,
        total[8:12].reshape(FF),
        down_grad,
        early,
        head_grad.T,
        head_shift,
    )


def solution(mesh):
    items, groups = ITEMS_AXES, VARS_AXES
    fine = Mesh(mesh.devices.reshape(4, 2, 4, 2, 2), ALL_AXES)
    in_specs = (
        P(items, None, None, groups),
        P(items, None),
        P(items, None, groups),
        P(groups, None),
        *[P()] * 14,
        P(None, groups),
        P(groups),
    )
    out_specs = (
        P(items, None, groups),
        P(items, None, None, groups),
        P(groups, None),
        *[P()] * 14,
        P(None, groups),
        P(groups),
    )
    return jax.shard_map(body, mesh=fine, in_specs=in_specs, out_specs=out_specs, check_vma=False)
```

```python
import functools

import jax
import jax.numpy as jnp
from jax import lax
from jax.experimental import pallas as pl
from jax.experimental.pallas import tpu as pltpu
from jax.sharding import Mesh
from jax.sharding import PartitionSpec as P

HEADS = 12
HEAD_DIM = 64
D = 768
FF = 3072
ITEM_ROWS = 128
OWN_ITEMS = 6
ROWS = OWN_ITEMS * ITEM_ROWS
GROUPS = 4
WIDTH = 80
PAIRS = HEADS // 2
SLOTS = 512
FF_TILE = 768
CUT = 384
REST = 1280
CHUNK = 256
F32 = jnp.float32
BF16 = jnp.bfloat16
VMEM_LIMIT = 58 * 1024 * 1024

ITEMS_AXES = ("z", "ylo", "x")
VARS_AXES = ("yhi", "core")
ALL_AXES = ITEMS_AXES + VARS_AXES


def dot(left, right):
    return jnp.dot(left, right, preferred_element_type=F32)


def dot_nt(left, right):
    return lax.dot_general(left, right, (((1,), (1,)), ((), ())), preferred_element_type=F32)


def dot_tn(left, right):
    return lax.dot_general(left, right, (((0,), (0,)), ((), ())), preferred_element_type=F32)


def normalise(values):
    centre = values - jnp.mean(values, axis=-1, keepdims=True)
    scale = lax.rsqrt(jnp.mean(centre * centre, axis=-1, keepdims=True) + 1e-06)
    return centre * scale, scale


def norm_back(grad, unit, scale, gain):
    wide = grad * gain
    first = jnp.mean(wide, axis=-1, keepdims=True)
    second = jnp.mean(wide * unit, axis=-1, keepdims=True)
    return scale * (wide - first - unit * second)


def column_sum(values):
    return jnp.sum(values, axis=0, keepdims=True)


def low_half():
    return lax.broadcasted_iota(jnp.int32, (ITEM_ROWS, ITEM_ROWS), 1) < HEAD_DIM


def stack_heads(block, first):
    zero = jnp.zeros_like(block)
    return jnp.concatenate([jnp.where(first, block, zero), jnp.where(first, zero, block)], axis=0)


def join_heads(both, first):
    return jnp.where(first, both[:ITEM_ROWS], both[ITEM_ROWS:])


def call(kernel, out_shape, **kwargs):
    return pl.pallas_call(
        kernel,
        out_shape=out_shape,
        compiler_params=pltpu.CompilerParams(vmem_limit_bytes=VMEM_LIMIT),
        cost_estimate=pl.CostEstimate(flops=1_000_000, bytes_accessed=10_000, transcendentals=0),
        **kwargs,
    )


def shape(*dims, dtype=F32):
    return jax.ShapeDtypeStruct(dims, dtype)


def by_partner(*dims):
    return pl.BlockSpec((1,) + dims, lambda step, me: (me[0] ^ step,) + (0,) * len(dims))


def throughout(*dims):
    return pl.BlockSpec(dims, lambda step, me: (0,) * len(dims))


def pick_kernel(me, patches, visible, cotangent, head_rows, head_bias, *outs):
    step = pl.program_id(0)
    head_sum = outs[8]
    numbers = lax.broadcasted_iota(jnp.int32, (SLOTS // 2, ITEM_ROWS // 2), 0)
    first = (me[0] ^ step) * OWN_ITEMS
    picked = []
    total = jnp.zeros((WIDTH, ITEM_ROWS), F32)
    for item in range(OWN_ITEMS):
        hot = (visible[pl.ds(first + item, 1), :] == numbers).astype(BF16)
        rows = [dot(patches[0, item, time], hot) for time in range(2)]
        picked.append(jnp.concatenate(rows, axis=1).astype(BF16))
        total += cotangent[0, item].astype(F32)
    head_sum[...] = jnp.where(step == 0, total, head_sum[...] + total)
    for index in range(GROUPS):

        @pl.when(step == index)
        def _():
            out, cot_out = outs[index], outs[GROUPS + index]
            for item in range(OWN_ITEMS):
                lanes = slice(item * ITEM_ROWS, (item + 1) * ITEM_ROWS)
                out[:, lanes] = picked[item]
                cot_out[0:WIDTH, lanes] = cotangent[0, item]
            cot_out[WIDTH : 2 * WIDTH, :] = head_rows[...]
            cot_out[2 * WIDTH :, :] = jnp.zeros((16, D), BF16)
            rows = lax.broadcasted_iota(jnp.int32, (16, WIDTH), 0)
            bias = jnp.where(rows == 0, head_bias[...].astype(F32), 0.0)
            cot_out[2 * WIDTH :, 0:WIDTH] = bias.astype(BF16)


def pick(me, patches, visible, cotangent, head_rows, head_bias):
    outs = call(
        pick_kernel,
        [shape(WIDTH, D, dtype=BF16)] * 4
        + [shape(2 * WIDTH + 16, D, dtype=BF16)] * 4
        + [shape(WIDTH, ITEM_ROWS)],
        grid_spec=pltpu.PrefetchScalarGridSpec(
            num_scalar_prefetch=1,
            grid=(GROUPS,),
            in_specs=[
                by_partner(OWN_ITEMS, 2, WIDTH, SLOTS // 2),
                throughout(GROUPS * OWN_ITEMS, ITEM_ROWS // 2),
                by_partner(OWN_ITEMS, WIDTH, ITEM_ROWS),
                throughout(WIDTH, D),
                throughout(1, WIDTH),
            ],
            out_specs=[throughout(WIDTH, D)] * 4
            + [throughout(2 * WIDTH + 16, D)] * 4
            + [throughout(WIDTH, ITEM_ROWS)],
        ),
    )(me, patches, visible, cotangent, head_rows, head_bias)
    return outs[:4], outs[4:8], outs[8]


def put_kernel(me, visible, first_rows, second_rows, third_rows, fourth_rows, out, recon):
    step = pl.program_id(0)
    numbers = lax.broadcasted_iota(jnp.int32, (SLOTS // 2, ITEM_ROWS // 2), 0)
    cut = ITEM_ROWS // 2
    for index, rows in enumerate((first_rows, second_rows, third_rows, fourth_rows)):

        @pl.when(step == index)
        def _():
            recon[0] = rows[OWN_ITEMS:]
            for item in range(OWN_ITEMS):
                hot = (visible[0, item : item + 1, :] == numbers).astype(BF16)
                for time in range(2):
                    block = rows[item, :, time * cut : (time + 1) * cut]
                    out[0, item, time] = dot_nt(block, hot).astype(BF16)


def put(me, visible, blocks):
    return call(
        put_kernel,
        (
            shape(GROUPS, OWN_ITEMS, 2, WIDTH, SLOTS // 2, dtype=BF16),
            shape(GROUPS, OWN_ITEMS, WIDTH, ITEM_ROWS, dtype=BF16),
        ),
        grid_spec=pltpu.PrefetchScalarGridSpec(
            num_scalar_prefetch=1,
            grid=(GROUPS,),
            in_specs=[by_partner(OWN_ITEMS, ITEM_ROWS // 2)]
            + [throughout(2 * OWN_ITEMS, WIDTH, ITEM_ROWS)] * 4,
            out_specs=[
                by_partner(OWN_ITEMS, 2, WIDTH, SLOTS // 2),
                by_partner(OWN_ITEMS, WIDTH, ITEM_ROWS),
            ],
        ),
    )(me, visible, *blocks)


EMBED_BIAS, GAIN_ONE, SHIFT_ONE, PROJ_BIAS, GAIN_TWO, SHIFT_TWO, DOWN_BIAS, HEAD_BIAS = range(8)


PARTS = ROWS // CHUNK
CHUNK_ITEMS = CHUNK // ITEM_ROWS
TILES = FF // FF_TILE


def whole(*dims):
    return pl.BlockSpec(dims, lambda *step: (0,) * len(dims), pipeline_mode=pl.Buffered(1))


def held(*dims):
    return pl.BlockSpec(dims, lambda *step: (0,) * len(dims))


def rows_at(first, rows, width, count):
    return pl.BlockSpec((rows, width), lambda step, *_: (jnp.clip(step - first, 0, count - 1), 0))


def columns_at(first, rows, width, count):
    return pl.BlockSpec((rows, width), lambda step, *_: (0, jnp.clip(step - first, 0, count - 1)))


def attention_kernel(
    first_in, second_in, third_in, fourth_in, first_weight, second_weight, third_weight, fourth_weight,
    position, table, small, qkv_far, qkv_bias, proj_far,
    unit_one, scale_one, flipped_one, qkv, probs, flipped_attended, residual, unit_two, scale_two,
    normed_two, flipped_two,
    embedded, attended, qkv_weight, proj_weight, arrivals,
):
    step = pl.program_id(0)
    first = low_half()
    picked = (first_in, second_in, third_in, fourth_in)
    embeds = (first_weight, second_weight, third_weight, fourth_weight)
    qkv_copy = pltpu.make_async_copy(qkv_far, qkv_weight, arrivals.at[0])
    proj_copy = pltpu.make_async_copy(proj_far, proj_weight, arrivals.at[1])

    @pl.when(step == 0)
    def _():
        qkv_copy.start()
        proj_copy.start()

    here = pl.ds(pl.multiple_of(step * CHUNK, CHUNK), CHUNK)
    slots = lax.broadcasted_iota(jnp.int32, (CHUNK, SLOTS), 1)
    hot = (position[...] == slots).astype(BF16)
    values = dot(hot, table[...]) + small[EMBED_BIAS : EMBED_BIAS + 1, :]
    for source, weight in zip(picked, embeds):
        values += dot_tn(source[:, here], weight[...])
    embedded[...] = values
    unit, scale = normalise(values)
    unit_one[...] = unit.astype(BF16)
    scale_one[...] = jnp.broadcast_to(scale, (CHUNK, ITEM_ROWS))
    normed = unit * small[GAIN_ONE : GAIN_ONE + 1, :] + small[SHIFT_ONE : SHIFT_ONE + 1, :]
    normed = normed.astype(BF16)
    flipped_one[...] = normed.T
    pl.when(step == 0)(qkv_copy.wait)
    for part in range(3):
        columns = slice(part * D, (part + 1) * D)
        mixed = dot(normed, qkv_weight[:, columns]) + qkv_bias[:, columns]
        qkv[:, columns] = mixed.astype(BF16)
    for item in range(CHUNK_ITEMS):
        rows = slice(item * ITEM_ROWS, (item + 1) * ITEM_ROWS)
        for pair in range(PAIRS):
            lanes = [
                slice(part * D + pair * ITEM_ROWS, part * D + (pair + 1) * ITEM_ROWS)
                for part in range(3)
            ]
            queries = qkv[rows, lanes[0]] * jnp.asarray(HEAD_DIM**-0.5, BF16)
            scores = dot_nt(stack_heads(queries, first), qkv[rows, lanes[1]])
            weights = jnp.exp(scores - jnp.max(scores, axis=-1, keepdims=True))
            weights = weights * (1.0 / jnp.sum(weights, axis=-1, keepdims=True))
            weights = weights.astype(BF16)
            spot = (item * PAIRS + pair) * CHUNK
            probs[spot : spot + CHUNK, :] = weights
            made = join_heads(dot(weights, qkv[rows, lanes[2]]), first)
            attended[rows, lanes[0]] = made.astype(BF16)
    mixed = attended[...]
    flipped_attended[...] = mixed.T
    pl.when(step == 0)(proj_copy.wait)
    values = embedded[...] + dot(mixed, proj_weight[...]) + small[PROJ_BIAS : PROJ_BIAS + 1, :]
    residual[...] = values + small[DOWN_BIAS : DOWN_BIAS + 1, :]
    unit, scale = normalise(values)
    unit_two[...] = unit.astype(BF16)
    scale_two[...] = jnp.broadcast_to(scale, (CHUNK, ITEM_ROWS))
    normed = unit * small[GAIN_TWO : GAIN_TWO + 1, :] + small[SHIFT_TWO : SHIFT_TWO + 1, :]
    normed = normed.astype(BF16)
    normed_two[...] = normed
    flipped_two[...] = normed.T


def attention(*operands):
    far = pl.BlockSpec(memory_space=pl.ANY)
    return call(
        attention_kernel,
        (
            shape(ROWS, D, dtype=BF16),
            shape(ROWS, ITEM_ROWS),
            shape(D, ROWS, dtype=BF16),
            shape(ROWS, 3 * D, dtype=BF16),
            shape(OWN_ITEMS * PAIRS * CHUNK, ITEM_ROWS, dtype=BF16),
            shape(D, ROWS, dtype=BF16),
            shape(ROWS, D),
            shape(ROWS, D, dtype=BF16),
            shape(ROWS, ITEM_ROWS),
            shape(ROWS, D, dtype=BF16),
            shape(D, ROWS, dtype=BF16),
        ),
        grid=(PARTS,),
        in_specs=[whole(WIDTH, D)] * 8
        + [
            rows_at(0, CHUNK, 1, PARTS),
            whole(SLOTS, D),
            whole(8, D),
            far,
            whole(1, 3 * D),
            far,
        ],
        out_specs=[
            rows_at(0, CHUNK, D, PARTS),
            rows_at(0, CHUNK, ITEM_ROWS, PARTS),
            columns_at(0, D, CHUNK, PARTS),
            rows_at(0, CHUNK, 3 * D, PARTS),
            rows_at(0, CHUNK_ITEMS * PAIRS * CHUNK, ITEM_ROWS, PARTS),
            columns_at(0, D, CHUNK, PARTS),
            rows_at(0, CHUNK, D, PARTS),
            rows_at(0, CHUNK, D, PARTS),
            rows_at(0, CHUNK, ITEM_ROWS, PARTS),
            rows_at(0, CHUNK, D, PARTS),
            columns_at(0, D, CHUNK, PARTS),
        ],
        scratch_shapes=[
            pltpu.VMEM((CHUNK, D), F32),
            pltpu.VMEM((CHUNK, D), BF16),
            pltpu.VMEM((D, 3 * D), BF16),
            pltpu.VMEM((D, D), BF16),
            pltpu.SemaphoreType.DMA((2,)),
        ],
    )(*operands)


BACK = TILES
LAST = BACK + TILES + PARTS


def block_kernel(
    me, normed_two, residual_far, up_weight, up_bias, down_weight, head_sum, first_cot, second_cot, third_cot,
    fourth_cot, flipped_two_far, unit_two, scale_two, small, proj_far, qkv, probs, flipped_one_far,
    flipped_attended_far,
    down_grad, recon, head_grad, up_grad, up_sum, grad_qkv, grad_res, sums, mixed_grad,
    total, activated, slope, down_low, attn_grad, residual, flipped_two, proj_weight, flipped_one,
    flipped_attended, arrivals,
):
    step = pl.program_id(0)
    first = low_half()
    pairs = (
        (residual_far, residual),
        (flipped_two_far, flipped_two),
        (proj_far, proj_weight),
        (flipped_one_far, flipped_one),
        (flipped_attended_far, flipped_attended),
    )
    copies = [
        pltpu.make_async_copy(source, target, arrivals.at[index])
        for index, (source, target) in enumerate(pairs)
    ]
    residual_copy, flipped_two_copy, proj_copy, flipped_one_copy, flipped_attended_copy = copies

    @pl.when(step == 0)
    def _():
        for copy in copies:
            copy.start()
        for start in range(0, ROWS, CHUNK):
            rows = slice(start, start + CHUNK)
            grad = jnp.zeros((CHUNK, D), F32)
            for source in (first_cot, second_cot, third_cot, fourth_cot):
                grad += dot_tn(source[0:WIDTH, rows], source[WIDTH : 2 * WIDTH, :])
            down_low[rows, :] = grad.astype(BF16)
            line = column_sum(grad)
            if start:
                line += head_grad[GROUPS * WIDTH : GROUPS * WIDTH + 1, :]
            head_grad[GROUPS * WIDTH : GROUPS * WIDTH + 1, :] = line
        head_grad[GROUPS * WIDTH + 1 :, :] = jnp.zeros((15, D), F32)

    @pl.when(step < TILES)
    def _():
        bias = up_bias[...]
        tile = pl.ds(pl.multiple_of(step * FF_TILE, FF_TILE), FF_TILE)
        for start in range(0, ROWS, CHUNK):
            rows = slice(start, start + CHUNK)
            hidden = dot(normed_two[rows, :], up_weight[...]) + bias
            square = hidden * hidden
            inner = 0.7978845608028654 + (0.7978845608028654 * 0.044715) * square
            curve = jnp.tanh(hidden * inner)
            half = 0.5 + 0.5 * curve
            made = hidden * half
            low = made.astype(BF16)
            activated[rows, :] = low
            rise = 0.7978845608028654 + (0.7978845608028654 * 3 * 0.044715) * square
            slope[rows, tile] = (half + made * (rise - rise * curve)).astype(BF16)
            made = dot(low, down_weight[...])
            total[rows, :] = jnp.where(step == 0, made, total[rows, :] + made)
        down_grad[...] = dot_tn(activated[...], down_low[...]).astype(BF16)

    @pl.when(step == TILES - 1)
    def _():
        residual_copy.wait()
        low = (total[...] + residual[...]).astype(BF16)
        for index, source in enumerate((first_cot, second_cot, third_cot, fourth_cot)):
            group = me[0] ^ index
            column = source[2 * WIDTH :, 0:ITEM_ROWS].astype(F32).T[0:WIDTH, 0:1]
            made = (dot_nt(source[WIDTH : 2 * WIDTH, :], low) + column).astype(BF16)
            for item in range(OWN_ITEMS):
                block = made[:, item * ITEM_ROWS : (item + 1) * ITEM_ROWS]
                recon[index, item] = block
            rows = pl.ds(pl.multiple_of(group * WIDTH, 16), WIDTH)
            head_grad[rows, :] = dot(source[0:WIDTH, :], low)
        rows = lax.broadcasted_iota(jnp.int32, (16, D), 0)
        padded = jnp.concatenate([head_sum[...], jnp.zeros((ITEM_ROWS - WIDTH, ITEM_ROWS), F32)], axis=0)
        line = column_sum(padded.T)
        line = jnp.concatenate([line, jnp.zeros((1, D - ITEM_ROWS), F32)], axis=1)
        head_grad[GROUPS * WIDTH :, :] += jnp.where(rows == 1 + me[0], line, 0.0)
        sums[...] = jnp.zeros_like(sums)

    @pl.when(jnp.logical_and(step >= BACK, step < BACK + TILES))
    def _():
        tile = pl.ds(pl.multiple_of((step - BACK) * FF_TILE, FF_TILE), FF_TILE)
        grad = dot_nt(down_low[...], down_weight[...]) * slope[:, tile].astype(F32)
        hidden_low = grad.astype(BF16)
        pl.when(step == BACK)(flipped_two_copy.wait)
        up_sum[...] = column_sum(hidden_low.astype(F32))
        up_grad[...] = dot(flipped_two[...], hidden_low).astype(BF16)
        made = dot_nt(hidden_low, up_weight[...])
        total[...] = jnp.where(step == BACK, made, total[...] + made)

    @pl.when(jnp.logical_and(step >= BACK + TILES, step < LAST))
    def _():
        part = step - BACK - TILES
        pl.when(step == BACK + TILES)(proj_copy.wait)
        here = pl.ds(pl.multiple_of(part * CHUNK, CHUNK), CHUNK)
        unit = unit_two[...].astype(F32)
        grad = total[here, :]
        back = norm_back(grad, unit, scale_two[:, 0:1], small[GAIN_TWO : GAIN_TWO + 1, :])
        back += down_low[here, :].astype(F32)
        grad_res[...] = back
        low = back.astype(BF16)
        slope[here, 3 * D :] = low
        attn_grad[...] = dot_nt(low, proj_weight[...]).astype(BF16)
        sums[0:1, :] += column_sum(grad * unit)
        sums[1:2, :] += column_sum(grad)
        sums[2:3, :] += column_sum(back)
        scaling = jnp.asarray(HEAD_DIM**-0.5, F32)
        for item in range(CHUNK_ITEMS):
            rows = slice(item * ITEM_ROWS, (item + 1) * ITEM_ROWS)
            for pair in range(PAIRS):
                lanes = [
                    slice(kind * D + pair * ITEM_ROWS, kind * D + (pair + 1) * ITEM_ROWS)
                    for kind in range(3)
                ]
                queries = stack_heads(qkv[rows, lanes[0]], first)
                cot = stack_heads(attn_grad[rows, lanes[0]], first)
                spot = (item * PAIRS + pair) * CHUNK
                low = probs[spot : spot + CHUNK, :]
                wide = low.astype(F32)
                grad_probs = dot_nt(cot, qkv[rows, lanes[2]])
                grad_qkv[rows, lanes[2]] = dot_tn(low, cot).astype(BF16)
                centre = jnp.sum(wide * grad_probs, axis=-1, keepdims=True)
                scores_low = (wide * (grad_probs - centre)).astype(BF16)
                made = join_heads(dot(scores_low, qkv[rows, lanes[1]]), first)
                grad_qkv[rows, lanes[0]] = (made * scaling).astype(BF16)
                made = dot_tn(scores_low, queries) * scaling
                grad_qkv[rows, lanes[1]] = made.astype(BF16)
        slope[here, : 3 * D] = grad_qkv[...]
        sums[3:4, :] += column_sum(grad_qkv[:, :D].astype(F32))
        sums[4:5, :] += column_sum(grad_qkv[:, 2 * D :].astype(F32))

    for tile in range(4):

        @pl.when(step == LAST + tile)
        def _():
            if tile == 0:
                flipped_one_copy.wait()
            if tile == 3:
                flipped_attended_copy.wait()
            left = flipped_one if tile < 3 else flipped_attended
            made = dot(left[...], slope[:, tile * D : (tile + 1) * D])
            mixed_grad[...] = made.astype(BF16)


def block(me, *operands):
    def again(step):
        return jnp.where(step < BACK, step, jnp.clip(step - BACK, 0, TILES - 1))

    far = pl.BlockSpec(memory_space=pl.ANY)
    return call(
        block_kernel,
        (
            shape(FF, D, dtype=BF16),
            shape(GROUPS, OWN_ITEMS, WIDTH, ITEM_ROWS, dtype=BF16),
            shape(GROUPS * WIDTH + 16, D),
            shape(FF, D, dtype=BF16),
            shape(1, FF),
            shape(ROWS, 3 * D, dtype=BF16),
            shape(ROWS, D),
            shape(8, D),
            shape(4 * D, D, dtype=BF16),
        ),
        grid_spec=pltpu.PrefetchScalarGridSpec(
            num_scalar_prefetch=1,
            grid=(LAST + 4,),
            in_specs=[
                whole(ROWS, D),
                far,
                pl.BlockSpec((D, FF_TILE), lambda step, me: (0, again(step))),
                columns_at(0, 1, FF_TILE, TILES),
                pl.BlockSpec((FF_TILE, D), lambda step, me: (again(step), 0)),
                whole(WIDTH, ITEM_ROWS),
            ]
            + [whole(2 * WIDTH + 16, D)] * 4
            + [
                far,
                rows_at(BACK + TILES, CHUNK, D, PARTS),
                rows_at(BACK + TILES, CHUNK, ITEM_ROWS, PARTS),
                whole(8, D),
                far,
                rows_at(BACK + TILES, CHUNK, 3 * D, PARTS),
                rows_at(BACK + TILES, CHUNK_ITEMS * PAIRS * CHUNK, ITEM_ROWS, PARTS),
                far,
                far,
            ],
            out_specs=[
                rows_at(0, FF_TILE, D, TILES),
                held(GROUPS, OWN_ITEMS, WIDTH, ITEM_ROWS),
                held(GROUPS * WIDTH + 16, D),
                rows_at(BACK, FF_TILE, D, TILES),
                columns_at(BACK, 1, FF_TILE, TILES),
                rows_at(BACK + TILES, CHUNK, 3 * D, PARTS),
                rows_at(BACK + TILES, CHUNK, D, PARTS),
                held(8, D),
                rows_at(LAST, D, D, 4),
            ],
            scratch_shapes=[
                pltpu.VMEM((ROWS, D), F32),
                pltpu.VMEM((ROWS, FF_TILE), BF16),
                pltpu.VMEM((ROWS, FF), BF16),
                pltpu.VMEM((ROWS, D), BF16),
                pltpu.VMEM((CHUNK, D), BF16),
                pltpu.VMEM((ROWS, D), F32),
                pltpu.VMEM((D, ROWS), BF16),
                pltpu.VMEM((D, D), BF16),
                pltpu.VMEM((D, ROWS), BF16),
                pltpu.VMEM((D, ROWS), BF16),
                pltpu.SemaphoreType.DMA((5,)),
            ],
        ),
    )(me, *operands)


def write_halves(core, values, send, keep):
    left, right = values[:, :CUT], values[:, CUT:]

    @pl.when(core == 0)
    def _():
        keep[...] = left
        send[...] = right

    @pl.when(core != 0)
    def _():
        keep[...] = right
        send[...] = left


EMBED_AT = SLOTS
HEAD_AT = EMBED_AT + GROUPS * WIDTH
SUMS_AT = HEAD_AT + GROUPS * WIDTH + 16


def embed_back_kernel(
    place, grads, qkv_weight, unit_one, scale_one, grad_res, small, first_in, second_in, third_in, fourth_in,
    first_weight, second_weight, third_weight, fourth_weight, position, up_sum, sums, head_grad, recon,
    send, keep, first_out, second_out, third_out, fourth_out, embedded_low, rest,
):
    gain_one = small[GAIN_ONE : GAIN_ONE + 1, :]
    me = place[0]
    sources = (first_in, second_in, third_in, fourth_in)
    outs = (first_out, second_out, third_out, fourth_out)
    for index, out in enumerate(outs):
        out[OWN_ITEMS:] = recon[index]

    def first_norm(step, carry):
        rows = pl.ds(pl.multiple_of(step * CHUNK, CHUNK), CHUNK)
        grad = dot_nt(grads[rows, :], qkv_weight[...])
        unit = unit_one[rows, :].astype(F32)
        total = grad_res[rows, :] + norm_back(grad, unit, scale_one[rows, 0:1], gain_one)
        low = total.astype(BF16)
        embedded_low[rows, :] = low
        for index, weight in enumerate((first_weight, second_weight, third_weight, fourth_weight)):
            made = dot_nt(weight[...], low).astype(BF16)
            for part in range(CHUNK // ITEM_ROWS):
                block = made[:, part * ITEM_ROWS : (part + 1) * ITEM_ROWS]
                item = step * (CHUNK // ITEM_ROWS) + part
                outs[index][pl.ds(item, 1)] = block[None]
        gain, shift, bias = carry
        return gain + column_sum(grad * unit), shift + column_sum(grad), bias + column_sum(total)

    none = jnp.zeros((1, D), F32)
    gain, shift, bias = lax.fori_loop(0, ROWS // CHUNK, first_norm, (none, none, none))
    slots = lax.broadcasted_iota(jnp.int32, (SLOTS, ROWS), 0)
    hot = (position[...] == slots).astype(BF16)
    rest[0:SLOTS, :] = dot(hot, embedded_low[...])
    for index, source in enumerate(sources):
        rows = pl.ds(pl.multiple_of(EMBED_AT + (me ^ index) * WIDTH, 16), WIDTH)
        rest[rows, :] = dot(source[...], embedded_low[...])
    rest[HEAD_AT:SUMS_AT, :] = head_grad[...]
    rest[SUMS_AT:, :] = jnp.zeros((REST - SUMS_AT, D), F32)
    for row, value in enumerate((gain, shift, bias)):
        rest[SUMS_AT + row : SUMS_AT + row + 1, :] = value
    rest[SUMS_AT + 3 : SUMS_AT + 8, :] = sums[0:5, :]
    for row in range(FF // D):
        at = SUMS_AT + 8 + row
        rest[at : at + 1, :] = up_sum[:, row * D : (row + 1) * D]
    write_halves(lax.rem(me, 2), rest[...].astype(BF16), send, keep)


def embed_backward(place, *operands):
    vmem = pl.BlockSpec(memory_space=pltpu.VMEM)
    return call(
        embed_back_kernel,
        (
            shape(REST, CUT, dtype=BF16),
            shape(REST, CUT, dtype=BF16),
        )
        + (shape(2 * OWN_ITEMS, WIDTH, ITEM_ROWS, dtype=BF16),) * 4,
        in_specs=[pl.BlockSpec(memory_space=pltpu.SMEM)] + [vmem] * len(operands),
        out_specs=[vmem] * 6,
        scratch_shapes=[pltpu.VMEM((ROWS, D), BF16), pltpu.VMEM((REST, D), F32)],
    )(place, *operands)


WIDEN_STEPS = 6


def widen_kernel(down, up, mixed, down_out, up_out, qkv_out, proj_out):
    down_out[...] = down[...].astype(F32)
    for tile in range(4):
        lanes = slice(tile * D, (tile + 1) * D)
        up_out[:, lanes] = up[tile].astype(F32)
        if tile < 3:
            qkv_out[:, lanes] = mixed[tile].astype(F32)
    proj_out[...] = mixed[3].astype(F32)


def widen(down, up, mixed):
    rows = D // WIDEN_STEPS
    tiles = pl.BlockSpec((4, rows, D), lambda step: (0, step, 0))
    block = lambda rows, width: pl.BlockSpec((rows, width), lambda step: (step, 0))
    return call(
        widen_kernel,
        (shape(FF, D), shape(D, FF), shape(D, 3 * D), shape(D, D)),
        grid=(WIDEN_STEPS,),
        in_specs=[block(4 * rows, D), tiles, tiles],
        out_specs=[block(4 * rows, D), block(rows, FF), block(rows, 3 * D), block(rows, D)],
    )(down, up.reshape(4, D, D), mixed.reshape(4, D, D))


def extract_kernel(place, own, other, position_out, embed_out, head_out, totals_out):
    group = place[0]
    parts = (
        (position_out, 0),
        (embed_out, pl.multiple_of(EMBED_AT + group * WIDTH, 16)),
        (head_out, pl.multiple_of(HEAD_AT + group * WIDTH, 16)),
        (totals_out, SUMS_AT - 16),
    )

    def write(left, right):
        for out, start in parts:
            rows = pl.ds(start, out.shape[0])
            out[:, :CUT] = left[rows, :].astype(F32)
            out[:, CUT:] = right[rows, :].astype(F32)

    pl.when(lax.rem(group, 2) == 0)(lambda: write(own, other))
    pl.when(lax.rem(group, 2) != 0)(lambda: write(other, own))


def extract(me, own, other):
    vmem = pl.BlockSpec(memory_space=pltpu.VMEM)
    return call(
        extract_kernel,
        (shape(SLOTS, D), shape(WIDTH, D), shape(WIDTH, D), shape(32, D)),
        in_specs=[pl.BlockSpec(memory_space=pltpu.SMEM), vmem, vmem],
        out_specs=[vmem] * 4,
    )(me, own, other)


def tie(value, *tokens):
    return lax.optimization_barrier((value, tokens))[0]


SWAP = [(0, 1), (1, 0)]
PLANES = {"x": ("z", "ylo", "yhi")}


def other_core(value):
    return lax.ppermute(value, "core", SWAP)


def shift(value, axis, distance):
    return lax.ppermute(value, axis, [(i, (i + distance) % 4) for i in range(4)])


def quarters(keep, arrived, axis):
    own = (keep.astype(F32) + arrived.astype(F32)).astype(BF16)
    rows = own.shape[0] // 4
    place = lax.axis_index(axis)
    return [
        lax.dynamic_slice_in_dim(own, ((place + step) % 4) * rows, rows, 0) for step in range(4)
    ]


def sum_quarter(parts, axis):
    total = parts[0].astype(F32)
    for distance in (1, 3, 2):
        total += shift(parts[distance], axis, distance).astype(F32)
    return total.astype(BF16)


def split_plane(block, axis):
    lanes = block.shape[1] if block.shape[0] % 128 == 0 else ITEM_ROWS
    return lax.all_to_all(block.reshape(16, -1, lanes), PLANES[axis], 0, 0)


def join_plane(parts, axis):
    share = jnp.sum(parts.astype(F32), axis=0).astype(BF16)
    parts = lax.all_to_all(jnp.broadcast_to(share[None], parts.shape), PLANES[axis], 0, 0)
    return parts.reshape(-1, CUT)


def join_quarters(own, axis):
    turned = [own, shift(own, axis, 3), shift(own, axis, 2), shift(own, axis, 1)]
    turned = jnp.concatenate(turned + turned[:3], axis=0)
    start = ((4 - lax.axis_index(axis)) % 4) * own.shape[0]
    return lax.dynamic_slice_in_dim(turned, start, 4 * own.shape[0], 0)


def body(
    patches,
    visible,
    recon_cotangent,
    embed_weight,
    embed_bias,
    position_table,
    attn_norm_gain,
    attn_norm_bias,
    qkv_weight,
    qkv_bias,
    proj_weight,
    proj_bias,
    mlp_norm_gain,
    mlp_norm_bias,
    up_weight,
    up_bias,
    down_weight,
    down_bias,
    head_weight,
    head_bias,
):
    my_group = lax.axis_index(VARS_AXES)
    me = my_group.astype(jnp.int32).reshape(1)
    batch_items = patches.shape[0]
    patch_count = patches.shape[2]

    def partners(blocks):
        return [
            blocks[0],
            other_core(blocks[1]),
            lax.ppermute(blocks[2], "yhi", SWAP),
            lax.ppermute(blocks[3], ("yhi", "core"), [(i, 3 - i) for i in range(4)]),
        ]

    items_visible = visible.reshape(GROUPS, OWN_ITEMS, ITEM_ROWS // 2)
    far_embed = lax.ppermute(embed_weight, "yhi", SWAP)
    near_embed = other_core(embed_weight)
    to_embed, to_head, head_sum = pick(
        me,
        jnp.swapaxes(patches, 2, 3).reshape(GROUPS, OWN_ITEMS, 2, WIDTH, patch_count),
        visible,
        jnp.swapaxes(recon_cotangent, 1, 2).reshape(GROUPS, OWN_ITEMS, WIDTH, ITEM_ROWS),
        head_weight.T,
        head_bias[None],
    )
    picked = partners(to_embed)
    embeds = [embed_weight, near_embed, far_embed, other_core(far_embed)]
    for_embed = [*picked, *embeds]
    for_head = partners(to_head)
    own_visible = lax.dynamic_slice_in_dim(visible, my_group * OWN_ITEMS, OWN_ITEMS, 0)
    position = jnp.concatenate([own_visible, own_visible + patch_count], axis=1)
    zero = jnp.zeros((D,), BF16)
    small = jnp.stack(
        [
            embed_bias,
            attn_norm_gain,
            attn_norm_bias,
            proj_bias,
            mlp_norm_gain,
            mlp_norm_bias,
            down_bias,
            zero,
        ]
    ).astype(F32)
    joined_bias = jnp.concatenate([qkv_bias[0], zero, qkv_bias[1]]).astype(F32)[None]

    (
        unit_one,
        scale_one,
        flipped_one,
        qkv,
        probs,
        flipped_attended,
        residual,
        unit_two,
        scale_two,
        normed_two,
        flipped_two,
    ) = attention(
        *for_embed,
        position.reshape(ROWS, 1),
        position_table,
        small,
        qkv_weight,
        joined_bias,
        proj_weight,
    )
    down_grad, recon, head_grad, up_grad, up_sum, grad_qkv, grad_res, sums, mixed_grad = block(
        me,
        normed_two,
        residual,
        up_weight,
        up_bias.astype(F32)[None],
        down_weight,
        head_sum,
        *for_head,
        flipped_two,
        unit_two,
        scale_two,
        small,
        proj_weight,
        qkv,
        probs,
        flipped_one,
        flipped_attended,
    )
    down_grad, up_grad, mixed_grad = lax.psum((down_grad, up_grad, mixed_grad), ALL_AXES)
    rest_send, rest_keep, *blocks = embed_backward(
        me,
        grad_qkv,
        qkv_weight,
        unit_one,
        scale_one,
        grad_res,
        small,
        *for_embed,
        position.reshape(1, ROWS),
        up_sum,
        sums,
        head_grad,
        recon,
    )
    rest_parts = quarters(rest_keep, other_core(rest_send), "x")
    rest_plane = split_plane(sum_quarter(rest_parts, "x"), "x")
    rest_own = join_quarters(join_plane(rest_plane, "x"), "x")
    blocks = partners([tie(block, rest_plane) for block in blocks])
    patch_grad, recon = put(me, items_visible, blocks)
    position_grad, embed_grad, head_grad, total = extract(me, rest_own, other_core(rest_own))
    down_grad, up_grad, qkv_grad, proj_grad = widen(down_grad, up_grad, mixed_grad)
    patch_grad = patch_grad.reshape(batch_items, 2, WIDTH, patch_count)
    patch_grad = jnp.swapaxes(patch_grad, 2, 3)
    head_shift = lax.dynamic_index_in_dim(total, 1 + my_group, 0, False)[:WIDTH]
    early, total = total[0], total[16:]
    return (
        jnp.swapaxes(recon.reshape(batch_items, WIDTH, ITEM_ROWS), 1, 2),
        patch_grad,
        embed_grad,
        total[2],
        position_grad,
        total[0],
        total[1],
        qkv_grad,
        total[6:8],
        proj_grad,
        total[5],
        total[3],
        total[4],
        up_grad,
        total[8:12].reshape(FF),
        down_grad,
        early,
        head_grad.T,
        head_shift,
    )


def solution(mesh):
    items, groups = ITEMS_AXES, VARS_AXES
    fine = Mesh(mesh.devices.reshape(4, 2, 4, 2, 2), ALL_AXES)
    in_specs = (
        P(items, None, None, groups),
        P(items, None),
        P(items, None, groups),
        P(groups, None),
        *[P()] * 14,
        P(None, groups),
        P(groups),
    )
    out_specs = (
        P(items, None, groups),
        P(items, None, None, groups),
        P(groups, None),
        *[P()] * 14,
        P(None, groups),
        P(groups),
    )
    return jax.shard_map(body, mesh=fine, in_specs=in_specs, out_specs=out_specs, check_vma=False)
```
